32 devices in a mesh: row: 8 (over z, y), col: 4 (over x, core).
Axes of the slice: x: 2, y: 2, z: 4, core: 2. Of those that a mesh axis runs over, the one named last changes fastest.
Arguments:
- queries: bfloat16 [768, 8192], P('col', 'row'), may hold values from -16 to 16
- key_rows: bfloat16 [768, 8192], P('col', 'row'), may hold values from -16 to 16
- values: bfloat16 [768, 8192], P('col', 'row'), may hold values from -6 to 6
- block_lists: int32 [32, 16], P('row'), may hold values from 0 to 31, as said below
- counts: int32 [32], P('row'), may hold values from 1 to 16, as said below
- out_proj: bfloat16 [768, 768], P('col'), may hold values from -0.21875 to 0.21875
- stream: bfloat16 [8192, 768], P('row'), may hold values from -6 to 6
- norm_gain: float32 [768], replicated, may hold values from 0.1 to 1.9
- head_proj: bfloat16 [96, 768], replicated, may hold values from -0.21875 to 0.21875
- patches: float32 [8192, 48], P('row'), may hold values from -6 to 6
- token_order: int32 [8192], P('row'), may hold values from 0 to 8191, as said below
- cotangent: float32 [8192, 48], P('row'), may hold values from -6 to 6
Outputs:
- latent_out: float32 [8192, 48], P('row')
- grad_queries: bfloat16 [768, 8192], P('col', 'row')
- grad_keys: bfloat16 [768, 8192], P('col', 'row')
- grad_values: bfloat16 [768, 8192], P('col', 'row')
The draws below stay inside these ranges and needn't reach their ends.
Inputs may be any that keep to these rules, and one draw needn't show every extreme that they name: `block_lists`: entry 0 of row b is b; entries 1 to counts[b] - 1 are distinct blocks from b - 15 to b - 1; later entries equal b. counts[b] is at most b + 1; every block whose index is 31 modulo 32 has 16. A permutation; token_order[t] lies in block 31 - t // 256.
All inputs are finite; a program needn't handle non-finite values.
Results may differ from the reference program's by a relative error of at most 0.012.
The reference program's roundings to bfloat16 on the way (of `rounded`, `attended`, `normed`, `grad_params`, `grad_hidden`, `grad_attended` and `grad_scores`) count: a program that leaves them out, or rounds other values in their place, can miss the bound.
Values may be sent and summed in bfloat16 or wider, within the bound.
No kernel may reach another device: no remote copies, remote signals or barrier semaphores. Data moves between devices by JAX's collectives and lax.ppermute only.
A program may use at most 128 MiB of HBM per device.

```python
import jax
import jax.numpy as jnp
from jax import lax

HEADS = 12
HEAD_DIM = 64
D = 768
C = 48
BLOCK = 256
LIST = 16
TOKENS = 8192
NBLK = 32


def query_key_pair(key):
    query_draw = jax.random.fold_in(key, 11)
    key_draw = jax.random.fold_in(key, 12)
    array_shape = (TOKENS, D)
    query_part = jnp.clip(jax.random.normal(query_draw, array_shape, jnp.float32), -4.0, 4.0)
    key_part = jnp.clip(jax.random.normal(key_draw, array_shape, jnp.float32), -4.0, 4.0)
    return (query_part, key_part)


def draw_queries(key, part):
    return query_key_pair(key)[0].T.astype(jnp.bfloat16)


def draw_key_rows(key, part):
    return query_key_pair(key)[1].T.astype(jnp.bfloat16)


def neighbour_table(key):
    table_draw = jax.random.fold_in(key, 21)
    block_ids = jnp.arange(NBLK, dtype=jnp.int32)
    group_levels = jax.random.randint(jax.random.fold_in(table_draw, 1), (NBLK // 8 + 1,), 1, LIST + 1)
    wanted = group_levels[block_ids // 8]
    wanted = jnp.where(block_ids % 32 == 31, LIST, wanted)
    live_count = jnp.minimum(wanted, block_ids + 1)
    offsets = jnp.arange(1, LIST, dtype=jnp.int32)
    ranking = jax.random.randint(jax.random.fold_in(table_draw, 2), (NBLK, LIST - 1), 0, 1 << 20) * LIST + offsets[None, :]
    ranking = jnp.where(offsets[None, :] <= block_ids[:, None], ranking, (1 << 26) + offsets[None, :])
    chosen = jnp.take_along_axis(jnp.broadcast_to(offsets[None, :], (NBLK, LIST - 1)), jnp.argsort(ranking, axis=1), axis=1)
    entries = jnp.where(offsets[None, :] < live_count[:, None], block_ids[:, None] - chosen, block_ids[:, None])
    table = jnp.concatenate([block_ids[:, None], entries], axis=1).astype(jnp.int32)
    return (table, live_count.astype(jnp.int32))


def draw_block_lists(key, part):
    return neighbour_table(key)[0]


def draw_counts(key, part):
    return neighbour_table(key)[1]


def draw_token_order(key, part):
    order_draw = jax.random.fold_in(key, 31)
    block_draws = jax.random.split(order_draw, NBLK)
    inside = jax.vmap(lambda block_key: jax.random.permutation(block_key, BLOCK))(block_draws)
    source = (NBLK - 1 - jnp.arange(NBLK, dtype=jnp.int32))[:, None] * BLOCK + inside.astype(jnp.int32)
    return source.reshape(TOKENS).astype(jnp.int32)


def levels(stream_key, shape, shards, smallest, top_value):
    def one(dim, blocks):
        draws = jax.random.uniform(jax.random.fold_in(jax.random.fold_in(stream_key, 6), dim), (blocks,), jnp.float32, smallest / len(shards), top_value / len(shards))
        return jnp.repeat(jnp.exp(draws), shape[dim] // blocks).reshape((-1,) + (1,) * (len(shape) - dim - 1))

    loudness = one(*shards[0])
    for cut in shards[1:]:
        loudness = loudness * one(*cut)
    return loudness


def gaussian(stream_key, extent, scale, limit, cuts=(), kind=jnp.bfloat16):
    loudness = levels(stream_key, extent, cuts, -0.22, 0.18) if cuts else 1.0
    values = jax.random.normal(stream_key, extent, jnp.float32) * scale * loudness
    return jnp.minimum(jnp.maximum(values, -limit), limit).astype(kind)


def setup_inputs(seed: int = 0) -> dict:
    splits = jax.random.split(jax.random.key(seed), 13)
    return {
        "queries": draw_queries(jax.random.fold_in(splits[12], 71), 0),
        "key_rows": draw_key_rows(jax.random.fold_in(splits[12], 71), 0),
        "values": gaussian(splits[2], (D, TOKENS), 1.0, 6.0, ((0, 4), (1, 8))),
        "block_lists": draw_block_lists(jax.random.fold_in(splits[12], 71), 0),
        "counts": draw_counts(jax.random.fold_in(splits[12], 71), 0),
        "out_proj": gaussian(splits[5], (D, D), D ** -0.5, 0.21875, ((0, 4),)),
        "stream": gaussian(splits[6], (TOKENS, D), 1.0, 6.0, ((0, 8),)),
        "norm_gain": jnp.clip(1.0 + 0.18 * jax.random.normal(splits[7], (D,), jnp.float32), 0.1, 1.9),
        "head_proj": gaussian(splits[8], (2 * C, D), D ** -0.5, 0.21875),
        "patches": gaussian(splits[9], (TOKENS, C), 1.0, 6.0, ((0, 8),), jnp.float32),
        "token_order": draw_token_order(jax.random.fold_in(splits[12], 71), 0),
        "cotangent": gaussian(splits[11], (TOKENS, C), 1.0, 6.0, ((0, 8),), jnp.float32),
    }


NEG = -1e+30
EPS = 1e-05

def reference(queries, key_rows, values, block_lists, counts, out_proj, stream, norm_gain, head_proj, patches, token_order, cotangent):
    score_scale = HEAD_DIM ** (-0.5)
    query_blocks = queries.T.reshape(NBLK, BLOCK, HEADS, HEAD_DIM)
    key_blocks = key_rows.T.reshape(NBLK, BLOCK, HEADS, HEAD_DIM)
    value_blocks = values.T.reshape(NBLK, BLOCK, HEADS, HEAD_DIM)
    grad_latent = jnp.zeros_like(cotangent).at[token_order].set(cotangent).reshape(NBLK, BLOCK, C)
    patch_blocks = patches.reshape(NBLK, BLOCK, C)
    stream_blocks = stream.reshape(NBLK, BLOCK, D)
    entry_ids = jnp.arange(LIST).astype(jnp.int32)
    rows_at = jnp.arange(BLOCK).astype(jnp.int32)

    def one_block(state_in, block_no):
        grad_keys, grad_values = state_in
        entries = block_lists[block_no]
        live_count = counts[block_no]
        query_tile = query_blocks[block_no].astype(jnp.float32)
        key_tiles = key_blocks[entries].astype(jnp.float32)
        value_tiles = value_blocks[entries].astype(jnp.float32)
        scores = jnp.einsum('qhe,jkhe->hqjk', query_tile, key_tiles) * score_scale
        allowed = (entry_ids[:, None, None] < live_count) & ((entry_ids[:, None, None] > 0) | (rows_at[None, None, :] <= rows_at[None, :, None]))
        allowed = jnp.transpose(allowed, (1, 0, 2))[None]
        scores = jnp.where(allowed, scores, NEG)
        row_max = lax.optimization_barrier(jnp.max(scores, axis=(2, 3), keepdims=True))
        weights = jnp.exp(scores - row_max)
        probs = weights / lax.optimization_barrier(jnp.sum(weights, axis=(2, 3), keepdims=True))
        rounded = lax.optimization_barrier(probs.astype(jnp.bfloat16)).astype(jnp.float32)
        attended = jnp.einsum('hqjk,jkhe->qhe', rounded, value_tiles).astype(jnp.bfloat16)
        flat_rows = attended.reshape(BLOCK, D)
        mixed_sum = jnp.dot(flat_rows, out_proj, preferred_element_type=jnp.float32)
        hidden = stream_blocks[block_no].astype(jnp.float32) + mixed_sum
        inverse = lax.rsqrt(lax.optimization_barrier(jnp.mean(hidden * hidden, axis=-1, keepdims=True)) + EPS)
        normed = (hidden * inverse * norm_gain).astype(jnp.bfloat16)
        params = lax.dot_general(normed, head_proj, (((1,), (1,)), ((), ())), preferred_element_type=jnp.float32)
        shift_mean = params[:, :C]
        log_scale = params[:, C:]
        factor = jnp.exp(-log_scale)
        latent = (patch_blocks[block_no] - shift_mean) * factor
        grad_here = grad_latent[block_no]
        grad_params = jnp.concatenate([-grad_here * factor, -grad_here * latent - 1.0], axis=-1).astype(jnp.bfloat16)
        grad_normed = jnp.dot(grad_params, head_proj, preferred_element_type=jnp.float32)
        gained = grad_normed * norm_gain
        grad_hidden = (inverse * gained - hidden * inverse ** 3 * lax.optimization_barrier(jnp.mean(hidden * gained, axis=-1, keepdims=True))).astype(jnp.bfloat16)
        grad_attended = jnp.dot(grad_hidden, out_proj.T, preferred_element_type=jnp.float32).astype(jnp.bfloat16)
        grad_tile = grad_attended.reshape(BLOCK, HEADS, HEAD_DIM).astype(jnp.float32)
        weight_sum = lax.optimization_barrier(jnp.sum(grad_tile * attended.astype(jnp.float32), axis=-1)).T
        grad_probs = jnp.einsum('qhe,jkhe->hqjk', grad_tile, value_tiles)
        grad_scores = (probs * (grad_probs - weight_sum[:, :, None, None]) * score_scale).astype(jnp.bfloat16)
        grad_scores = lax.optimization_barrier(grad_scores).astype(jnp.float32)
        grad_query = jnp.einsum('hqjk,jkhe->qhe', grad_scores, key_tiles).astype(jnp.bfloat16)
        grad_key = jnp.einsum('hqjk,qhe->jkhe', grad_scores, query_tile)
        grad_value = jnp.einsum('hqjk,qhe->jkhe', rounded, grad_tile)
        grad_keys = grad_keys.at[entries].add(grad_key)
        grad_values = grad_values.at[entries].add(grad_value)
        return ((grad_keys, grad_values), (latent, grad_query.reshape(BLOCK, D)))
    zeros = jnp.zeros((NBLK, BLOCK, HEADS, HEAD_DIM), jnp.float32)
    (grad_keys, grad_values), (latents, grad_query) = lax.scan(one_block, (zeros, zeros), jnp.arange(NBLK).astype(jnp.int32))
    latent_all = latents.reshape(TOKENS, C)
    return (latent_all[token_order], grad_query.reshape(TOKENS, D).T, grad_keys.astype(jnp.bfloat16).reshape(TOKENS, D).T, grad_values.astype(jnp.bfloat16).reshape(TOKENS, D).T)
```

```python
import jax
import jax.numpy as jnp
from jax import lax
from jax.experimental import pallas as pl
from jax.experimental.pallas import tpu as pltpu
from jax.sharding import PartitionSpec as P

HEAD_DIM = 64
BLOCK = 256
LIST = 16
REACH = 4

NEG = -1e30
EPS = 1e-05
SCALE = HEAD_DIM ** (-0.5)
F32 = jnp.float32
BF16 = jnp.bfloat16


def dot(a, b, ca=1, cb=0):
    return lax.dot_general(a, b, (((ca,), (cb,)), ((), ())), preferred_element_type=F32)


def vmem(count):
    return [pl.BlockSpec(memory_space=pltpu.VMEM)] * count


def smem(count):
    return [pl.BlockSpec(memory_space=pltpu.SMEM)] * count


def hop(array, by):
    size = lax.axis_size("row")
    pairs = [(i, i + by) for i in range(size) if 0 <= i + by < size]
    return lax.ppermute(array, "row", pairs)


def mate(array):
    return lax.ppermute(array, "row", [(i, i ^ 1) for i in range(lax.axis_size("row"))])


def mirror(array):
    size = lax.axis_size("row")
    return lax.ppermute(array, "row", [(i, size - 1 - i) for i in range(size)])


def across(array, bits):
    return lax.ppermute(array, "col", [(i, i ^ bits) for i in range(lax.axis_size("col"))])


def split3(x):
    hi = x.astype(BF16)
    rest = x - hi.astype(F32)
    mid = rest.astype(BF16)
    low = (rest - mid.astype(F32)).astype(BF16)
    return hi, mid, low


def scatter_kernel(order_ref, x_ref, o_ref):
    rows = lax.broadcasted_iota(jnp.int32, (BLOCK, BLOCK), 0)
    pick = (rows == order_ref[...]).astype(BF16)
    hi, mid, low = split3(x_ref[...])
    o_ref[...] = (dot(pick, hi) + dot(pick, mid)) + dot(pick, low)


def gather_kernel(order_ref, x_ref, o_ref):
    columns = lax.broadcasted_iota(jnp.int32, (BLOCK, BLOCK), 1)
    pick = (columns == order_ref[...]).astype(BF16)
    hi, mid, low = split3(x_ref[...])
    o_ref[...] = (dot(pick, hi) + dot(pick, mid)) + dot(pick, low)


def permuted(kernel, order, x):
    return pl.pallas_call(
        kernel,
        out_shape=jax.ShapeDtypeStruct(x.shape, F32),
        in_specs=vmem(2),
        out_specs=vmem(1)[0],
    )(order, x)


def forward_kernel(lists_ref, counts_ref, place_ref, q_ref, kv0, kv1, kv2, kv3, kv4,
                   att_ref, lse_ref, key_rows, value_cols, acc_ref):
    heads = q_ref.shape[0] // HEAD_DIM
    blocks = q_ref.shape[1] // BLOCK
    for distance, ref in enumerate((kv0, kv1, kv2, kv3, kv4)):
        for b in range(blocks):
            slot = (REACH - distance) * blocks + b
            cols = slice(b * BLOCK, (b + 1) * BLOCK)
            value_cols[slot] = ref[1, :, cols]
            for h in range(heads):
                key_rows[slot, h] = ref[0, h * HEAD_DIM:(h + 1) * HEAD_DIM, cols].T
    base = REACH * blocks - place_ref[0] * blocks
    keep = (lax.broadcasted_iota(jnp.int32, (BLOCK, BLOCK), 0)
            <= lax.broadcasted_iota(jnp.int32, (BLOCK, BLOCK), 1))

    def one_block(b, carry):
        cols = pl.ds(pl.multiple_of(b * BLOCK, BLOCK), BLOCK)
        acc_ref[...] = jnp.zeros_like(acc_ref)

        def entry(slot, state, masked):
            out = []
            for h in range(heads):
                rows = slice(h * HEAD_DIM, (h + 1) * HEAD_DIM)
                top, total = state[2 * h], state[2 * h + 1]
                scores = dot(key_rows[slot, h], q_ref[rows, cols] * BF16(SCALE))
                if masked:
                    scores = jnp.where(keep, scores, NEG)
                newest = jnp.maximum(top, jnp.max(scores, axis=0, keepdims=True))
                weights = jnp.exp(scores - newest)
                fade = jnp.exp(top - newest)
                total = total * fade + jnp.sum(weights, axis=0, keepdims=True)
                acc_ref[rows] = acc_ref[rows] * fade + dot(
                    value_cols[slot, rows], weights.astype(BF16))
                out += [newest, total]
            return tuple(out)

        state = (jnp.full((1, BLOCK), NEG, F32), jnp.zeros((1, BLOCK), F32)) * heads
        state = entry(lists_ref[b, 0] + base, state, True)
        state = lax.fori_loop(
            1, counts_ref[b], lambda j, s: entry(lists_ref[b, j] + base, s, False), state)
        for h in range(heads):
            rows = slice(h * HEAD_DIM, (h + 1) * HEAD_DIM)
            att_ref[rows, cols] = (acc_ref[rows] / state[2 * h + 1]).astype(BF16)
            lse_ref[h, :, cols] = state[2 * h] + jnp.log(state[2 * h + 1])
        return carry

    lax.fori_loop(0, blocks, one_block, 0)


def forward(lists, counts, place, queries, slabs):
    width, tokens = queries.shape
    heads, slots = width // HEAD_DIM, (REACH + 1) * (tokens // BLOCK)
    return pl.pallas_call(
        forward_kernel,
        out_shape=(jax.ShapeDtypeStruct((width, tokens), BF16),
                   jax.ShapeDtypeStruct((heads, 1, tokens), F32)),
        in_specs=smem(3) + vmem(6),
        out_specs=tuple(vmem(2)),
        scratch_shapes=[
            pltpu.VMEM((slots, heads, BLOCK, HEAD_DIM), BF16),
            pltpu.VMEM((slots, width, BLOCK), BF16),
            pltpu.VMEM((width, BLOCK), F32),
        ],
        compiler_params=pltpu.CompilerParams(vmem_limit_bytes=48 << 20),
        cost_estimate=pl.CostEstimate(
            flops=10 * 10 ** 9, bytes_accessed=6 << 20, transcendentals=10 ** 7),
    )(lists, counts, place, queries, *slabs)


def flow_kernel(place_ref, a0, a1, a2, a3, w_ref, stream_ref, gain_ref, head_ref, patch_ref,
                grad_ref, latent_ref, g0, g1, g2, g3, wide, back):
    width = a0.shape[0]
    channels = patch_ref.shape[1]
    me = place_ref[1]
    for k, ref in enumerate((a0, a1, a2, a3)):
        wide[pl.ds(pl.multiple_of(jnp.bitwise_xor(me, k) * width, width), width)] = ref[...]
    hidden = stream_ref[...].astype(F32) + dot(wide[...], w_ref[...], 0, 0)
    inverse = lax.rsqrt(jnp.mean(hidden * hidden, axis=-1, keepdims=True) + EPS)
    gain = gain_ref[...]
    normed = (hidden * inverse * gain).astype(BF16)
    shift = dot(normed, head_ref[:channels], 1, 1)
    log_scale = dot(normed, head_ref[channels:], 1, 1)
    factor = jnp.exp(-log_scale)
    latent = (patch_ref[...] - shift) * factor
    latent_ref[...] = latent
    grad = grad_ref[...]
    grad_shift = (-grad * factor).astype(BF16)
    grad_log = (-grad * latent - 1.0).astype(BF16)
    gained = (dot(grad_shift, head_ref[:channels]) + dot(grad_log, head_ref[channels:])) * gain
    grad_hidden = (
        inverse * gained
        - hidden * inverse ** 3 * jnp.mean(hidden * gained, axis=-1, keepdims=True)
    ).astype(BF16)
    back[...] = dot(w_ref[...], grad_hidden, 1, 1).astype(BF16)
    for k, ref in enumerate((g0, g1, g2, g3)):
        ref[...] = back[pl.ds(pl.multiple_of(jnp.bitwise_xor(me, k) * width, width), width)]


def flow(place, parts, weights, stream, gain, head_proj, patches, grad):
    width = parts[0].shape[0]
    return pl.pallas_call(
        flow_kernel,
        out_shape=(jax.ShapeDtypeStruct(patches.shape, F32),)
        + (jax.ShapeDtypeStruct((width, BLOCK), BF16),) * 4,
        in_specs=smem(1) + vmem(10),
        out_specs=tuple(vmem(5)),
        scratch_shapes=[pltpu.VMEM((4 * width, BLOCK), BF16)] * 2,
        compiler_params=pltpu.CompilerParams(vmem_limit_bytes=48 << 20),
    )(place, *parts, weights, stream, gain, head_proj, patches, grad)


def backward_kernel(lists_ref, counts_ref, place_ref, q_ref, kv0, kv1, kv2, kv3, kv4,
                    att_ref, lse_ref, g0, g1, g2, g3,
                    dq_ref, d0, d1, d2, d3, d4,
                    key_rows, value_rows, key_cols, grad_cols, grad_keys, grad_values, acc_ref):
    heads = q_ref.shape[0] // HEAD_DIM
    blocks = q_ref.shape[1] // BLOCK
    me = place_ref[1]
    for k, ref in enumerate((g0, g1, g2, g3)):
        grad_cols[jnp.bitwise_xor(me, k)] = ref[...]
    for distance, ref in enumerate((kv0, kv1, kv2, kv3, kv4)):
        for b in range(blocks):
            slot = (REACH - distance) * blocks + b
            cols = slice(b * BLOCK, (b + 1) * BLOCK)
            key_cols[slot] = ref[0, :, cols]
            for h in range(heads):
                rows = slice(h * HEAD_DIM, (h + 1) * HEAD_DIM)
                key_rows[slot, h] = ref[0, rows, cols].T
                value_rows[slot, h] = ref[1, rows, cols].T
    grad_keys[...] = jnp.zeros_like(grad_keys)
    grad_values[...] = jnp.zeros_like(grad_values)
    base = REACH * blocks - place_ref[0] * blocks
    keep = (lax.broadcasted_iota(jnp.int32, (BLOCK, BLOCK), 0)
            <= lax.broadcasted_iota(jnp.int32, (BLOCK, BLOCK), 1))

    def one_block(b, carry):
        cols = pl.ds(pl.multiple_of(b * BLOCK, BLOCK), BLOCK)
        acc_ref[...] = jnp.zeros_like(acc_ref)
        sums = []
        for h in range(heads):
            rows = slice(h * HEAD_DIM, (h + 1) * HEAD_DIM)
            sums.append(jnp.sum(grad_cols[b, rows].astype(F32) * att_ref[rows, cols].astype(F32),
                                axis=0, keepdims=True))

        def entry(slot, masked):
            for h in range(heads):
                rows = slice(h * HEAD_DIM, (h + 1) * HEAD_DIM)
                query = q_ref[rows, cols] * BF16(SCALE)
                grad = grad_cols[b, rows]
                scores = dot(key_rows[slot, h], query)
                if masked:
                    scores = jnp.where(keep, scores, NEG)
                probs = jnp.exp(scores - lse_ref[h, :, cols])
                grad_scores = (probs * (dot(value_rows[slot, h], grad) - sums[h])).astype(BF16)
                acc_ref[rows] += dot(key_cols[slot, rows], grad_scores)
                grad_keys[slot, rows] += dot(query, grad_scores, 1, 1)
                grad_values[slot, rows] += dot(grad, probs.astype(BF16), 1, 1)

        entry(lists_ref[b, 0] + base, True)

        @pl.loop(1, counts_ref[b])
        def _(j):
            entry(lists_ref[b, j] + base, False)

        dq_ref[:, cols] = (acc_ref[...] * SCALE).astype(BF16)
        return carry

    lax.fori_loop(0, blocks, one_block, 0)
    for distance, ref in enumerate((d0, d1, d2, d3, d4)):
        for b in range(blocks):
            slot = (REACH - distance) * blocks + b
            cols = slice(b * BLOCK, (b + 1) * BLOCK)
            ref[0, :, cols] = grad_keys[slot].astype(ref.dtype)
            ref[1, :, cols] = grad_values[slot].astype(ref.dtype)


def backward(lists, counts, place, queries, slabs, attended, lse, grads):
    width, tokens = queries.shape
    heads, blocks = width // HEAD_DIM, tokens // BLOCK
    slots = (REACH + 1) * blocks
    return pl.pallas_call(
        backward_kernel,
        out_shape=(jax.ShapeDtypeStruct((width, tokens), BF16),
                   jax.ShapeDtypeStruct((2, width, tokens), F32))
        + (jax.ShapeDtypeStruct((2, width, tokens), BF16),) * REACH,
        in_specs=smem(3) + vmem(12),
        out_specs=tuple(vmem(2 + REACH)),
        scratch_shapes=[
            pltpu.VMEM((slots, heads, BLOCK, HEAD_DIM), BF16),
            pltpu.VMEM((slots, heads, BLOCK, HEAD_DIM), BF16),
            pltpu.VMEM((slots, width, BLOCK), BF16),
            pltpu.VMEM((blocks, width, BLOCK), BF16),
            pltpu.VMEM((slots, width, BLOCK), F32),
            pltpu.VMEM((slots, width, BLOCK), F32),
            pltpu.VMEM((width, BLOCK), F32),
        ],
        compiler_params=pltpu.CompilerParams(vmem_limit_bytes=56 << 20),
        cost_estimate=pl.CostEstimate(
            flops=20 * 10 ** 9, bytes_accessed=12 << 20, transcendentals=10 ** 7),
    )(lists, counts, place, queries, *slabs, attended, lse, *grads)


def on_device(queries, key_rows, values, block_lists, counts, out_proj, stream, norm_gain,
              head_proj, patches, token_order, cotangent):
    width, tokens = queries.shape
    blocks = tokens // BLOCK
    cols = lax.axis_size("col")
    row, col = lax.axis_index("row"), lax.axis_index("col")
    odd = row % 2 == 1
    place = jnp.stack([row, col]).astype(jnp.int32)

    def token_block(array, b):
        return lax.dynamic_slice_in_dim(array, b * BLOCK, BLOCK, 0)

    own = jnp.stack([key_rows, values])
    slab2 = hop(own, 2)
    slab1 = mate(jnp.where(odd, slab2, own))
    slab4 = hop(slab2, 2)
    slab3 = mate(jnp.where(odd, slab4, slab2))
    slabs = (own, slab1, slab2, slab3, slab4)

    other = blocks - 1 - col
    order = token_block(token_order, other) % BLOCK
    grad_latent = mirror(
        permuted(scatter_kernel, order.reshape(1, BLOCK), token_block(cotangent, other)))
    weights = lax.all_gather(out_proj, "col", axis=0, tiled=True)

    attended, lse = forward(block_lists, counts, place, queries, slabs)

    def block_of(array, b):
        return lax.dynamic_slice_in_dim(array, b * BLOCK, BLOCK, 1)

    parts = [block_of(attended, col)] + [
        across(block_of(attended, jnp.bitwise_xor(col, k)), k) for k in range(1, cols)]
    latent, *grads = flow(
        place, parts, weights, token_block(stream, col), norm_gain.reshape(1, -1), head_proj,
        token_block(patches, col), grad_latent)
    grads = [grads[0]] + [across(grads[k], k) for k in range(1, cols)]

    reordered = permuted(gather_kernel, order.reshape(BLOCK, 1), mirror(latent))
    latent_out = lax.all_gather(reordered, "col", axis=0)[::-1].reshape(cotangent.shape)

    grad_queries, own_grad, part1, part2, part3, part4 = backward(
        block_lists, counts, place, queries, slabs, attended, lse, grads)
    zero = jnp.zeros_like(part1)
    from3 = mate(part3)
    from1 = mate(part1)
    far = hop(part4 + jnp.where(odd, from3, zero), -2)
    near = hop(part2 + jnp.where(odd, from1, from3) + far, -2)
    own_grad = own_grad + jnp.where(odd, zero, from1).astype(F32) + near.astype(F32)
    own_grad = own_grad.astype(BF16)
    return (latent_out, grad_queries, own_grad[0], own_grad[1])


def solution(mesh):
    return jax.shard_map(
        on_device,
        mesh=mesh,
        in_specs=(
            P("col", "row"),
            P("col", "row"),
            P("col", "row"),
            P("row", None),
            P("row"),
            P("col", None),
            P("row", None),
            P(),
            P(),
            P("row", None),
            P("row"),
            P("row", None),
        ),
        out_specs=(P("row", None), P("col", "row"), P("col", "row"), P("col", "row")),
        check_vma=False,
    )
```

```python
import functools

import jax
import jax.numpy as jnp
from jax import lax
from jax.experimental import pallas as pl
from jax.experimental.pallas import tpu as pltpu
from jax.sharding import PartitionSpec as P

HEAD_DIM = 64
BLOCK = 256
LIST = 16
REACH = 4

NEG = -1e30
EPS = 1e-05
SCALE = HEAD_DIM ** (-0.5)
F32 = jnp.float32
BF16 = jnp.bfloat16


def dot(a, b, ca=1, cb=0):
    return lax.dot_general(a, b, (((ca,), (cb,)), ((), ())), preferred_element_type=F32)


def vmem(count):
    return [pl.BlockSpec(memory_space=pltpu.VMEM)] * count


def smem(count):
    return [pl.BlockSpec(memory_space=pltpu.SMEM)] * count


def hop(array, by):
    size = lax.axis_size("row")
    pairs = [(i, i + by) for i in range(size) if 0 <= i + by < size]
    return lax.ppermute(array, "row", pairs)


def mate(array):
    return lax.ppermute(array, "row", [(i, i ^ 1) for i in range(lax.axis_size("row"))])


def upward(array):
    return lax.ppermute(array, "row", [(i, i + 1) for i in range(0, lax.axis_size("row"), 2)])


def downward(array):
    return lax.ppermute(array, "row", [(i + 1, i) for i in range(0, lax.axis_size("row"), 2)])


def mirror(array):
    size = lax.axis_size("row")
    return lax.ppermute(array, "row", [(i, size - 1 - i) for i in range(size)])


def across(array, bits):
    return lax.ppermute(array, "col", [(i, i ^ bits) for i in range(lax.axis_size("col"))])


def split3(x):
    hi = x.astype(BF16)
    rest = x - hi.astype(F32)
    mid = rest.astype(BF16)
    low = (rest - mid.astype(F32)).astype(BF16)
    return hi, mid, low


def scatter_kernel(order_ref, x_ref, o_ref):
    rows = lax.broadcasted_iota(jnp.int32, (BLOCK, BLOCK), 0)
    pick = (rows == order_ref[...]).astype(BF16)
    hi, mid, low = split3(x_ref[...])
    o_ref[...] = (dot(pick, hi) + dot(pick, mid)) + dot(pick, low)


def gather_kernel(order_ref, x_ref, o_ref):
    columns = lax.broadcasted_iota(jnp.int32, (BLOCK, BLOCK), 1)
    pick = (columns == order_ref[...]).astype(BF16)
    hi, mid, low = split3(x_ref[...])
    o_ref[...] = (dot(pick, hi) + dot(pick, mid)) + dot(pick, low)


def permuted(kernel, order, x):
    return pl.pallas_call(
        kernel,
        out_shape=jax.ShapeDtypeStruct(x.shape, F32),
        in_specs=vmem(2),
        out_specs=vmem(1)[0],
    )(order, x)


def live_slots(lists_ref, counts_ref, place_ref, regions, blocks, first, items_ref):
    row = place_ref[0]
    odd = lax.rem(row, 2)
    wanted = [jnp.where(odd == 1, region[1], region[0]) for region in regions]
    found = []
    for b in range(blocks):

        def look(j, count, b=b):
            block = lists_ref[b, j]
            distance = row - lax.div(block, blocks)
            slot, hit = 0, 0
            for r, want in enumerate(wanted):
                here = (distance == want).astype(jnp.int32)
                slot = slot + here * r * blocks
                hit = hit + here
            items_ref[b * LIST + count] = slot + lax.rem(block, blocks)
            return count + hit

        found.append(lax.fori_loop(first, counts_ref[b], look, 0))
    return found


def staged(place_ref, regions, refs, copy):
    odd = lax.rem(place_ref[0], 2)
    at = 0
    for r, region in enumerate(regions):
        if region[2] == "both":
            copy(r, refs[at])
            at += 1
            continue
        for parity in (0, 1):
            if region[parity] >= 0:
                pl.when(odd == parity)(lambda r=r, ref=refs[at]: copy(r, ref))
                at += 1


def region_inputs(regions):
    return sum(1 if region[2] == "both" else (region[0] >= 0) + (region[1] >= 0)
               for region in regions)


def causal():
    return (lax.broadcasted_iota(jnp.int32, (BLOCK, BLOCK), 0)
            <= lax.broadcasted_iota(jnp.int32, (BLOCK, BLOCK), 1))


def head_rows(h):
    return slice(h * HEAD_DIM, (h + 1) * HEAD_DIM)


def forward_kernel(regions, opening, closing, lists_ref, counts_ref, place_ref, q_ref, *refs):
    heads = q_ref.shape[0] // HEAD_DIM
    blocks = q_ref.shape[1] // BLOCK
    refs = list(refs)
    slabs = [refs.pop(0) for _ in range(region_inputs(regions))]
    if not opening:
        acc_in, stat_in = refs.pop(0), refs.pop(0)
    if closing:
        att_ref, lse_ref = refs.pop(0), refs.pop(0)
        key_rows, value_cols, items, acc_ref = refs
    else:
        acc_ref, stat_ref = refs.pop(0), refs.pop(0)
        key_rows, value_cols, items = refs

    def copy(r, ref):
        for b in range(blocks):
            slot, cols = r * blocks + b, slice(b * BLOCK, (b + 1) * BLOCK)
            value_cols[slot] = ref[1, :, cols]
            for h in range(heads):
                key_rows[slot, h] = ref[0, head_rows(h), cols].T

    staged(place_ref, regions, slabs, copy)
    found = live_slots(
        lists_ref, counts_ref, place_ref, regions, blocks, 1 if opening else 0, items)
    acc_ref[...] = jnp.zeros_like(acc_ref) if opening else acc_in[...]
    keep = causal()

    for b in range(blocks):
        cols = slice(b * BLOCK, (b + 1) * BLOCK)
        queries = [q_ref[head_rows(h), cols] * BF16(SCALE) for h in range(heads)]

        def entry(slot, state, masked, cols=cols, queries=queries):
            out = []
            for h in range(heads):
                rows = head_rows(h)
                top, total = state[2 * h], state[2 * h + 1]
                scores = dot(key_rows[slot, h], queries[h])
                if masked:
                    scores = jnp.where(keep, scores, NEG)
                newest = jnp.maximum(top, jnp.max(scores, axis=0, keepdims=True))
                weights = jnp.exp(scores - newest)
                fade = jnp.exp(top - newest)
                total = total * fade + jnp.sum(weights, axis=0, keepdims=True)
                acc_ref[rows, cols] = acc_ref[rows, cols] * fade + dot(
                    value_cols[slot, rows], weights.astype(BF16))
                out += [newest, total]
            return tuple(out)

        if opening:
            state = (jnp.full((1, BLOCK), NEG, F32), jnp.zeros((1, BLOCK), F32)) * heads
            state = entry(b, state, True)
        else:
            state = tuple(stat_in[i, :, cols] for i in range(2 * heads))
        state = lax.fori_loop(
            0, found[b], lambda i, s: entry(items[b * LIST + i], s, False), state)
        for h in range(heads):
            if closing:
                att_ref[head_rows(h), cols] = (
                    acc_ref[head_rows(h), cols] / state[2 * h + 1]).astype(BF16)
                lse_ref[h, :, cols] = state[2 * h] + jnp.log(state[2 * h + 1])
            else:
                stat_ref[2 * h, :, cols] = state[2 * h]
                stat_ref[2 * h + 1, :, cols] = state[2 * h + 1]


def forward(tables, queries, regions, slabs, state=None, closing=False, pairs=16):
    width, tokens = queries.shape
    heads = width // HEAD_DIM
    slots = len(regions) * (tokens // BLOCK)
    running = (jax.ShapeDtypeStruct((width, tokens), F32),
               jax.ShapeDtypeStruct((2 * heads, 1, tokens), F32))
    result = (jax.ShapeDtypeStruct((width, tokens), BF16),
              jax.ShapeDtypeStruct((heads, 1, tokens), F32))
    state = () if state is None else state
    return pl.pallas_call(
        functools.partial(forward_kernel, regions, not state, closing),
        out_shape=result if closing else running,
        in_specs=smem(3) + vmem(1 + len(slabs) + len(state)),
        out_specs=tuple(vmem(2)),
        scratch_shapes=[
            pltpu.VMEM((slots, heads, BLOCK, HEAD_DIM), BF16),
            pltpu.VMEM((slots, width, BLOCK), BF16),
            pltpu.SMEM((tokens // BLOCK * LIST,), jnp.int32),
        ] + [pltpu.VMEM((width, tokens), F32)] * closing,
        compiler_params=pltpu.CompilerParams(vmem_limit_bytes=48 << 20),
        cost_estimate=pl.CostEstimate(
            flops=pairs * 10 ** 9, bytes_accessed=6 << 20, transcendentals=pairs * 10 ** 5),
    )(*tables, queries, *slabs, *state)


def flow_kernel(place_ref, a0, a1, a2, a3, w_ref, stream_ref, gain_ref, head_ref, patch_ref,
                grad_ref, latent_ref, g0, g1, g2, g3, wide, back):
    width = a0.shape[0]
    channels = patch_ref.shape[1]
    me = place_ref[1]
    for k, ref in enumerate((a0, a1, a2, a3)):
        wide[pl.ds(pl.multiple_of(jnp.bitwise_xor(me, k) * width, width), width)] = ref[...]
    hidden = stream_ref[...].astype(F32) + dot(wide[...], w_ref[...], 0, 0)
    inverse = lax.rsqrt(jnp.mean(hidden * hidden, axis=-1, keepdims=True) + EPS)
    gain = gain_ref[...]
    normed = (hidden * inverse * gain).astype(BF16)
    shift = dot(normed, head_ref[:channels], 1, 1)
    log_scale = dot(normed, head_ref[channels:], 1, 1)
    factor = jnp.exp(-log_scale)
    latent = (patch_ref[...] - shift) * factor
    latent_ref[...] = latent
    grad = grad_ref[...]
    grad_shift = (-grad * factor).astype(BF16)
    grad_log = (-grad * latent - 1.0).astype(BF16)
    gained = (dot(grad_shift, head_ref[:channels]) + dot(grad_log, head_ref[channels:])) * gain
    grad_hidden = (
        inverse * gained
        - hidden * inverse ** 3 * jnp.mean(hidden * gained, axis=-1, keepdims=True)
    ).astype(BF16)
    back[...] = dot(w_ref[...], grad_hidden, 1, 1).astype(BF16)
    for k, ref in enumerate((g0, g1, g2, g3)):
        ref[...] = back[pl.ds(pl.multiple_of(jnp.bitwise_xor(me, k) * width, width), width)]


def flow(place, parts, weights, stream, gain, head_proj, patches, grad):
    width = parts[0].shape[0]
    return pl.pallas_call(
        flow_kernel,
        out_shape=(jax.ShapeDtypeStruct(patches.shape, F32),)
        + (jax.ShapeDtypeStruct((width, BLOCK), BF16),) * 4,
        in_specs=smem(1) + vmem(10),
        out_specs=tuple(vmem(5)),
        scratch_shapes=[pltpu.VMEM((4 * width, BLOCK), BF16)] * 2,
        compiler_params=pltpu.CompilerParams(vmem_limit_bytes=48 << 20),
    )(place, *parts, weights, stream, gain, head_proj, patches, grad)


def backward_kernel(regions, diagonal, last, lists_ref, counts_ref, place_ref, q_ref, att_ref,
                    lse_ref, g0, g1, g2, g3, *refs):
    heads = q_ref.shape[0] // HEAD_DIM
    blocks = q_ref.shape[1] // BLOCK
    refs = list(refs)
    slabs = [refs.pop(0) for _ in range(region_inputs(regions))]
    dq_in = None if len(refs) < 10 + len(regions) else refs.pop(0)
    dq_ref = refs.pop(0)
    outs = [refs.pop(0) for _ in regions]
    key_rows, value_rows, key_cols, grad_cols, grad_keys, grad_values, items, acc_ref = refs
    me = place_ref[1]
    for k, ref in enumerate((g0, g1, g2, g3)):
        grad_cols[jnp.bitwise_xor(me, k)] = ref[...]

    def copy(r, ref):
        for b in range(blocks):
            slot, cols = r * blocks + b, slice(b * BLOCK, (b + 1) * BLOCK)
            key_cols[slot] = ref[0, :, cols]
            for h in range(heads):
                key_rows[slot, h] = ref[0, head_rows(h), cols].T
                value_rows[slot, h] = ref[1, head_rows(h), cols].T

    staged(place_ref, regions, slabs, copy)
    grad_keys[...] = jnp.zeros_like(grad_keys)
    grad_values[...] = jnp.zeros_like(grad_values)
    found = live_slots(
        lists_ref, counts_ref, place_ref, regions, blocks, 1 if diagonal else 0, items)
    acc_ref[...] = jnp.zeros_like(acc_ref) if dq_in is None else dq_in[...]
    keep = causal()

    for b in range(blocks):
        cols = slice(b * BLOCK, (b + 1) * BLOCK)
        queries, grads, sums, tops = [], [], [], []
        for h in range(heads):
            rows = head_rows(h)
            queries.append(q_ref[rows, cols] * BF16(SCALE))
            grads.append(grad_cols[b, rows])
            sums.append(jnp.sum(grads[h].astype(F32) * att_ref[rows, cols].astype(F32),
                                axis=0, keepdims=True))
            tops.append(lse_ref[h, :, cols])

        def entry(slot, masked, cols=cols, queries=queries, grads=grads, sums=sums, tops=tops):
            for h in range(heads):
                rows = head_rows(h)
                scores = dot(key_rows[slot, h], queries[h])
                if masked:
                    scores = jnp.where(keep, scores, NEG)
                probs = jnp.exp(scores - tops[h])
                grad_scores = (
                    probs * (dot(value_rows[slot, h], grads[h]) - sums[h])).astype(BF16)
                acc_ref[rows, cols] += dot(key_cols[slot, rows], grad_scores)
                grad_keys[slot, rows] += dot(queries[h], grad_scores, 1, 1)
                grad_values[slot, rows] += dot(grads[h], probs.astype(BF16), 1, 1)

        if diagonal:
            entry(b, True)

        @pl.loop(0, found[b])
        def _(i, b=b, entry=entry):
            entry(items[b * LIST + i], False)

    if last:
        dq_ref[...] = (acc_ref[...] * SCALE).astype(BF16)
    else:
        dq_ref[...] = acc_ref[...]
    for r, ref in enumerate(outs):
        for b in range(blocks):
            cols = slice(b * BLOCK, (b + 1) * BLOCK)
            ref[0, :, cols] = grad_keys[r * blocks + b].astype(ref.dtype)
            ref[1, :, cols] = grad_values[r * blocks + b].astype(ref.dtype)


def backward(tables, queries, attended, lse, grads, regions, slabs, dq=None, last=False, pairs=16):
    width, tokens = queries.shape
    heads, blocks = width // HEAD_DIM, tokens // BLOCK
    slots = len(regions) * blocks
    diagonal = regions[0][0] == 0
    given = () if dq is None else (dq,)
    return pl.pallas_call(
        functools.partial(backward_kernel, regions, diagonal, last),
        out_shape=(jax.ShapeDtypeStruct((width, tokens), BF16 if last else F32),)
        + (jax.ShapeDtypeStruct((2, width, tokens), F32 if diagonal else BF16),) * len(regions),
        in_specs=smem(3) + vmem(7 + len(slabs) + len(given)),
        out_specs=tuple(vmem(1 + len(regions))),
        scratch_shapes=[
            pltpu.VMEM((slots, heads, BLOCK, HEAD_DIM), BF16),
            pltpu.VMEM((slots, heads, BLOCK, HEAD_DIM), BF16),
            pltpu.VMEM((slots, width, BLOCK), BF16),
            pltpu.VMEM((blocks, width, BLOCK), BF16),
            pltpu.VMEM((slots, width, BLOCK), F32),
            pltpu.VMEM((slots, width, BLOCK), F32),
            pltpu.SMEM((blocks * LIST,), jnp.int32),
            pltpu.VMEM((width, tokens), F32),
        ],
        compiler_params=pltpu.CompilerParams(vmem_limit_bytes=48 << 20),
        cost_estimate=pl.CostEstimate(
            flops=pairs * 10 ** 9, bytes_accessed=8 << 20, transcendentals=pairs * 10 ** 5),
    )(*tables, queries, attended, lse, *grads, *slabs, *given)


def on_device(queries, key_rows, values, block_lists, counts, out_proj, stream, norm_gain,
              head_proj, patches, token_order, cotangent):
    width, tokens = queries.shape
    blocks = tokens // BLOCK
    cols = lax.axis_size("col")
    row, col = lax.axis_index("row"), lax.axis_index("col")
    odd = row % 2 == 1
    place = jnp.stack([row, col]).astype(jnp.int32)

    def token_block(array, b):
        return lax.dynamic_slice_in_dim(array, b * BLOCK, BLOCK, 0)

    tables = (block_lists, counts, place)
    own = jnp.stack([key_rows, values])
    slab2 = hop(own, 2)
    up1 = upward(own)
    slab4 = hop(slab2, 2)
    up2 = upward(slab2)
    down1 = downward(slab2)
    down2 = downward(slab4)

    other = blocks - 1 - col
    order = token_block(token_order, other) % BLOCK
    grad_latent = mirror(
        permuted(scatter_kernel, order.reshape(1, BLOCK), token_block(cotangent, other)))
    weights = lax.all_gather(out_proj, "col", axis=0, tiled=True)

    state = forward(tables, queries, [(0, 0, "both")], [own], pairs=10)
    state = forward(tables, queries, [(2, 2, "both"), (-1, 1, "one")], [slab2, up1], state,
                    pairs=20)
    state = forward(tables, queries, [(4, 4, "both"), (1, 3, "each")], [slab4, down1, up2], state,
                    pairs=20)
    attended, lse = forward(tables, queries, [(3, -1, "one")], [down2], state, True, pairs=8)

    def block_of(array, b):
        return lax.dynamic_slice_in_dim(array, b * BLOCK, BLOCK, 1)

    parts = [block_of(attended, col)] + [
        across(block_of(attended, jnp.bitwise_xor(col, k)), k) for k in range(1, cols)]
    latent, *grads = flow(
        place, parts, weights, token_block(stream, col), norm_gain.reshape(1, -1), head_proj,
        token_block(patches, col), grad_latent)
    *grads, mirrored = lax.optimization_barrier(
        [grads[0]] + [across(grads[k], k) for k in range(1, cols)] + [mirror(latent)])

    shared = (tables, queries, attended, lse, grads)
    grad_queries, part3, part4 = backward(
        *shared, [(3, 3, "each"), (4, 4, "both")], [down2, up2, slab4], pairs=20)
    from3 = mate(part3)
    reordered = permuted(gather_kernel, order.reshape(BLOCK, 1), mirrored)
    grad_queries, reordered = lax.optimization_barrier((grad_queries, reordered))
    pieces = [reordered] + [across(reordered, k) for k in range(1, cols)]
    grad_queries, part1 = backward(
        *shared, [(1, 1, "each")], [down1, up1], grad_queries, pairs=20)
    from1 = mate(part1)
    zero = jnp.zeros_like(part1)
    far = part4 + jnp.where(odd, from3, zero)
    grad_queries, far, *pieces = lax.optimization_barrier([grad_queries, far] + pieces)
    far = hop(far, -2)
    grad_queries, part2 = backward(*shared, [(2, 2, "both")], [slab2], grad_queries, pairs=20)
    near = part2 + jnp.where(odd, from1, from3) + far
    grad_queries, near = lax.optimization_barrier((grad_queries, near))
    near = hop(near, -2)
    grad_queries, own_grad = backward(
        *shared, [(0, 0, "both")], [own], grad_queries, True, pairs=10)
    latent_out = jnp.zeros((blocks, BLOCK, patches.shape[1]), F32)
    for k, piece in enumerate(pieces):
        latent_out = lax.dynamic_update_index_in_dim(
            latent_out, piece, blocks - 1 - jnp.bitwise_xor(col, k), 0)
    latent_out = latent_out.reshape(cotangent.shape)
    own_grad = own_grad + jnp.where(odd, zero, from1).astype(F32) + near.astype(F32)
    own_grad = own_grad.astype(BF16)
    return (latent_out, grad_queries, own_grad[0], own_grad[1])


def solution(mesh):
    return jax.shard_map(
        on_device,
        mesh=mesh,
        in_specs=(
            P("col", "row"),
            P("col", "row"),
            P("col", "row"),
            P("row", None),
            P("row"),
            P("col", None),
            P("row", None),
            P(),
            P(),
            P("row", None),
            P("row"),
            P("row", None),
        ),
        out_specs=(P("row", None), P("col", "row"), P("col", "row"), P("col", "row")),
        check_vma=False,
    )
```

```python
import functools

import jax
import jax.numpy as jnp
from jax import lax
from jax.experimental import pallas as pl
from jax.experimental.pallas import tpu as pltpu
from jax.sharding import PartitionSpec as P

HEAD_DIM = 64
BLOCK = 256
LIST = 16
REACH = 4

NEG = -1e30
EPS = 1e-05
SCALE = HEAD_DIM ** (-0.5)
F32 = jnp.float32
BF16 = jnp.bfloat16


def dot(a, b, ca=1, cb=0):
    return lax.dot_general(a, b, (((ca,), (cb,)), ((), ())), preferred_element_type=F32)


def vmem(count):
    return [pl.BlockSpec(memory_space=pltpu.VMEM)] * count


def smem(count):
    return [pl.BlockSpec(memory_space=pltpu.SMEM)] * count


def hop(array, by):
    size = lax.axis_size("row")
    pairs = [(i, i + by) for i in range(size) if 0 <= i + by < size]
    return lax.ppermute(array, "row", pairs)


def mate(array):
    return lax.ppermute(array, "row", [(i, i ^ 1) for i in range(lax.axis_size("row"))])


def upward(array):
    return lax.ppermute(array, "row", [(i, i + 1) for i in range(0, lax.axis_size("row"), 2)])


def downward(array):
    return lax.ppermute(array, "row", [(i + 1, i) for i in range(0, lax.axis_size("row"), 2)])


def mirror(array):
    size = lax.axis_size("row")
    return lax.ppermute(array, "row", [(i, size - 1 - i) for i in range(size)])


def across(array, bits):
    return lax.ppermute(array, "col", [(i, i ^ bits) for i in range(lax.axis_size("col"))])


def split3(x):
    hi = x.astype(BF16)
    rest = x - hi.astype(F32)
    mid = rest.astype(BF16)
    low = (rest - mid.astype(F32)).astype(BF16)
    return hi, mid, low


def picked(place_ref, order_ref, blocks):
    cols = pl.ds(pl.multiple_of((blocks - 1 - place_ref[1]) * BLOCK, BLOCK), BLOCK)
    rows = lax.broadcasted_iota(jnp.int32, (BLOCK, BLOCK), 0)
    return (rows == lax.rem(order_ref[:, cols], BLOCK)).astype(BF16), cols


def scatter_kernel(place_ref, order_ref, x_ref, o_ref):
    pick, cols = picked(place_ref, order_ref, x_ref.shape[1] // BLOCK)
    hi, mid, low = split3(x_ref[:, cols])
    o_ref[...] = (dot(hi, pick, 1, 1) + dot(mid, pick, 1, 1)) + dot(low, pick, 1, 1)


def gather_kernel(place_ref, order_ref, x_ref, o_ref):
    pick, _ = picked(place_ref, order_ref, order_ref.shape[1] // BLOCK)
    hi, mid, low = split3(x_ref[...])
    o_ref[...] = (dot(hi, pick) + dot(mid, pick)) + dot(low, pick)


def permuted(kernel, place, order, x):
    return pl.pallas_call(
        kernel,
        out_shape=jax.ShapeDtypeStruct((x.shape[0], BLOCK), F32),
        in_specs=smem(1) + vmem(2),
        out_specs=vmem(1)[0],
    )(place, order, x)


def assemble_kernel(place_ref, p0, p1, p2, p3, o_ref):
    blocks = o_ref.shape[1] // BLOCK
    for k, ref in enumerate((p0, p1, p2, p3)):
        at = (blocks - 1 - jnp.bitwise_xor(place_ref[1], k)) * BLOCK
        o_ref[:, pl.ds(pl.multiple_of(at, BLOCK), BLOCK)] = ref[...]


def assembled(place, pieces, tokens):
    return pl.pallas_call(
        assemble_kernel,
        out_shape=jax.ShapeDtypeStruct((pieces[0].shape[0], tokens), F32),
        in_specs=smem(1) + vmem(4),
        out_specs=vmem(1)[0],
    )(place, *pieces)


def live_slots(lists_ref, counts_ref, place_ref, regions, blocks, first, items_ref):
    row = place_ref[0]
    odd = lax.rem(row, 2)
    wanted = [jnp.where(odd == 1, region[1], region[0]) for region in regions]
    found = []
    for b in range(blocks):

        def look(j, count, b=b):
            block = lists_ref[b, j]
            distance = row - lax.div(block, blocks)
            slot, hit = 0, 0
            for r, want in enumerate(wanted):
                here = (distance == want).astype(jnp.int32)
                slot = slot + here * r * blocks
                hit = hit + here
            items_ref[b * LIST + count] = slot + lax.rem(block, blocks)
            return count + hit

        found.append(lax.fori_loop(first, counts_ref[b], look, 0))
    return found


def staged(place_ref, regions, refs, copy):
    odd = lax.rem(place_ref[0], 2)
    at = 0
    for r, region in enumerate(regions):
        if region[2] == "both":
            copy(r, refs[at])
            at += 1
            continue
        for parity in (0, 1):
            if region[parity] >= 0:
                pl.when(odd == parity)(lambda r=r, ref=refs[at]: copy(r, ref))
                at += 1


def region_inputs(regions):
    return sum(1 if region[2] == "both" else (region[0] >= 0) + (region[1] >= 0)
               for region in regions)


def causal():
    return (lax.broadcasted_iota(jnp.int32, (BLOCK, BLOCK), 0)
            <= lax.broadcasted_iota(jnp.int32, (BLOCK, BLOCK), 1))


def head_rows(h):
    return slice(h * HEAD_DIM, (h + 1) * HEAD_DIM)


def forward_kernel(regions, opening, closing, lists_ref, counts_ref, place_ref, q_ref, *refs):
    heads = q_ref.shape[0] // HEAD_DIM
    blocks = q_ref.shape[1] // BLOCK
    refs = list(refs)
    slabs = [refs.pop(0) for _ in range(region_inputs(regions))]
    if not opening:
        acc_in, stat_in = refs.pop(0), refs.pop(0)
    if closing:
        att_ref, lse_ref = refs.pop(0), refs.pop(0)
        key_rows, value_cols, items, acc_ref = refs
    else:
        acc_ref, stat_ref = refs.pop(0), refs.pop(0)
        key_rows, value_cols, items = refs

    def copy(r, ref):
        for b in range(blocks):
            slot, cols = r * blocks + b, slice(b * BLOCK, (b + 1) * BLOCK)
            value_cols[slot] = ref[1, :, cols]
            for h in range(heads):
                key_rows[slot, h] = ref[0, head_rows(h), cols].T

    staged(place_ref, regions, slabs, copy)
    found = live_slots(
        lists_ref, counts_ref, place_ref, regions, blocks, 1 if opening else 0, items)
    acc_ref[...] = jnp.zeros_like(acc_ref) if opening else acc_in[...]
    keep = causal()

    for b in range(blocks):
        cols = slice(b * BLOCK, (b + 1) * BLOCK)
        queries = [q_ref[head_rows(h), cols] * BF16(SCALE) for h in range(heads)]

        def entry(slot, state, masked, cols=cols, queries=queries):
            out = []
            for h in range(heads):
                rows = head_rows(h)
                top, total = state[2 * h], state[2 * h + 1]
                scores = dot(key_rows[slot, h], queries[h])
                if masked:
                    scores = jnp.where(keep, scores, NEG)
                newest = jnp.maximum(top, jnp.max(scores, axis=0, keepdims=True))
                weights = jnp.exp(scores - newest)
                fade = jnp.exp(top - newest)
                total = total * fade + jnp.sum(weights, axis=0, keepdims=True)
                acc_ref[rows, cols] = acc_ref[rows, cols] * fade + dot(
                    value_cols[slot, rows], weights.astype(BF16))
                out += [newest, total]
            return tuple(out)

        if opening:
            state = (jnp.full((1, BLOCK), NEG, F32), jnp.zeros((1, BLOCK), F32)) * heads
            state = entry(b, state, True)
        else:
            state = tuple(stat_in[i, :, cols] for i in range(2 * heads))
        state = lax.fori_loop(
            0, found[b], lambda i, s: entry(items[b * LIST + i], s, False), state)
        for h in range(heads):
            if closing:
                att_ref[head_rows(h), cols] = (
                    acc_ref[head_rows(h), cols] / state[2 * h + 1]).astype(BF16)
                lse_ref[h, :, cols] = state[2 * h] + jnp.log(state[2 * h + 1])
            else:
                stat_ref[2 * h, :, cols] = state[2 * h]
                stat_ref[2 * h + 1, :, cols] = state[2 * h + 1]


def forward(tables, queries, regions, slabs, state=None, closing=False, pairs=1):
    width, tokens = queries.shape
    heads = width // HEAD_DIM
    slots = len(regions) * (tokens // BLOCK)
    running = (jax.ShapeDtypeStruct((width, tokens), F32),
               jax.ShapeDtypeStruct((2 * heads, 1, tokens), F32))
    result = (jax.ShapeDtypeStruct((width, tokens), BF16),
              jax.ShapeDtypeStruct((heads, 1, tokens), F32))
    state = () if state is None else state
    return pl.pallas_call(
        functools.partial(forward_kernel, regions, not state, closing),
        out_shape=result if closing else running,
        in_specs=smem(3) + vmem(1 + len(slabs) + len(state)),
        out_specs=tuple(vmem(2)),
        scratch_shapes=[
            pltpu.VMEM((slots, heads, BLOCK, HEAD_DIM), BF16),
            pltpu.VMEM((slots, width, BLOCK), BF16),
            pltpu.SMEM((tokens // BLOCK * LIST,), jnp.int32),
        ] + [pltpu.VMEM((width, tokens), F32)] * closing,
        compiler_params=pltpu.CompilerParams(vmem_limit_bytes=48 << 20),
        cost_estimate=pl.CostEstimate(
            flops=pairs * 10 ** 9, bytes_accessed=6 << 20, transcendentals=pairs * 10 ** 5),
    )(*tables, queries, *slabs, *state)


def flow_kernel(place_ref, a0, a1, a2, a3, w0, w1, w2, w3, stream_ref, gain_ref, head_ref,
                patch_ref, grad_ref, latent_ref, g0, g1, g2, g3, wide, weights):
    width = a0.shape[0]
    channels = patch_ref.shape[0]
    cols = pl.ds(pl.multiple_of(place_ref[1] * BLOCK, BLOCK), BLOCK)
    for k, (part, weight) in enumerate(zip((a0, a1, a2, a3), (w0, w1, w2, w3))):
        wide[k * width:(k + 1) * width] = part[...]
        weights[k * width:(k + 1) * width] = weight[...]
    hidden = stream_ref[cols].astype(F32) + dot(wide[...], weights[...], 0, 0)
    inverse = lax.rsqrt(jnp.mean(hidden * hidden, axis=-1, keepdims=True) + EPS)
    gain = gain_ref[...]
    normed = (hidden * inverse * gain).astype(BF16)
    params = dot(head_ref[...], normed, 1, 1)
    factor = jnp.exp(-params[channels:])
    latent = (patch_ref[:, cols] - params[:channels]) * factor
    latent_ref[...] = latent
    grad = grad_ref[...]
    grad_params = jnp.concatenate([-grad * factor, -grad * latent - 1.0], axis=0).astype(BF16)
    gained = dot(grad_params, head_ref[...], 0, 0) * gain
    grad_hidden = (
        inverse * gained
        - hidden * inverse ** 3 * jnp.mean(hidden * gained, axis=-1, keepdims=True)
    ).astype(BF16)
    wide[...] = dot(weights[...], grad_hidden, 1, 1).astype(BF16)
    for k, ref in enumerate((g0, g1, g2, g3)):
        ref[...] = wide[k * width:(k + 1) * width]


def flow(place, parts, weights, stream, gain, head_proj, patches, grad):
    width = parts[0].shape[0]
    return pl.pallas_call(
        flow_kernel,
        out_shape=(jax.ShapeDtypeStruct(grad.shape, F32),)
        + (jax.ShapeDtypeStruct((width, BLOCK), BF16),) * 4,
        in_specs=smem(1) + vmem(13),
        out_specs=tuple(vmem(5)),
        scratch_shapes=[
            pltpu.VMEM((4 * width, BLOCK), BF16), pltpu.VMEM((4 * width, stream.shape[1]), BF16)],
        compiler_params=pltpu.CompilerParams(vmem_limit_bytes=48 << 20),
    )(place, *parts, *weights, stream, gain, head_proj, patches, grad)


def backward_kernel(regions, diagonal, last, lists_ref, counts_ref, place_ref, q_ref, att_ref,
                    lse_ref, g0, g1, g2, g3, *refs):
    heads = q_ref.shape[0] // HEAD_DIM
    blocks = q_ref.shape[1] // BLOCK
    refs = list(refs)
    slabs = [refs.pop(0) for _ in range(region_inputs(regions))]
    dq_in = None if len(refs) < 10 + len(regions) else refs.pop(0)
    dq_ref = refs.pop(0)
    outs = [refs.pop(0) for _ in regions]
    key_rows, value_rows, key_cols, grad_cols, grad_keys, grad_values, items, acc_ref = refs
    me = place_ref[1]
    for k, ref in enumerate((g0, g1, g2, g3)):
        grad_cols[jnp.bitwise_xor(me, k)] = ref[...]

    def copy(r, ref):
        for b in range(blocks):
            slot, cols = r * blocks + b, slice(b * BLOCK, (b + 1) * BLOCK)
            key_cols[slot] = ref[0, :, cols]
            for h in range(heads):
                key_rows[slot, h] = ref[0, head_rows(h), cols].T
                value_rows[slot, h] = ref[1, head_rows(h), cols].T

    staged(place_ref, regions, slabs, copy)
    grad_keys[...] = jnp.zeros_like(grad_keys)
    grad_values[...] = jnp.zeros_like(grad_values)
    found = live_slots(
        lists_ref, counts_ref, place_ref, regions, blocks, 1 if diagonal else 0, items)
    acc_ref[...] = jnp.zeros_like(acc_ref) if dq_in is None else dq_in[...]
    keep = causal()

    for b in range(blocks):
        cols = slice(b * BLOCK, (b + 1) * BLOCK)
        queries, grads, sums, tops = [], [], [], []
        for h in range(heads):
            rows = head_rows(h)
            queries.append(q_ref[rows, cols] * BF16(SCALE))
            grads.append(grad_cols[b, rows])
            sums.append(jnp.sum(grads[h].astype(F32) * att_ref[rows, cols].astype(F32),
                                axis=0, keepdims=True))
            tops.append(lse_ref[h, :, cols])

        def entry(slot, masked, cols=cols, queries=queries, grads=grads, sums=sums, tops=tops):
            for h in range(heads):
                rows = head_rows(h)
                scores = dot(key_rows[slot, h], queries[h])
                if masked:
                    scores = jnp.where(keep, scores, NEG)
                probs = jnp.exp(scores - tops[h])
                grad_scores = (
                    probs * (dot(value_rows[slot, h], grads[h]) - sums[h])).astype(BF16)
                acc_ref[rows, cols] += dot(key_cols[slot, rows], grad_scores)
                grad_keys[slot, rows] += dot(queries[h], grad_scores, 1, 1)
                grad_values[slot, rows] += dot(grads[h], probs.astype(BF16), 1, 1)

        if diagonal:
            entry(b, True)

        @pl.loop(0, found[b])
        def _(i, b=b, entry=entry):
            entry(items[b * LIST + i], False)

    if last:
        dq_ref[...] = (acc_ref[...] * SCALE).astype(BF16)
    else:
        dq_ref[...] = acc_ref[...]
    for r, ref in enumerate(outs):
        for b in range(blocks):
            cols = slice(b * BLOCK, (b + 1) * BLOCK)
            ref[0, :, cols] = grad_keys[r * blocks + b].astype(ref.dtype)
            ref[1, :, cols] = grad_values[r * blocks + b].astype(ref.dtype)


def backward(tables, queries, attended, lse, grads, regions, slabs, dq=None, last=False, pairs=1):
    width, tokens = queries.shape
    heads, blocks = width // HEAD_DIM, tokens // BLOCK
    slots = len(regions) * blocks
    diagonal = regions[0][0] == 0
    given = () if dq is None else (dq,)
    return pl.pallas_call(
        functools.partial(backward_kernel, regions, diagonal, last),
        out_shape=(jax.ShapeDtypeStruct((width, tokens), BF16 if last else F32),)
        + (jax.ShapeDtypeStruct((2, width, tokens), F32 if diagonal else BF16),) * len(regions),
        in_specs=smem(3) + vmem(7 + len(slabs) + len(given)),
        out_specs=tuple(vmem(1 + len(regions))),
        scratch_shapes=[
            pltpu.VMEM((slots, heads, BLOCK, HEAD_DIM), BF16),
            pltpu.VMEM((slots, heads, BLOCK, HEAD_DIM), BF16),
            pltpu.VMEM((slots, width, BLOCK), BF16),
            pltpu.VMEM((blocks, width, BLOCK), BF16),
            pltpu.VMEM((slots, width, BLOCK), F32),
            pltpu.VMEM((slots, width, BLOCK), F32),
            pltpu.SMEM((blocks * LIST,), jnp.int32),
            pltpu.VMEM((width, tokens), F32),
        ],
        compiler_params=pltpu.CompilerParams(vmem_limit_bytes=48 << 20),
        cost_estimate=pl.CostEstimate(
            flops=pairs * 10 ** 9, bytes_accessed=8 << 20, transcendentals=pairs * 10 ** 5),
    )(*tables, queries, attended, lse, *grads, *slabs, *given)


def on_device(queries, key_rows, values, block_lists, counts, out_proj, stream, norm_gain,
              head_proj, patches, token_order, cotangent):
    width, tokens = queries.shape
    cols = lax.axis_size("col")
    row, col = lax.axis_index("row"), lax.axis_index("col")
    odd = row % 2 == 1
    place = jnp.stack([row, col]).astype(jnp.int32)

    tables = (block_lists, counts, place)
    own = jnp.stack([key_rows, values])
    slab2 = hop(own, 2)
    state = forward(tables, queries, [(0, 0, "both")], [own], pairs=1)
    *state, slab2, out_proj = lax.optimization_barrier([*state, slab2, out_proj])
    up1 = upward(own)
    slab4 = hop(slab2, 2)
    up2 = upward(slab2)
    down1 = downward(slab2)

    order = token_order.reshape(1, tokens)
    grad_latent = mirror(permuted(scatter_kernel, place, order, cotangent.T))
    weights = [out_proj] + [across(out_proj, k) for k in range(1, cols)]

    state = forward(tables, queries, [(2, 2, "both")], [slab2], tuple(state), pairs=1)
    *state, slab4 = lax.optimization_barrier([*state, slab4])
    down2 = downward(slab4)
    state = forward(tables, queries, [(1, 1, "each")], [down1, up1], tuple(state), pairs=1)
    state = forward(tables, queries, [(4, 4, "both"), (-1, 3, "one")], [slab4, up2], state,
                    pairs=1)
    attended, lse = forward(tables, queries, [(3, -1, "one")], [down2], state, True, pairs=1)

    def block_of(array, b):
        return lax.dynamic_slice_in_dim(array, b * BLOCK, BLOCK, 1)

    parts = [block_of(attended, col)] + [
        across(block_of(attended, jnp.bitwise_xor(col, k)), k) for k in range(1, cols)]
    latent, *grads = flow(
        place, parts, weights, stream, norm_gain.reshape(1, -1), head_proj, patches.T,
        grad_latent)
    *grads, mirrored = lax.optimization_barrier(
        [grads[0]] + [across(grads[k], k) for k in range(1, cols)] + [mirror(latent)])

    shared = (tables, queries, attended, lse, grads)
    grad_queries, part3, part4 = backward(
        *shared, [(3, 3, "each"), (4, 4, "both")], [down2, up2, slab4], pairs=1)
    from3 = mate(part3)
    reordered = permuted(gather_kernel, place, order, mirrored)
    grad_queries, reordered = lax.optimization_barrier((grad_queries, reordered))
    pieces = [reordered] + [across(reordered, k) for k in range(1, cols)]
    grad_queries, part1 = backward(
        *shared, [(1, 1, "each")], [down1, up1], grad_queries, pairs=1)
    from1 = mate(part1)
    zero = jnp.zeros_like(part1)
    far = part4 + jnp.where(odd, from3, zero)
    grad_queries, far, *pieces = lax.optimization_barrier([grad_queries, far] + pieces)
    far = hop(far, -2)
    latent_out = assembled(place, pieces, tokens).T
    grad_queries, part2 = backward(*shared, [(2, 2, "both")], [slab2], grad_queries, pairs=1)
    near = part2 + jnp.where(odd, from1, from3) + far
    grad_queries, near = lax.optimization_barrier((grad_queries, near))
    near = hop(near, -2)
    grad_queries, own_grad = backward(
        *shared, [(0, 0, "both")], [own], grad_queries, True, pairs=1)
    own_grad = own_grad + jnp.where(odd, zero, from1).astype(F32) + near.astype(F32)
    own_grad = own_grad.astype(BF16)
    return (latent_out, grad_queries, own_grad[0], own_grad[1])


def solution(mesh):
    return jax.shard_map(
        on_device,
        mesh=mesh,
        in_specs=(
            P("col", "row"),
            P("col", "row"),
            P("col", "row"),
            P("row", None),
            P("row"),
            P("col", None),
            P("row", None),
            P(),
            P(),
            P("row", None),
            P("row"),
            P("row", None),
        ),
        out_specs=(P("row", None), P("col", "row"), P("col", "row"), P("col", "row")),
        check_vma=False,
    )
```

```python
import functools

import jax
import jax.numpy as jnp
from jax import lax
from jax.experimental import pallas as pl
from jax.experimental.pallas import tpu as pltpu
from jax.sharding import PartitionSpec as P

HEAD_DIM = 64
BLOCK = 256
LIST = 16
REACH = 4

NEG = -1e30
EPS = 1e-05
SCALE = HEAD_DIM ** (-0.5)
F32 = jnp.float32
BF16 = jnp.bfloat16


def dot(a, b, ca=1, cb=0):
    return lax.dot_general(a, b, (((ca,), (cb,)), ((), ())), preferred_element_type=F32)


def vmem(count):
    return [pl.BlockSpec(memory_space=pltpu.VMEM)] * count


def smem(count):
    return [pl.BlockSpec(memory_space=pltpu.SMEM)] * count


def hop(array, by):
    size = lax.axis_size("row")
    pairs = [(i, i + by) for i in range(size) if 0 <= i + by < size]
    return lax.ppermute(array, "row", pairs)


def mate(array):
    return lax.ppermute(array, "row", [(i, i ^ 1) for i in range(lax.axis_size("row"))])


def upward(array):
    return lax.ppermute(array, "row", [(i, i + 1) for i in range(0, lax.axis_size("row"), 2)])


def downward(array):
    return lax.ppermute(array, "row", [(i + 1, i) for i in range(0, lax.axis_size("row"), 2)])


def mirror(array):
    size = lax.axis_size("row")
    return lax.ppermute(array, "row", [(i, size - 1 - i) for i in range(size)])


def across(array, bits):
    return lax.ppermute(array, "col", [(i, i ^ bits) for i in range(lax.axis_size("col"))])


def split3(x):
    hi = x.astype(BF16)
    rest = x - hi.astype(F32)
    mid = rest.astype(BF16)
    low = (rest - mid.astype(F32)).astype(BF16)
    return hi, mid, low


def picked(place_ref, order_ref, blocks):
    cols = pl.ds(pl.multiple_of((blocks - 1 - place_ref[1]) * BLOCK, BLOCK), BLOCK)
    rows = lax.broadcasted_iota(jnp.int32, (BLOCK, BLOCK), 0)
    return (rows == lax.rem(order_ref[:, cols], BLOCK)).astype(BF16), cols


def scatter_kernel(place_ref, order_ref, x_ref, o_ref):
    pick, cols = picked(place_ref, order_ref, x_ref.shape[1] // BLOCK)
    hi, mid, low = split3(x_ref[:, cols])
    o_ref[...] = (dot(hi, pick, 1, 1) + dot(mid, pick, 1, 1)) + dot(low, pick, 1, 1)


def gather_kernel(place_ref, order_ref, x_ref, o_ref):
    pick, _ = picked(place_ref, order_ref, order_ref.shape[1] // BLOCK)
    hi, mid, low = split3(x_ref[...])
    o_ref[...] = (dot(hi, pick) + dot(mid, pick)) + dot(low, pick)


def permuted(kernel, place, order, x):
    return pl.pallas_call(
        kernel,
        out_shape=jax.ShapeDtypeStruct((x.shape[0], BLOCK), F32),
        in_specs=smem(1) + vmem(2),
        out_specs=vmem(1)[0],
    )(place, order, x)


def assemble_kernel(place_ref, p0, p1, p2, p3, o_ref):
    blocks = o_ref.shape[1] // BLOCK
    for k, ref in enumerate((p0, p1, p2, p3)):
        at = (blocks - 1 - jnp.bitwise_xor(place_ref[1], k)) * BLOCK
        o_ref[:, pl.ds(pl.multiple_of(at, BLOCK), BLOCK)] = ref[...]


def assembled(place, pieces, tokens):
    return pl.pallas_call(
        assemble_kernel,
        out_shape=jax.ShapeDtypeStruct((pieces[0].shape[0], tokens), F32),
        in_specs=smem(1) + vmem(4),
        out_specs=vmem(1)[0],
    )(place, *pieces)


def live_items(lists_ref, counts_ref, place_ref, regions, blocks, first, items_ref, together):
    row = place_ref[0]
    odd = lax.rem(row, 2)
    slots = len(regions) * blocks
    wanted = [jnp.where(odd == 1, region[1], region[0]) for region in regions]
    found = []
    total = 0
    for b in range(blocks):

        def look(j, count, b=b):
            block = lists_ref[b, j]
            distance = row - lax.div(block, blocks)
            slot, hit = b * slots, 0
            for r, want in enumerate(wanted):
                here = (distance == want).astype(jnp.int32)
                slot = slot + here * r * blocks
                hit = hit + here
            items_ref[count] = slot + lax.rem(block, blocks)
            return count + hit

        start = total if together else b * LIST
        total = lax.fori_loop(first, counts_ref[b], look, start)
        found.append(total - start)
    return total if together else found


def staged(place_ref, regions, refs, copy):
    odd = lax.rem(place_ref[0], 2)
    at = 0
    for r, region in enumerate(regions):
        if region[2] == "both":
            copy(r, refs[at])
            at += 1
            continue
        for parity in (0, 1):
            if region[parity] >= 0:
                pl.when(odd == parity)(lambda r=r, ref=refs[at]: copy(r, ref))
                at += 1


def region_inputs(regions):
    return sum(1 if region[2] == "both" else (region[0] >= 0) + (region[1] >= 0)
               for region in regions)


def causal():
    return (lax.broadcasted_iota(jnp.int32, (BLOCK, BLOCK), 0)
            <= lax.broadcasted_iota(jnp.int32, (BLOCK, BLOCK), 1))


def head_rows(h):
    return slice(h * HEAD_DIM, (h + 1) * HEAD_DIM)


def forward_kernel(regions, opening, closing, lists_ref, counts_ref, place_ref, q_ref, *refs):
    heads = q_ref.shape[0] // HEAD_DIM
    blocks = q_ref.shape[1] // BLOCK
    slots = len(regions) * blocks
    refs = list(refs)
    slabs = [refs.pop(0) for _ in range(region_inputs(regions))]
    if not opening:
        acc_in, stat_in = refs.pop(0), refs.pop(0)
    if closing:
        att_ref, lse_ref = refs.pop(0), refs.pop(0)
    else:
        acc_out, stat_out = refs.pop(0), refs.pop(0)
    key_rows, value_cols, scaled, items, found_ref, acc_ref, stat_ref = refs
    if not closing:
        acc_ref, stat_ref = acc_out, stat_out

    def copy(r, ref):
        for b in range(blocks):
            slot, cols = r * blocks + b, slice(b * BLOCK, (b + 1) * BLOCK)
            value_cols[slot] = ref[1, :, cols]
            for h in range(heads):
                key_rows[slot, h] = ref[0, head_rows(h), cols].T

    staged(place_ref, regions, slabs, copy)
    for b, found in enumerate(live_items(
            lists_ref, counts_ref, place_ref, regions, blocks, int(opening), items, False)):
        found_ref[b] = found
        scaled[b] = q_ref[:, b * BLOCK:(b + 1) * BLOCK] * BF16(SCALE)
    if not opening:
        acc_ref[...] = acc_in[...]
        stat_ref[...] = stat_in[...]

    def entries(b, chosen, masked=False):
        scores = [[dot(key_rows[slot, h], scaled[b, head_rows(h)]) for slot in chosen]
                  for h in range(heads)]
        for h in range(heads):
            rows = head_rows(h)
            tiles = scores[h]
            if masked:
                keep = causal()
                tiles = [jnp.where(keep, tile, NEG) for tile in tiles]
            peak = tiles[0]
            for tile in tiles[1:]:
                peak = jnp.maximum(peak, tile)
            peak = jnp.max(peak, axis=0, keepdims=True)
            if masked:
                newest, total, acc = peak, 0.0, 0.0
            else:
                newest = jnp.maximum(stat_ref[b, 2 * h], peak)
                fade = jnp.exp(stat_ref[b, 2 * h] - newest)
                total = stat_ref[b, 2 * h + 1] * fade
                acc = acc_ref[b, rows] * fade
            for slot, tile in zip(chosen, tiles):
                weights = jnp.exp(tile - newest)
                total = total + jnp.sum(weights, axis=0, keepdims=True)
                acc = acc + dot(value_cols[slot, rows], weights.astype(BF16))
            acc_ref[b, rows] = acc
            stat_ref[b, 2 * h] = newest
            stat_ref[b, 2 * h + 1] = total

    def one_block(b, carry):
        found = found_ref[b]
        if opening:
            entries(b, [b], True)

        def slot_at(i):
            return items[b * LIST + i] - b * slots

        @pl.loop(0, lax.div(found, 2))
        def _(i):
            entries(b, [slot_at(2 * i), slot_at(2 * i + 1)])

        @pl.when(lax.rem(found, 2) == 1)
        def _():
            entries(b, [slot_at(found - 1)])

        return carry

    lax.fori_loop(0, blocks, one_block, 0)
    if closing:
        for b in range(blocks):
            cols = slice(b * BLOCK, (b + 1) * BLOCK)
            for h in range(heads):
                top, total = stat_ref[b, 2 * h], stat_ref[b, 2 * h + 1]
                att_ref[head_rows(h), cols] = (acc_ref[b, head_rows(h)] / total).astype(BF16)
                lse_ref[b, h] = top + jnp.log(total)


def forward(tables, queries, regions, slabs, state=None, closing=False, pairs=16):
    width, tokens = queries.shape
    heads, blocks = width // HEAD_DIM, tokens // BLOCK
    slots = len(regions) * blocks
    acc, stat = (blocks, width, BLOCK), (blocks, 2 * heads, 1, BLOCK)
    result = (jax.ShapeDtypeStruct((width, tokens), BF16),
              jax.ShapeDtypeStruct((blocks, heads, 1, BLOCK), F32))
    state = () if state is None else state
    return pl.pallas_call(
        functools.partial(forward_kernel, regions, not state, closing),
        out_shape=result if closing else tuple(
            jax.ShapeDtypeStruct(shape, F32) for shape in (acc, stat)),
        in_specs=smem(3) + vmem(1 + len(slabs) + len(state)),
        out_specs=tuple(vmem(2)),
        scratch_shapes=[
            pltpu.VMEM((slots, heads, BLOCK, HEAD_DIM), BF16),
            pltpu.VMEM((slots, width, BLOCK), BF16),
            pltpu.VMEM((blocks, width, BLOCK), BF16),
            pltpu.SMEM((blocks * LIST,), jnp.int32),
            pltpu.SMEM((blocks,), jnp.int32),
            pltpu.VMEM(acc if closing else (8, BLOCK), F32),
            pltpu.VMEM(stat if closing else (8, BLOCK), F32),
        ],
        compiler_params=pltpu.CompilerParams(vmem_limit_bytes=48 << 20),
        cost_estimate=pl.CostEstimate(
            flops=pairs * 10 ** 9, bytes_accessed=6 << 20, transcendentals=pairs * 10 ** 5),
    )(*tables, queries, *slabs, *state)


def flow_kernel(place_ref, a0, a1, a2, a3, w0, w1, w2, w3, stream_ref, gain_ref, head_ref,
                patch_ref, grad_ref, latent_ref, g0, g1, g2, g3, wide, weights):
    width = a0.shape[0]
    channels = patch_ref.shape[0]
    cols = pl.ds(pl.multiple_of(place_ref[1] * BLOCK, BLOCK), BLOCK)
    for k, (part, weight) in enumerate(zip((a0, a1, a2, a3), (w0, w1, w2, w3))):
        wide[k * width:(k + 1) * width] = part[...]
        weights[k * width:(k + 1) * width] = weight[...]
    hidden = stream_ref[cols].astype(F32) + dot(wide[...], weights[...], 0, 0)
    inverse = lax.rsqrt(jnp.mean(hidden * hidden, axis=-1, keepdims=True) + EPS)
    gain = gain_ref[...]
    normed = (hidden * inverse * gain).astype(BF16)
    params = dot(head_ref[...], normed, 1, 1)
    factor = jnp.exp(-params[channels:])
    latent = (patch_ref[:, cols] - params[:channels]) * factor
    latent_ref[...] = latent
    grad = grad_ref[...]
    grad_params = jnp.concatenate([-grad * factor, -grad * latent - 1.0], axis=0).astype(BF16)
    gained = dot(grad_params, head_ref[...], 0, 0) * gain
    grad_hidden = (
        inverse * gained
        - hidden * inverse ** 3 * jnp.mean(hidden * gained, axis=-1, keepdims=True)
    ).astype(BF16)
    wide[...] = dot(weights[...], grad_hidden, 1, 1).astype(BF16)
    for k, ref in enumerate((g0, g1, g2, g3)):
        ref[...] = wide[k * width:(k + 1) * width]


def flow(place, parts, weights, stream, gain, head_proj, patches, grad):
    width = parts[0].shape[0]
    return pl.pallas_call(
        flow_kernel,
        out_shape=(jax.ShapeDtypeStruct(grad.shape, F32),)
        + (jax.ShapeDtypeStruct((width, BLOCK), BF16),) * 4,
        in_specs=smem(1) + vmem(13),
        out_specs=tuple(vmem(5)),
        scratch_shapes=[
            pltpu.VMEM((4 * width, BLOCK), BF16), pltpu.VMEM((4 * width, stream.shape[1]), BF16)],
        compiler_params=pltpu.CompilerParams(vmem_limit_bytes=48 << 20),
    )(place, *parts, *weights, stream, gain, head_proj, patches, grad)


def backward_kernel(regions, diagonal, last, lists_ref, counts_ref, place_ref, q_ref, att_ref,
                    lse_ref, g0, g1, g2, g3, *refs):
    heads = q_ref.shape[0] // HEAD_DIM
    blocks = q_ref.shape[1] // BLOCK
    slots = len(regions) * blocks
    refs = list(refs)
    slabs = [refs.pop(0) for _ in range(region_inputs(regions))]
    dq_in = None if len(refs) < 12 + len(regions) else refs.pop(0)
    dq_ref = refs.pop(0)
    outs = [refs.pop(0) for _ in regions]
    (key_rows, value_rows, key_cols, grad_cols, scaled, sums, grad_keys, grad_values, items,
     acc_ref) = refs
    me = place_ref[1]
    for k, ref in enumerate((g0, g1, g2, g3)):
        grad_cols[jnp.bitwise_xor(me, k)] = ref[...]

    def copy(r, ref):
        for b in range(blocks):
            slot, cols = r * blocks + b, slice(b * BLOCK, (b + 1) * BLOCK)
            key_cols[slot] = ref[0, :, cols]
            for h in range(heads):
                key_rows[slot, h] = ref[0, head_rows(h), cols].T
                value_rows[slot, h] = ref[1, head_rows(h), cols].T

    staged(place_ref, regions, slabs, copy)
    grad_keys[...] = jnp.zeros_like(grad_keys)
    grad_values[...] = jnp.zeros_like(grad_values)
    found = live_items(
        lists_ref, counts_ref, place_ref, regions, blocks, int(diagonal), items, True)
    for b in range(blocks):
        cols = slice(b * BLOCK, (b + 1) * BLOCK)
        scaled[b] = q_ref[:, cols] * BF16(SCALE)
        for h in range(heads):
            rows = head_rows(h)
            sums[b, h] = jnp.sum(
                grad_cols[b, rows].astype(F32) * att_ref[rows, cols].astype(F32),
                axis=0, keepdims=True)
    acc_ref[...] = jnp.zeros_like(acc_ref) if dq_in is None else dq_in[...]

    def entries(chosen, masked=False):
        tiles = [(b, slot, h, head_rows(h)) for b, slot in chosen for h in range(heads)]
        scores = [dot(key_rows[slot, h], scaled[b, rows]) for b, slot, h, rows in tiles]
        if masked:
            keep = causal()
            scores = [jnp.where(keep, tile, NEG) for tile in scores]
        grads = [dot(value_rows[slot, h], grad_cols[b, rows]) for b, slot, h, rows in tiles]
        probs = [jnp.exp(tile - lse_ref[b, h]) for tile, (b, _, h, _) in zip(scores, tiles)]
        grads = [(p * (g - sums[b, h])).astype(BF16)
                 for p, g, (b, _, h, _) in zip(probs, grads, tiles)]
        probs = [p.astype(BF16) for p in probs]
        for p, g, (b, slot, h, rows) in zip(probs, grads, tiles):
            acc_ref[b, rows] += dot(key_cols[slot, rows], g)
            grad_keys[slot, rows] += dot(scaled[b, rows], g, 1, 1)
            grad_values[slot, rows] += dot(grad_cols[b, rows], p, 1, 1)

    def item_at(i):
        return lax.div(items[i], slots), lax.rem(items[i], slots)

    if diagonal:

        @pl.loop(0, blocks // 2)
        def _(i):
            entries([(2 * i, 2 * i), (2 * i + 1, 2 * i + 1)], True)

    @pl.loop(0, lax.div(found, 2))
    def _(i):
        entries([item_at(2 * i), item_at(2 * i + 1)])

    @pl.when(lax.rem(found, 2) == 1)
    def _():
        entries([item_at(found - 1)])

    if last:
        for b in range(blocks):
            dq_ref[:, b * BLOCK:(b + 1) * BLOCK] = (acc_ref[b] * SCALE).astype(BF16)
    else:
        dq_ref[...] = acc_ref[...]
    for r, ref in enumerate(outs):
        for b in range(blocks):
            cols = slice(b * BLOCK, (b + 1) * BLOCK)
            ref[0, :, cols] = grad_keys[r * blocks + b].astype(ref.dtype)
            ref[1, :, cols] = grad_values[r * blocks + b].astype(ref.dtype)


def backward(tables, queries, attended, lse, grads, regions, slabs, dq=None, last=False, pairs=1):
    width, tokens = queries.shape
    heads, blocks = width // HEAD_DIM, tokens // BLOCK
    slots = len(regions) * blocks
    diagonal = regions[0][0] == 0
    given = () if dq is None else (dq,)
    return pl.pallas_call(
        functools.partial(backward_kernel, regions, diagonal, last),
        out_shape=(jax.ShapeDtypeStruct((width, tokens), BF16) if last else
                   jax.ShapeDtypeStruct((blocks, width, BLOCK), F32),)
        + (jax.ShapeDtypeStruct((2, width, tokens), F32 if diagonal else BF16),) * len(regions),
        in_specs=smem(3) + vmem(7 + len(slabs) + len(given)),
        out_specs=tuple(vmem(1 + len(regions))),
        scratch_shapes=[
            pltpu.VMEM((slots, heads, BLOCK, HEAD_DIM), BF16),
            pltpu.VMEM((slots, heads, BLOCK, HEAD_DIM), BF16),
            pltpu.VMEM((slots, width, BLOCK), BF16),
            pltpu.VMEM((blocks, width, BLOCK), BF16),
            pltpu.VMEM((blocks, width, BLOCK), BF16),
            pltpu.VMEM((blocks, heads, 1, BLOCK), F32),
            pltpu.VMEM((slots, width, BLOCK), F32),
            pltpu.VMEM((slots, width, BLOCK), F32),
            pltpu.SMEM((blocks * LIST,), jnp.int32),
            pltpu.VMEM((blocks, width, BLOCK), F32),
        ],
        compiler_params=pltpu.CompilerParams(vmem_limit_bytes=48 << 20),
        cost_estimate=pl.CostEstimate(
            flops=pairs * 10 ** 9, bytes_accessed=8 << 20, transcendentals=pairs * 10 ** 5),
    )(*tables, queries, attended, lse, *grads, *slabs, *given)


def on_device(queries, key_rows, values, block_lists, counts, out_proj, stream, norm_gain,
              head_proj, patches, token_order, cotangent):
    width, tokens = queries.shape
    cols = lax.axis_size("col")
    row, col = lax.axis_index("row"), lax.axis_index("col")
    odd = row % 2 == 1
    place = jnp.stack([row, col]).astype(jnp.int32)

    tables = (block_lists, counts, place)
    own = jnp.stack([key_rows, values])
    slab2 = hop(own, 2)
    state = forward(tables, queries, [(0, 0, "both")], [own], pairs=1)
    *state, slab2, out_proj = lax.optimization_barrier([*state, slab2, out_proj])
    up1 = upward(own)
    slab4 = hop(slab2, 2)
    up2 = upward(slab2)
    down1 = downward(slab2)

    order = token_order.reshape(1, tokens)
    grad_latent = mirror(permuted(scatter_kernel, place, order, cotangent.T))
    weights = [out_proj] + [across(out_proj, k) for k in range(1, cols)]

    state = forward(tables, queries, [(2, 2, "both")], [slab2], tuple(state), pairs=1)
    *state, slab4 = lax.optimization_barrier([*state, slab4])
    down2 = downward(slab4)
    state = forward(tables, queries, [(1, 1, "each")], [down1, up1], tuple(state), pairs=1)
    state = forward(tables, queries, [(4, 4, "both"), (-1, 3, "one")], [slab4, up2], state,
                    pairs=1)
    attended, lse = forward(tables, queries, [(3, -1, "one")], [down2], state, True, pairs=1)

    def block_of(array, b):
        return lax.dynamic_slice_in_dim(array, b * BLOCK, BLOCK, 1)

    parts = [block_of(attended, col)] + [
        across(block_of(attended, jnp.bitwise_xor(col, k)), k) for k in range(1, cols)]
    latent, *grads = flow(
        place, parts, weights, stream, norm_gain.reshape(1, -1), head_proj, patches.T,
        grad_latent)
    *grads, mirrored = lax.optimization_barrier(
        [grads[0]] + [across(grads[k], k) for k in range(1, cols)] + [mirror(latent)])

    shared = (tables, queries, attended, lse, grads)
    grad_queries, part3, part4 = backward(
        *shared, [(3, 3, "each"), (4, 4, "both")], [down2, up2, slab4], pairs=1)
    from3 = mate(part3)
    reordered = permuted(gather_kernel, place, order, mirrored)
    grad_queries, reordered = lax.optimization_barrier((grad_queries, reordered))
    pieces = [reordered] + [across(reordered, k) for k in range(1, cols)]
    grad_queries, part1 = backward(
        *shared, [(1, 1, "each")], [down1, up1], grad_queries, pairs=1)
    from1 = mate(part1)
    zero = jnp.zeros_like(part1)
    far = part4 + jnp.where(odd, from3, zero)
    grad_queries, far, *pieces = lax.optimization_barrier([grad_queries, far] + pieces)
    far = hop(far, -2)
    latent_out = assembled(place, pieces, tokens).T
    grad_queries, part2 = backward(*shared, [(2, 2, "both")], [slab2], grad_queries, pairs=1)
    near = part2 + jnp.where(odd, from1, from3) + far
    grad_queries, near = lax.optimization_barrier((grad_queries, near))
    near = hop(near, -2)
    grad_queries, own_grad = backward(
        *shared, [(0, 0, "both")], [own], grad_queries, True, pairs=1)
    own_grad = own_grad + jnp.where(odd, zero, from1).astype(F32) + near.astype(F32)
    own_grad = own_grad.astype(BF16)
    return (latent_out, grad_queries, own_grad[0], own_grad[1])


def solution(mesh):
    return jax.shard_map(
        on_device,
        mesh=mesh,
        in_specs=(
            P("col", "row"),
            P("col", "row"),
            P("col", "row"),
            P("row", None),
            P("row"),
            P("col", None),
            P("row", None),
            P(),
            P(),
            P("row", None),
            P("row"),
            P("row", None),
        ),
        out_specs=(P("row", None), P("col", "row"), P("col", "row"), P("col", "row")),
        check_vma=False,
    )
```

```python
import functools

import jax
import jax.numpy as jnp
from jax import lax
from jax.experimental import pallas as pl
from jax.experimental.pallas import tpu as pltpu
from jax.sharding import PartitionSpec as P

HEAD_DIM = 64
BLOCK = 256
LIST = 16
REACH = 4

NEG = -1e30
EPS = 1e-05
SCALE = HEAD_DIM ** (-0.5)
F32 = jnp.float32
BF16 = jnp.bfloat16


def dot(a, b, ca=1, cb=0):
    return lax.dot_general(a, b, (((ca,), (cb,)), ((), ())), preferred_element_type=F32)


def vmem(count):
    return [pl.BlockSpec(memory_space=pltpu.VMEM)] * count


def smem(count):
    return [pl.BlockSpec(memory_space=pltpu.SMEM)] * count


def hop(array, by):
    size = lax.axis_size("row")
    pairs = [(i, i + by) for i in range(size) if 0 <= i + by < size]
    return lax.ppermute(array, "row", pairs)


def mate(array):
    return lax.ppermute(array, "row", [(i, i ^ 1) for i in range(lax.axis_size("row"))])


def upward(array):
    return lax.ppermute(array, "row", [(i, i + 1) for i in range(0, lax.axis_size("row"), 2)])


def downward(array):
    return lax.ppermute(array, "row", [(i + 1, i) for i in range(0, lax.axis_size("row"), 2)])


def mirror(array):
    size = lax.axis_size("row")
    return lax.ppermute(array, "row", [(i, size - 1 - i) for i in range(size)])


def across(array, bits):
    return lax.ppermute(array, "col", [(i, i ^ bits) for i in range(lax.axis_size("col"))])


def split3(x):
    hi = x.astype(BF16)
    rest = x - hi.astype(F32)
    mid = rest.astype(BF16)
    low = (rest - mid.astype(F32)).astype(BF16)
    return hi, mid, low


def picked(place_ref, order_ref, blocks):
    cols = pl.ds(pl.multiple_of((blocks - 1 - place_ref[1]) * BLOCK, BLOCK), BLOCK)
    rows = lax.broadcasted_iota(jnp.int32, (BLOCK, BLOCK), 0)
    return (rows == lax.rem(order_ref[:, cols], BLOCK)).astype(BF16), cols


def scatter_kernel(place_ref, order_ref, x_ref, o_ref):
    pick, cols = picked(place_ref, order_ref, x_ref.shape[1] // BLOCK)
    hi, mid, low = split3(x_ref[:, cols])
    o_ref[...] = (dot(hi, pick, 1, 1) + dot(mid, pick, 1, 1)) + dot(low, pick, 1, 1)


def gather_kernel(place_ref, order_ref, x_ref, o_ref):
    pick, _ = picked(place_ref, order_ref, order_ref.shape[1] // BLOCK)
    hi, mid, low = split3(x_ref[...])
    o_ref[...] = (dot(hi, pick) + dot(mid, pick)) + dot(low, pick)


def permuted(kernel, place, order, x):
    return pl.pallas_call(
        kernel,
        out_shape=jax.ShapeDtypeStruct((x.shape[0], BLOCK), F32),
        in_specs=smem(1) + vmem(2),
        out_specs=vmem(1)[0],
    )(place, order, x)


def assemble_kernel(place_ref, p0, p1, p2, p3, o_ref):
    blocks = o_ref.shape[1] // BLOCK
    for k, ref in enumerate((p0, p1, p2, p3)):
        at = (blocks - 1 - jnp.bitwise_xor(place_ref[1], k)) * BLOCK
        o_ref[:, pl.ds(pl.multiple_of(at, BLOCK), BLOCK)] = ref[...]


def assembled(place, pieces, tokens):
    return pl.pallas_call(
        assemble_kernel,
        out_shape=jax.ShapeDtypeStruct((pieces[0].shape[0], tokens), F32),
        in_specs=smem(1) + vmem(4),
        out_specs=vmem(1)[0],
    )(place, *pieces)


def live_items(lists_ref, counts_ref, place_ref, regions, blocks, first, items_ref, together):
    row = place_ref[0]
    odd = lax.rem(row, 2)
    slots = len(regions) * blocks
    wanted = [jnp.where(odd == 1, region[1], region[0]) for region in regions]
    found = []
    total = 0
    for b in range(blocks):

        def look(j, count, b=b):
            block = lists_ref[b, j]
            distance = row - lax.div(block, blocks)
            slot, hit = b * slots, 0
            for r, want in enumerate(wanted):
                here = (distance == want).astype(jnp.int32)
                slot = slot + here * r * blocks
                hit = hit + here
            items_ref[count] = slot + lax.rem(block, blocks)
            return count + hit

        start = total if together else b * LIST
        total = lax.fori_loop(first, counts_ref[b], look, start)
        found.append(total - start)
    return total if together else found


def staged(place_ref, regions, refs, copy):
    odd = lax.rem(place_ref[0], 2)
    at = 0
    for r, region in enumerate(regions):
        if region[2] == "both":
            copy(r, refs[at])
            at += 1
            continue
        for parity in (0, 1):
            if region[parity] >= 0:
                pl.when(odd == parity)(lambda r=r, ref=refs[at]: copy(r, ref))
                at += 1


def region_inputs(regions):
    return sum(1 if region[2] == "both" else (region[0] >= 0) + (region[1] >= 0)
               for region in regions)


def causal():
    return (lax.broadcasted_iota(jnp.int32, (BLOCK, BLOCK), 0)
            <= lax.broadcasted_iota(jnp.int32, (BLOCK, BLOCK), 1))


def head_rows(h):
    return slice(h * HEAD_DIM, (h + 1) * HEAD_DIM)


def forward_kernel(regions, opening, closing, lists_ref, counts_ref, place_ref, q_ref, *refs):
    heads = q_ref.shape[0] // HEAD_DIM
    blocks = q_ref.shape[1] // BLOCK
    slots = len(regions) * blocks
    refs = list(refs)
    slabs = [refs.pop(0) for _ in range(region_inputs(regions))]
    if not opening:
        acc_in, stat_in = refs.pop(0), refs.pop(0)
    if closing:
        att_ref, lse_ref = refs.pop(0), refs.pop(0)
    else:
        acc_out, stat_out = refs.pop(0), refs.pop(0)
    key_rows, value_cols, scaled, items, found_ref, acc_ref, stat_ref = refs
    if not closing:
        acc_ref, stat_ref = acc_out, stat_out

    def copy(r, ref):
        for b in range(blocks):
            slot, cols = r * blocks + b, slice(b * BLOCK, (b + 1) * BLOCK)
            value_cols[slot] = ref[1, :, cols]
            for h in range(heads):
                key_rows[slot, h] = ref[0, head_rows(h), cols].T

    staged(place_ref, regions, slabs, copy)
    for b, found in enumerate(live_items(
            lists_ref, counts_ref, place_ref, regions, blocks, int(opening), items, False)):
        found_ref[b] = found
        scaled[b] = q_ref[:, b * BLOCK:(b + 1) * BLOCK] * BF16(SCALE)
    if not opening:
        acc_ref[...] = acc_in[...]
        stat_ref[...] = stat_in[...]

    def entries(b, chosen, masked=False):
        scores = [[dot(key_rows[slot, h], scaled[b, head_rows(h)]) for slot in chosen]
                  for h in range(heads)]
        for h in range(heads):
            rows = head_rows(h)
            tiles = scores[h]
            if masked:
                keep = causal()
                tiles = [jnp.where(keep, tile, NEG) for tile in tiles]
            peak = tiles[0]
            for tile in tiles[1:]:
                peak = jnp.maximum(peak, tile)
            peak = jnp.max(peak, axis=0, keepdims=True)
            if masked:
                newest, total, acc = peak, 0.0, 0.0
            else:
                newest = jnp.maximum(stat_ref[b, 2 * h], peak)
                fade = jnp.exp(stat_ref[b, 2 * h] - newest)
                total = stat_ref[b, 2 * h + 1] * fade
                acc = acc_ref[b, rows] * fade
            for slot, tile in zip(chosen, tiles):
                weights = jnp.exp(tile - newest)
                total = total + jnp.sum(weights, axis=0, keepdims=True)
                acc = acc + dot(value_cols[slot, rows], weights.astype(BF16))
            acc_ref[b, rows] = acc
            stat_ref[b, 2 * h] = newest
            stat_ref[b, 2 * h + 1] = total

    def one_block(b, carry):
        found = found_ref[b]
        if opening:
            entries(b, [b], True)

        def slot_at(i):
            return items[b * LIST + i] - b * slots

        @pl.loop(0, lax.div(found, 2))
        def _(i):
            entries(b, [slot_at(2 * i), slot_at(2 * i + 1)])

        @pl.when(lax.rem(found, 2) == 1)
        def _():
            entries(b, [slot_at(found - 1)])

        return carry

    lax.fori_loop(0, blocks, one_block, 0)
    if closing:
        for b in range(blocks):
            cols = slice(b * BLOCK, (b + 1) * BLOCK)
            for h in range(heads):
                top, total = stat_ref[b, 2 * h], stat_ref[b, 2 * h + 1]
                att_ref[head_rows(h), cols] = (acc_ref[b, head_rows(h)] / total).astype(BF16)
                lse_ref[b, h] = top + jnp.log(total)


def forward(tables, queries, regions, slabs, state=None, closing=False, pairs=1):
    width, tokens = queries.shape
    heads, blocks = width // HEAD_DIM, tokens // BLOCK
    slots = len(regions) * blocks
    acc, stat = (blocks, width, BLOCK), (blocks, 2 * heads, 1, BLOCK)
    result = (jax.ShapeDtypeStruct((width, tokens), BF16),
              jax.ShapeDtypeStruct((blocks, heads, 1, BLOCK), F32))
    state = () if state is None else state
    return pl.pallas_call(
        functools.partial(forward_kernel, regions, not state, closing),
        out_shape=result if closing else tuple(
            jax.ShapeDtypeStruct(shape, F32) for shape in (acc, stat)),
        in_specs=smem(3) + vmem(1 + len(slabs) + len(state)),
        out_specs=tuple(vmem(2)),
        scratch_shapes=[
            pltpu.VMEM((slots, heads, BLOCK, HEAD_DIM), BF16),
            pltpu.VMEM((slots, width, BLOCK), BF16),
            pltpu.VMEM((blocks, width, BLOCK), BF16),
            pltpu.SMEM((blocks * LIST,), jnp.int32),
            pltpu.SMEM((blocks,), jnp.int32),
            pltpu.VMEM(acc if closing else (8, BLOCK), F32),
            pltpu.VMEM(stat if closing else (8, BLOCK), F32),
        ],
        compiler_params=pltpu.CompilerParams(vmem_limit_bytes=48 << 20),
        cost_estimate=pl.CostEstimate(
            flops=pairs * 10 ** 9, bytes_accessed=6 << 20, transcendentals=pairs * 10 ** 5),
    )(*tables, queries, *slabs, *state)


def flow_kernel(place_ref, a0, a1, a2, a3, w0, w1, w2, w3, stream_ref, gain_ref, head_ref,
                patch_ref, grad_ref, latent_ref, g0, g1, g2, g3, wide, weights):
    width = a0.shape[0]
    channels = patch_ref.shape[0]
    cols = pl.ds(pl.multiple_of(place_ref[1] * BLOCK, BLOCK), BLOCK)
    for k, (part, weight) in enumerate(zip((a0, a1, a2, a3), (w0, w1, w2, w3))):
        wide[k * width:(k + 1) * width] = part[...]
        weights[k * width:(k + 1) * width] = weight[...]
    hidden = stream_ref[cols].astype(F32) + dot(wide[...], weights[...], 0, 0)
    inverse = lax.rsqrt(jnp.mean(hidden * hidden, axis=-1, keepdims=True) + EPS)
    gain = gain_ref[...]
    normed = (hidden * inverse * gain).astype(BF16)
    params = dot(head_ref[...], normed, 1, 1)
    factor = jnp.exp(-params[channels:])
    latent = (patch_ref[:, cols] - params[:channels]) * factor
    latent_ref[...] = latent
    grad = grad_ref[...]
    grad_params = jnp.concatenate([-grad * factor, -grad * latent - 1.0], axis=0).astype(BF16)
    gained = dot(grad_params, head_ref[...], 0, 0) * gain
    grad_hidden = (
        inverse * gained
        - hidden * inverse ** 3 * jnp.mean(hidden * gained, axis=-1, keepdims=True)
    ).astype(BF16)
    wide[...] = dot(weights[...], grad_hidden, 1, 1).astype(BF16)
    for k, ref in enumerate((g0, g1, g2, g3)):
        ref[...] = wide[k * width:(k + 1) * width]


def flow(place, parts, weights, stream, gain, head_proj, patches, grad):
    width = parts[0].shape[0]
    return pl.pallas_call(
        flow_kernel,
        out_shape=(jax.ShapeDtypeStruct(grad.shape, F32),)
        + (jax.ShapeDtypeStruct((width, BLOCK), BF16),) * 4,
        in_specs=smem(1) + vmem(13),
        out_specs=tuple(vmem(5)),
        scratch_shapes=[
            pltpu.VMEM((4 * width, BLOCK), BF16), pltpu.VMEM((4 * width, stream.shape[1]), BF16)],
        compiler_params=pltpu.CompilerParams(vmem_limit_bytes=48 << 20),
    )(place, *parts, *weights, stream, gain, head_proj, patches, grad)


def backward_kernel(regions, diagonal, last, lists_ref, counts_ref, place_ref, q_ref, att_ref,
                    lse_ref, g0, g1, g2, g3, *refs):
    heads = q_ref.shape[0] // HEAD_DIM
    blocks = q_ref.shape[1] // BLOCK
    slots = len(regions) * blocks
    refs = list(refs)
    slabs = [refs.pop(0) for _ in range(region_inputs(regions))]
    dq_in = None if len(refs) < 12 + len(regions) else refs.pop(0)
    dq_ref = refs.pop(0)
    outs = [refs.pop(0) for _ in regions]
    (key_rows, value_rows, key_cols, grad_cols, scaled, sums, grad_keys, grad_values, items,
     acc_ref) = refs
    me = place_ref[1]
    for k, ref in enumerate((g0, g1, g2, g3)):
        grad_cols[jnp.bitwise_xor(me, k)] = ref[...]

    def copy(r, ref):
        for b in range(blocks):
            slot, cols = r * blocks + b, slice(b * BLOCK, (b + 1) * BLOCK)
            key_cols[slot] = ref[0, :, cols]
            for h in range(heads):
                key_rows[slot, h] = ref[0, head_rows(h), cols].T
                value_rows[slot, h] = ref[1, head_rows(h), cols].T

    staged(place_ref, regions, slabs, copy)
    grad_keys[...] = jnp.zeros_like(grad_keys)
    grad_values[...] = jnp.zeros_like(grad_values)
    found = live_items(
        lists_ref, counts_ref, place_ref, regions, blocks, int(diagonal), items, True)
    for b in range(blocks):
        cols = slice(b * BLOCK, (b + 1) * BLOCK)
        scaled[b] = q_ref[:, cols] * BF16(SCALE)
        for h in range(heads):
            rows = head_rows(h)
            sums[b, h] = jnp.sum(
                grad_cols[b, rows].astype(F32) * att_ref[rows, cols].astype(F32),
                axis=0, keepdims=True)
    acc_ref[...] = jnp.zeros_like(acc_ref) if dq_in is None else dq_in[...]

    def entries(chosen, masked=False):
        tiles = [(b, slot, h, head_rows(h)) for b, slot in chosen for h in range(heads)]
        scores = [dot(key_rows[slot, h], scaled[b, rows]) for b, slot, h, rows in tiles]
        if masked:
            keep = causal()
            scores = [jnp.where(keep, tile, NEG) for tile in scores]
        grads = [dot(value_rows[slot, h], grad_cols[b, rows]) for b, slot, h, rows in tiles]
        probs = [jnp.exp(tile - lse_ref[b, h]) for tile, (b, _, h, _) in zip(scores, tiles)]
        grads = [(p * (g - sums[b, h])).astype(BF16)
                 for p, g, (b, _, h, _) in zip(probs, grads, tiles)]
        probs = [p.astype(BF16) for p in probs]
        for p, g, (b, slot, h, rows) in zip(probs, grads, tiles):
            acc_ref[b, rows] += dot(key_cols[slot, rows], g)
            grad_keys[slot, rows] += dot(scaled[b, rows], g, 1, 1)
            grad_values[slot, rows] += dot(grad_cols[b, rows], p, 1, 1)

    def item_at(i):
        return lax.div(items[i], slots), lax.rem(items[i], slots)

    if diagonal:

        @pl.loop(0, blocks // 2)
        def _(i):
            entries([(2 * i, 2 * i), (2 * i + 1, 2 * i + 1)], True)

    @pl.loop(0, lax.div(found, 2))
    def _(i):
        entries([item_at(2 * i), item_at(2 * i + 1)])

    @pl.when(lax.rem(found, 2) == 1)
    def _():
        entries([item_at(found - 1)])

    if last:
        for b in range(blocks):
            dq_ref[:, b * BLOCK:(b + 1) * BLOCK] = (acc_ref[b] * SCALE).astype(BF16)
    else:
        dq_ref[...] = acc_ref[...]
    for r, ref in enumerate(outs):
        for b in range(blocks):
            cols = slice(b * BLOCK, (b + 1) * BLOCK)
            ref[0, :, cols] = grad_keys[r * blocks + b].astype(ref.dtype)
            ref[1, :, cols] = grad_values[r * blocks + b].astype(ref.dtype)


def backward(tables, queries, attended, lse, grads, regions, slabs, dq=None, last=False, pairs=1):
    width, tokens = queries.shape
    heads, blocks = width // HEAD_DIM, tokens // BLOCK
    slots = len(regions) * blocks
    diagonal = regions[0][0] == 0
    given = () if dq is None else (dq,)
    return pl.pallas_call(
        functools.partial(backward_kernel, regions, diagonal, last),
        out_shape=(jax.ShapeDtypeStruct((width, tokens), BF16) if last else
                   jax.ShapeDtypeStruct((blocks, width, BLOCK), F32),)
        + (jax.ShapeDtypeStruct((2, width, tokens), F32 if diagonal else BF16),) * len(regions),
        in_specs=smem(3) + vmem(7 + len(slabs) + len(given)),
        out_specs=tuple(vmem(1 + len(regions))),
        scratch_shapes=[
            pltpu.VMEM((slots, heads, BLOCK, HEAD_DIM), BF16),
            pltpu.VMEM((slots, heads, BLOCK, HEAD_DIM), BF16),
            pltpu.VMEM((slots, width, BLOCK), BF16),
            pltpu.VMEM((blocks, width, BLOCK), BF16),
            pltpu.VMEM((blocks, width, BLOCK), BF16),
            pltpu.VMEM((blocks, heads, 1, BLOCK), F32),
            pltpu.VMEM((slots, width, BLOCK), F32),
            pltpu.VMEM((slots, width, BLOCK), F32),
            pltpu.SMEM((blocks * LIST,), jnp.int32),
            pltpu.VMEM((blocks, width, BLOCK), F32),
        ],
        compiler_params=pltpu.CompilerParams(vmem_limit_bytes=48 << 20),
        cost_estimate=pl.CostEstimate(
            flops=pairs * 10 ** 9, bytes_accessed=8 << 20, transcendentals=pairs * 10 ** 5),
    )(*tables, queries, attended, lse, *grads, *slabs, *given)


def on_device(queries, key_rows, values, block_lists, counts, out_proj, stream, norm_gain,
              head_proj, patches, token_order, cotangent):
    width, tokens = queries.shape
    cols = lax.axis_size("col")
    row, col = lax.axis_index("row"), lax.axis_index("col")
    odd = row % 2 == 1
    place = jnp.stack([row, col]).astype(jnp.int32)

    tables = (block_lists, counts, place)
    tie = lax.optimization_barrier
    own = jnp.stack([key_rows, values])
    slab2 = hop(own, 2)
    state = forward(tables, queries, [(0, 0, "both")], [own])
    *state, out_proj, cotangent, own_again = tie([*state, out_proj, cotangent, own])
    order = token_order.reshape(1, tokens)
    grad_latent = mirror(permuted(scatter_kernel, place, order, cotangent.T))
    weights = [across(out_proj, k) for k in range(1, cols)]
    up1 = upward(own_again)
    *state, slab2, grad_latent, out_proj, w1, w2, w3 = tie(
        [*state, slab2, grad_latent, out_proj, *weights])
    weights = [out_proj, w1, w2, w3]
    slab4 = hop(slab2, 2)
    down1 = downward(slab2)
    up2 = upward(slab2)
    state = forward(tables, queries, [(2, 2, "both")], [slab2], tuple(state))
    *state, slab4 = tie([*state, slab4])
    down2 = downward(slab4)
    state = forward(tables, queries, [(1, 1, "each")], [down1, up1], tuple(state))
    state = forward(tables, queries, [(4, 4, "both"), (-1, 3, "one")], [slab4, up2], state)
    attended, lse = forward(tables, queries, [(3, -1, "one")], [down2], state, True)

    def block_of(array, b):
        return lax.dynamic_slice_in_dim(array, b * BLOCK, BLOCK, 1)

    parts = [block_of(attended, col)] + [
        across(block_of(attended, jnp.bitwise_xor(col, k)), k) for k in range(1, cols)]
    latent, *grads = flow(
        place, parts, weights, stream, norm_gain.reshape(1, -1), head_proj, patches.T,
        grad_latent)
    grads = [grads[0]] + [across(grads[k], k) for k in range(1, cols)]

    shared = (tables, queries, attended, lse, grads)
    grad_queries, part3 = backward(*shared, [(3, 3, "each")], [down2, up2])
    from3 = mate(part3)
    grad_queries, part4, part1 = backward(
        *shared, [(4, 4, "both"), (1, 1, "each")], [slab4, down1, up1], grad_queries)
    from1 = mate(part1)
    zero = jnp.zeros_like(part1)
    far = part4 + jnp.where(odd, from3, zero)
    grad_queries, far, latent = tie([grad_queries, far, latent])
    far = hop(far, -2)
    mirrored = mirror(latent)
    grad_queries, part2 = backward(*shared, [(2, 2, "both")], [slab2], grad_queries)
    grad_queries, mirrored = tie([grad_queries, mirrored])
    reordered = permuted(gather_kernel, place, order, mirrored)
    near = part2 + jnp.where(odd, from1, from3) + far
    grad_queries, near, reordered = tie([grad_queries, near, reordered])
    near = hop(near, -2)
    pieces = [reordered] + [across(reordered, k) for k in range(1, cols)]
    grad_queries, own_grad = backward(*shared, [(0, 0, "both")], [own], grad_queries, True)
    own_grad, *pieces = tie([own_grad] + pieces)
    latent_out = assembled(place, pieces, tokens).T
    own_grad = own_grad + jnp.where(odd, zero, from1).astype(F32) + near.astype(F32)
    own_grad = own_grad.astype(BF16)
    return (latent_out, grad_queries, own_grad[0], own_grad[1])


def solution(mesh):
    return jax.shard_map(
        on_device,
        mesh=mesh,
        in_specs=(
            P("col", "row"),
            P("col", "row"),
            P("col", "row"),
            P("row", None),
            P("row"),
            P("col", None),
            P("row", None),
            P(),
            P(),
            P("row", None),
            P("row"),
            P("row", None),
        ),
        out_specs=(P("row", None), P("col", "row"), P("col", "row"), P("col", "row")),
        check_vma=False,
    )
```

```python
import functools

import jax
import jax.numpy as jnp
from jax import lax
from jax.experimental import pallas as pl
from jax.experimental.pallas import tpu as pltpu
from jax.sharding import PartitionSpec as P

HEAD_DIM = 64
BLOCK = 256
LIST = 16
REACH = 4

NEG = -1e30
EPS = 1e-05
SCALE = HEAD_DIM ** (-0.5)
F32 = jnp.float32
BF16 = jnp.bfloat16


def dot(a, b, ca=1, cb=0):
    return lax.dot_general(a, b, (((ca,), (cb,)), ((), ())), preferred_element_type=F32)


def vmem(count):
    return [pl.BlockSpec(memory_space=pltpu.VMEM)] * count


def anywhere(count):
    return [pl.BlockSpec(memory_space=pl.ANY)] * count


def smem(count):
    return [pl.BlockSpec(memory_space=pltpu.SMEM)] * count


def hop(array, by):
    size = lax.axis_size("row")
    pairs = [(i, i + by) for i in range(size) if 0 <= i + by < size]
    return lax.ppermute(array, "row", pairs)


def mate(array):
    return lax.ppermute(array, "row", [(i, i ^ 1) for i in range(lax.axis_size("row"))])


def upward(array):
    return lax.ppermute(array, "row", [(i, i + 1) for i in range(0, lax.axis_size("row"), 2)])


def downward(array):
    return lax.ppermute(array, "row", [(i + 1, i) for i in range(0, lax.axis_size("row"), 2)])


def mirror(array):
    size = lax.axis_size("row")
    return lax.ppermute(array, "row", [(i, size - 1 - i) for i in range(size)])


def across(array, bits):
    return lax.ppermute(array, "col", [(i, i ^ bits) for i in range(lax.axis_size("col"))])


def split3(x):
    hi = x.astype(BF16)
    rest = x - hi.astype(F32)
    mid = rest.astype(BF16)
    low = (rest - mid.astype(F32)).astype(BF16)
    return hi, mid, low


def picked(place_ref, order_ref, blocks):
    cols = pl.ds(pl.multiple_of((blocks - 1 - place_ref[1]) * BLOCK, BLOCK), BLOCK)
    rows = lax.broadcasted_iota(jnp.int32, (BLOCK, BLOCK), 0)
    return (rows == lax.rem(order_ref[:, cols], BLOCK)).astype(BF16), cols


def scatter_kernel(place_ref, order_ref, x_ref, o_ref):
    pick, cols = picked(place_ref, order_ref, x_ref.shape[1] // BLOCK)
    hi, mid, low = split3(x_ref[:, cols])
    o_ref[...] = (dot(hi, pick, 1, 1) + dot(mid, pick, 1, 1)) + dot(low, pick, 1, 1)


def gather_kernel(place_ref, order_ref, x_ref, o_ref):
    pick, _ = picked(place_ref, order_ref, order_ref.shape[1] // BLOCK)
    hi, mid, low = split3(x_ref[...])
    o_ref[...] = (dot(hi, pick) + dot(mid, pick)) + dot(low, pick)


def permuted(kernel, place, order, x):
    return pl.pallas_call(
        kernel,
        out_shape=jax.ShapeDtypeStruct((x.shape[0], BLOCK), F32),
        in_specs=smem(1) + vmem(2),
        out_specs=vmem(1)[0],
    )(place, order, x)


def assemble_kernel(place_ref, p0, p1, p2, p3, o_ref):
    blocks = o_ref.shape[1] // BLOCK
    for k, ref in enumerate((p0, p1, p2, p3)):
        at = (blocks - 1 - jnp.bitwise_xor(place_ref[1], k)) * BLOCK
        o_ref[:, pl.ds(pl.multiple_of(at, BLOCK), BLOCK)] = ref[...]


def assembled(place, pieces, tokens):
    return pl.pallas_call(
        assemble_kernel,
        out_shape=jax.ShapeDtypeStruct((pieces[0].shape[0], tokens), F32),
        in_specs=smem(1) + vmem(4),
        out_specs=vmem(1)[0],
    )(place, *pieces)


def live_items(lists_ref, counts_ref, place_ref, regions, blocks, first, items_ref, together):
    row = place_ref[0]
    odd = lax.rem(row, 2)
    slots = len(regions) * blocks
    wanted = [jnp.where(odd == 1, region[1], region[0]) for region in regions]
    found = []
    total = 0
    for b in range(blocks):

        def look(j, count, b=b):
            block = lists_ref[b, j]
            distance = row - lax.div(block, blocks)
            slot, hit = b * slots, 0
            for r, want in enumerate(wanted):
                here = (distance == want).astype(jnp.int32)
                slot = slot + here * r * blocks
                hit = hit + here
            items_ref[count] = slot + lax.rem(block, blocks)
            return count + hit

        start = total if together else b * LIST
        total = lax.fori_loop(first, counts_ref[b], look, start)
        found.append(total - start)
    return total if together else found


def staged(place_ref, regions, refs, raw, sems, act):
    odd = lax.rem(place_ref[0], 2)
    at = 0
    for r, region in enumerate(regions):
        if region[2] == "both":
            act(r, pltpu.make_async_copy(refs[at], raw.at[r], sems.at[r]))
            at += 1
            continue
        for parity in (0, 1):
            if region[parity] >= 0:
                copy = pltpu.make_async_copy(refs[at], raw.at[r], sems.at[r])
                pl.when(odd == parity)(lambda r=r, copy=copy: act(r, copy))
                at += 1


def begin(r, copy):
    copy.start()


def region_inputs(regions):
    return sum(1 if region[2] == "both" else (region[0] >= 0) + (region[1] >= 0)
               for region in regions)


def causal():
    return (lax.broadcasted_iota(jnp.int32, (BLOCK, BLOCK), 0)
            <= lax.broadcasted_iota(jnp.int32, (BLOCK, BLOCK), 1))


def head_rows(h):
    return slice(h * HEAD_DIM, (h + 1) * HEAD_DIM)


def forward_kernel(regions, opening, closing, lists_ref, counts_ref, place_ref, q_ref, *refs):
    heads = q_ref.shape[0] // HEAD_DIM
    blocks = q_ref.shape[1] // BLOCK
    slots = len(regions) * blocks
    refs = list(refs)
    slabs = [refs.pop(0) for _ in range(region_inputs(regions))]
    if not opening:
        acc_in, stat_in = refs.pop(0), refs.pop(0)
    if closing:
        att_ref, lse_ref = refs.pop(0), refs.pop(0)
    else:
        acc_out, stat_out = refs.pop(0), refs.pop(0)
    (key_rows, value_cols, scaled, items, found_ref, acc_ref, stat_ref, raw, q_vmem, sems,
     q_sem) = refs
    if not closing:
        acc_ref, stat_ref = acc_out, stat_out

    q_copy = pltpu.make_async_copy(q_ref, q_vmem, q_sem)
    q_copy.start()
    staged(place_ref, regions, slabs, raw, sems, begin)
    for b, found in enumerate(live_items(
            lists_ref, counts_ref, place_ref, regions, blocks, int(opening), items, False)):
        found_ref[b] = found
    if not opening:
        acc_ref[...] = acc_in[...]
        stat_ref[...] = stat_in[...]
    q_copy.wait()
    for b in range(blocks):
        scaled[b] = q_vmem[:, b * BLOCK:(b + 1) * BLOCK] * BF16(SCALE)

    def spread(r, copy):
        copy.wait()
        for b in range(blocks):
            slot, cols = r * blocks + b, slice(b * BLOCK, (b + 1) * BLOCK)
            value_cols[slot] = raw[r, 1, :, cols]
            for h in range(heads):
                key_rows[slot, h] = raw[r, 0, head_rows(h), cols].T

    staged(place_ref, regions, slabs, raw, sems, spread)

    def entries(b, chosen, masked=False):
        scores = [[dot(key_rows[slot, h], scaled[b, head_rows(h)]) for slot in chosen]
                  for h in range(heads)]
        for h in range(heads):
            rows = head_rows(h)
            tiles = scores[h]
            if masked:
                keep = causal()
                tiles = [jnp.where(keep, tile, NEG) for tile in tiles]
            peak = tiles[0]
            for tile in tiles[1:]:
                peak = jnp.maximum(peak, tile)
            peak = jnp.max(peak, axis=0, keepdims=True)
            if masked:
                newest, total, acc = peak, 0.0, 0.0
            else:
                newest = jnp.maximum(stat_ref[b, 2 * h], peak)
                fade = jnp.exp(stat_ref[b, 2 * h] - newest)
                total = stat_ref[b, 2 * h + 1] * fade
                acc = acc_ref[b, rows] * fade
            for slot, tile in zip(chosen, tiles):
                weights = jnp.exp(tile - newest)
                total = total + jnp.sum(weights, axis=0, keepdims=True)
                acc = acc + dot(value_cols[slot, rows], weights.astype(BF16))
            acc_ref[b, rows] = acc
            stat_ref[b, 2 * h] = newest
            stat_ref[b, 2 * h + 1] = total

    def one_block(b, carry):
        found = found_ref[b]
        if opening:
            entries(b, [b], True)

        def slot_at(i):
            return items[b * LIST + i] - b * slots

        @pl.loop(0, lax.div(found, 2))
        def _(i):
            entries(b, [slot_at(2 * i), slot_at(2 * i + 1)])

        @pl.when(lax.rem(found, 2) == 1)
        def _():
            entries(b, [slot_at(found - 1)])

        return carry

    lax.fori_loop(0, blocks, one_block, 0)
    if closing:
        for b in range(blocks):
            cols = slice(b * BLOCK, (b + 1) * BLOCK)
            for h in range(heads):
                top, total = stat_ref[b, 2 * h], stat_ref[b, 2 * h + 1]
                att_ref[head_rows(h), cols] = (acc_ref[b, head_rows(h)] / total).astype(BF16)
                lse_ref[b, h] = top + jnp.log(total)


def forward(tables, queries, regions, slabs, state=None, closing=False, pairs=1):
    width, tokens = queries.shape
    heads, blocks = width // HEAD_DIM, tokens // BLOCK
    slots = len(regions) * blocks
    acc, stat = (blocks, width, BLOCK), (blocks, 2 * heads, 1, BLOCK)
    result = (jax.ShapeDtypeStruct((width, tokens), BF16),
              jax.ShapeDtypeStruct((blocks, heads, 1, BLOCK), F32))
    state = () if state is None else state
    return pl.pallas_call(
        functools.partial(forward_kernel, regions, not state, closing),
        out_shape=result if closing else tuple(
            jax.ShapeDtypeStruct(shape, F32) for shape in (acc, stat)),
        in_specs=smem(3) + anywhere(1 + len(slabs)) + vmem(len(state)),
        out_specs=tuple(vmem(2)),
        scratch_shapes=[
            pltpu.VMEM((slots, heads, BLOCK, HEAD_DIM), BF16),
            pltpu.VMEM((slots, width, BLOCK), BF16),
            pltpu.VMEM((blocks, width, BLOCK), BF16),
            pltpu.SMEM((blocks * LIST,), jnp.int32),
            pltpu.SMEM((blocks,), jnp.int32),
            pltpu.VMEM(acc if closing else (8, BLOCK), F32),
            pltpu.VMEM(stat if closing else (8, BLOCK), F32),
            pltpu.VMEM((len(regions), 2, width, tokens), BF16),
            pltpu.VMEM((width, tokens), BF16),
            pltpu.SemaphoreType.DMA((len(regions),)),
            pltpu.SemaphoreType.DMA,
        ],
        compiler_params=pltpu.CompilerParams(vmem_limit_bytes=48 << 20),
        cost_estimate=pl.CostEstimate(
            flops=pairs * 10 ** 9, bytes_accessed=6 << 20, transcendentals=pairs * 10 ** 5),
    )(*tables, queries, *slabs, *state)


def flow_kernel(place_ref, a0, a1, a2, a3, w0, w1, w2, w3, stream_ref, gain_ref, head_ref,
                patch_ref, grad_ref, latent_ref, g0, g1, g2, g3, wide, weights):
    width = a0.shape[0]
    channels = patch_ref.shape[0]
    cols = pl.ds(pl.multiple_of(place_ref[1] * BLOCK, BLOCK), BLOCK)
    for k, (part, weight) in enumerate(zip((a0, a1, a2, a3), (w0, w1, w2, w3))):
        wide[k * width:(k + 1) * width] = part[...]
        weights[k * width:(k + 1) * width] = weight[...]
    hidden = stream_ref[cols].astype(F32) + dot(wide[...], weights[...], 0, 0)
    inverse = lax.rsqrt(jnp.mean(hidden * hidden, axis=-1, keepdims=True) + EPS)
    gain = gain_ref[...]
    normed = (hidden * inverse * gain).astype(BF16)
    params = dot(head_ref[...], normed, 1, 1)
    factor = jnp.exp(-params[channels:])
    latent = (patch_ref[:, cols] - params[:channels]) * factor
    latent_ref[...] = latent
    grad = grad_ref[...]
    grad_params = jnp.concatenate([-grad * factor, -grad * latent - 1.0], axis=0).astype(BF16)
    gained = dot(grad_params, head_ref[...], 0, 0) * gain
    grad_hidden = (
        inverse * gained
        - hidden * inverse ** 3 * jnp.mean(hidden * gained, axis=-1, keepdims=True)
    ).astype(BF16)
    wide[...] = dot(weights[...], grad_hidden, 1, 1).astype(BF16)
    for k, ref in enumerate((g0, g1, g2, g3)):
        ref[...] = wide[k * width:(k + 1) * width]


def flow(place, parts, weights, stream, gain, head_proj, patches, grad):
    width = parts[0].shape[0]
    return pl.pallas_call(
        flow_kernel,
        out_shape=(jax.ShapeDtypeStruct(grad.shape, F32),)
        + (jax.ShapeDtypeStruct((width, BLOCK), BF16),) * 4,
        in_specs=smem(1) + vmem(13),
        out_specs=tuple(vmem(5)),
        scratch_shapes=[
            pltpu.VMEM((4 * width, BLOCK), BF16), pltpu.VMEM((4 * width, stream.shape[1]), BF16)],
        compiler_params=pltpu.CompilerParams(vmem_limit_bytes=48 << 20),
    )(place, *parts, *weights, stream, gain, head_proj, patches, grad)


def backward_kernel(regions, diagonal, last, lists_ref, counts_ref, place_ref, q_ref, att_ref,
                    lse_ref, g0, g1, g2, g3, *refs):
    heads = q_ref.shape[0] // HEAD_DIM
    blocks = q_ref.shape[1] // BLOCK
    slots = len(regions) * blocks
    refs = list(refs)
    slabs = [refs.pop(0) for _ in range(region_inputs(regions))]
    dq_in = None if len(refs) < 17 + len(regions) else refs.pop(0)
    dq_ref = refs.pop(0)
    outs = [refs.pop(0) for _ in regions]
    (key_rows, value_rows, key_cols, grad_cols, scaled, sums, grad_keys, grad_values, items,
     acc_ref, raw, q_vmem, att_vmem, sems, more_sems) = refs
    q_copy = pltpu.make_async_copy(q_ref, q_vmem, more_sems.at[0])
    att_copy = pltpu.make_async_copy(att_ref, att_vmem, more_sems.at[1])
    q_copy.start()
    att_copy.start()
    staged(place_ref, regions, slabs, raw, sems, begin)
    me = place_ref[1]
    for k, ref in enumerate((g0, g1, g2, g3)):
        grad_cols[jnp.bitwise_xor(me, k)] = ref[...]
    grad_keys[...] = jnp.zeros_like(grad_keys)
    grad_values[...] = jnp.zeros_like(grad_values)
    found = live_items(
        lists_ref, counts_ref, place_ref, regions, blocks, int(diagonal), items, True)
    acc_ref[...] = jnp.zeros_like(acc_ref) if dq_in is None else dq_in[...]
    q_copy.wait()
    att_copy.wait()
    for b in range(blocks):
        cols = slice(b * BLOCK, (b + 1) * BLOCK)
        scaled[b] = q_vmem[:, cols] * BF16(SCALE)
        for h in range(heads):
            rows = head_rows(h)
            sums[b, h] = jnp.sum(
                grad_cols[b, rows].astype(F32) * att_vmem[rows, cols].astype(F32),
                axis=0, keepdims=True)

    def spread(r, copy):
        copy.wait()
        for b in range(blocks):
            slot, cols = r * blocks + b, slice(b * BLOCK, (b + 1) * BLOCK)
            key_cols[slot] = raw[r, 0, :, cols]
            for h in range(heads):
                key_rows[slot, h] = raw[r, 0, head_rows(h), cols].T
                value_rows[slot, h] = raw[r, 1, head_rows(h), cols].T

    staged(place_ref, regions, slabs, raw, sems, spread)

    def entries(chosen, masked=False):
        tiles = [(b, slot, h, head_rows(h)) for b, slot in chosen for h in range(heads)]
        scores = [dot(key_rows[slot, h], scaled[b, rows]) for b, slot, h, rows in tiles]
        if masked:
            keep = causal()
            scores = [jnp.where(keep, tile, NEG) for tile in scores]
        grads = [dot(value_rows[slot, h], grad_cols[b, rows]) for b, slot, h, rows in tiles]
        probs = [jnp.exp(tile - lse_ref[b, h]) for tile, (b, _, h, _) in zip(scores, tiles)]
        grads = [(p * (g - sums[b, h])).astype(BF16)
                 for p, g, (b, _, h, _) in zip(probs, grads, tiles)]
        probs = [p.astype(BF16) for p in probs]
        for p, g, (b, slot, h, rows) in zip(probs, grads, tiles):
            acc_ref[b, rows] += dot(key_cols[slot, rows], g)
            grad_keys[slot, rows] += dot(scaled[b, rows], g, 1, 1)
            grad_values[slot, rows] += dot(grad_cols[b, rows], p, 1, 1)

    def item_at(i):
        return lax.div(items[i], slots), lax.rem(items[i], slots)

    if diagonal:

        @pl.loop(0, blocks // 2)
        def _(i):
            entries([(2 * i, 2 * i), (2 * i + 1, 2 * i + 1)], True)

    @pl.loop(0, lax.div(found, 2))
    def _(i):
        entries([item_at(2 * i), item_at(2 * i + 1)])

    @pl.when(lax.rem(found, 2) == 1)
    def _():
        entries([item_at(found - 1)])

    if last:
        for b in range(blocks):
            dq_ref[:, b * BLOCK:(b + 1) * BLOCK] = (acc_ref[b] * SCALE).astype(BF16)
    else:
        dq_ref[...] = acc_ref[...]
    for r, ref in enumerate(outs):
        for b in range(blocks):
            cols = slice(b * BLOCK, (b + 1) * BLOCK)
            ref[0, :, cols] = grad_keys[r * blocks + b].astype(ref.dtype)
            ref[1, :, cols] = grad_values[r * blocks + b].astype(ref.dtype)


def backward(tables, queries, attended, lse, grads, regions, slabs, dq=None, last=False, pairs=1):
    width, tokens = queries.shape
    heads, blocks = width // HEAD_DIM, tokens // BLOCK
    slots = len(regions) * blocks
    diagonal = regions[0][0] == 0
    given = () if dq is None else (dq,)
    return pl.pallas_call(
        functools.partial(backward_kernel, regions, diagonal, last),
        out_shape=(jax.ShapeDtypeStruct((width, tokens), BF16) if last else
                   jax.ShapeDtypeStruct((blocks, width, BLOCK), F32),)
        + (jax.ShapeDtypeStruct((2, width, tokens), F32 if diagonal else BF16),) * len(regions),
        in_specs=smem(3) + anywhere(2) + vmem(5) + anywhere(len(slabs)) + vmem(len(given)),
        out_specs=tuple(vmem(1 + len(regions))),
        scratch_shapes=[
            pltpu.VMEM((slots, heads, BLOCK, HEAD_DIM), BF16),
            pltpu.VMEM((slots, heads, BLOCK, HEAD_DIM), BF16),
            pltpu.VMEM((slots, width, BLOCK), BF16),
            pltpu.VMEM((blocks, width, BLOCK), BF16),
            pltpu.VMEM((blocks, width, BLOCK), BF16),
            pltpu.VMEM((blocks, heads, 1, BLOCK), F32),
            pltpu.VMEM((slots, width, BLOCK), F32),
            pltpu.VMEM((slots, width, BLOCK), F32),
            pltpu.SMEM((blocks * LIST,), jnp.int32),
            pltpu.VMEM((blocks, width, BLOCK), F32),
            pltpu.VMEM((len(regions), 2, width, tokens), BF16),
            pltpu.VMEM((width, tokens), BF16),
            pltpu.VMEM((width, tokens), BF16),
            pltpu.SemaphoreType.DMA((len(regions),)),
            pltpu.SemaphoreType.DMA((2,)),
        ],
        compiler_params=pltpu.CompilerParams(vmem_limit_bytes=48 << 20),
        cost_estimate=pl.CostEstimate(
            flops=pairs * 10 ** 9, bytes_accessed=8 << 20, transcendentals=pairs * 10 ** 5),
    )(*tables, queries, attended, lse, *grads, *slabs, *given)


def on_device(queries, key_rows, values, block_lists, counts, out_proj, stream, norm_gain,
              head_proj, patches, token_order, cotangent):
    width, tokens = queries.shape
    cols = lax.axis_size("col")
    row, col = lax.axis_index("row"), lax.axis_index("col")
    odd = row % 2 == 1
    place = jnp.stack([row, col]).astype(jnp.int32)

    tables = (block_lists, counts, place)
    tie = lax.optimization_barrier
    own = jnp.stack([key_rows, values])
    slab2 = hop(own, 2)
    state = forward(tables, queries, [(0, 0, "both")], [own])
    *state, out_proj, own_again = tie([*state, out_proj, own])
    order = token_order.reshape(1, tokens)
    landed = permuted(scatter_kernel, place, order, cotangent.T)
    weights = [across(out_proj, k) for k in range(1, cols)]
    up1 = upward(own_again)
    *state, slab2, landed, out_proj, w1, w2, w3 = tie(
        [*state, slab2, landed, out_proj, *weights])
    weights = [out_proj, w1, w2, w3]
    slab4 = hop(slab2, 2)
    down1 = downward(slab2)
    up2 = upward(slab2)
    state = forward(tables, queries, [(2, 2, "both")], [slab2], tuple(state))
    *state, slab4, landed = tie([*state, slab4, landed])
    down2 = downward(slab4)
    grad_latent = mirror(landed)
    state = forward(tables, queries, [(1, 1, "each")], [down1, up1], tuple(state))
    state = forward(tables, queries, [(4, 4, "both"), (-1, 3, "one")], [slab4, up2], state)
    *state, grad_latent = tie([*state, grad_latent])
    attended, lse = forward(tables, queries, [(3, -1, "one")], [down2], tuple(state), True)

    def block_of(array, b):
        return lax.dynamic_slice_in_dim(array, b * BLOCK, BLOCK, 1)

    parts = [block_of(attended, col)] + [
        across(block_of(attended, jnp.bitwise_xor(col, k)), k) for k in range(1, cols)]
    latent, *grads = flow(
        place, parts, weights, stream, norm_gain.reshape(1, -1), head_proj, patches.T,
        grad_latent)
    grads = [grads[0]] + [across(grads[k], k) for k in range(1, cols)]

    shared = (tables, queries, attended, lse, grads)
    grad_queries, part3 = backward(*shared, [(3, 3, "each")], [down2, up2])
    from3 = mate(part3)
    part3, latent = tie([part3, latent])
    mirrored = mirror(latent)
    grad_queries, part4, part1 = backward(
        *shared, [(4, 4, "both"), (1, 1, "each")], [slab4, down1, up1], grad_queries)
    from1 = mate(part1)
    zero = jnp.zeros_like(part1)
    far = part4 + jnp.where(odd, from3, zero)
    grad_queries, far, mirrored = tie([grad_queries, far, mirrored])
    far = hop(far, -2)
    reordered = permuted(gather_kernel, place, order, mirrored)
    pieces = [reordered] + [across(reordered, k) for k in range(1, cols)]
    grad_queries, part2 = backward(*shared, [(2, 2, "both")], [slab2], grad_queries)
    near = part2 + jnp.where(odd, from1, from3) + far
    grad_queries, near, *pieces = tie([grad_queries, near] + pieces)
    near = hop(near, -2)
    grad_queries, own_grad = backward(*shared, [(0, 0, "both")], [own], grad_queries, True)
    own_grad, *pieces = tie([own_grad] + pieces)
    latent_out = assembled(place, pieces, tokens).T
    own_grad = own_grad + jnp.where(odd, zero, from1).astype(F32) + near.astype(F32)
    own_grad = own_grad.astype(BF16)
    return (latent_out, grad_queries, own_grad[0], own_grad[1])


def solution(mesh):
    return jax.shard_map(
        on_device,
        mesh=mesh,
        in_specs=(
            P("col", "row"),
            P("col", "row"),
            P("col", "row"),
            P("row", None),
            P("row"),
            P("col", None),
            P("row", None),
            P(),
            P(),
            P("row", None),
            P("row"),
            P("row", None),
        ),
        out_specs=(P("row", None), P("col", "row"), P("col", "row"), P("col", "row")),
        check_vma=False,
    )
```

```python
import functools

import jax
import jax.numpy as jnp
from jax import lax
from jax.experimental import pallas as pl
from jax.experimental.pallas import tpu as pltpu
from jax.sharding import PartitionSpec as P

HEAD_DIM = 64
BLOCK = 256
LIST = 16
REACH = 4

NEG = -1e30
EPS = 1e-05
SCALE = HEAD_DIM ** (-0.5)
F32 = jnp.float32
BF16 = jnp.bfloat16


def dot(a, b, ca=1, cb=0):
    return lax.dot_general(a, b, (((ca,), (cb,)), ((), ())), preferred_element_type=F32)


def vmem(count):
    return [pl.BlockSpec(memory_space=pltpu.VMEM)] * count


def anywhere(count):
    return [pl.BlockSpec(memory_space=pl.ANY)] * count


def smem(count):
    return [pl.BlockSpec(memory_space=pltpu.SMEM)] * count


def hop(array, by):
    size = lax.axis_size("row")
    pairs = [(i, i + by) for i in range(size) if 0 <= i + by < size]
    return lax.ppermute(array, "row", pairs)


def mate(array):
    return lax.ppermute(array, "row", [(i, i ^ 1) for i in range(lax.axis_size("row"))])


def upward(array):
    return lax.ppermute(array, "row", [(i, i + 1) for i in range(0, lax.axis_size("row"), 2)])


def downward(array):
    return lax.ppermute(array, "row", [(i + 1, i) for i in range(0, lax.axis_size("row"), 2)])


def mirror(array):
    size = lax.axis_size("row")
    return lax.ppermute(array, "row", [(i, size - 1 - i) for i in range(size)])


def across(array, bits):
    return lax.ppermute(array, "col", [(i, i ^ bits) for i in range(lax.axis_size("col"))])


def split3(x):
    hi = x.astype(BF16)
    rest = x - hi.astype(F32)
    mid = rest.astype(BF16)
    low = (rest - mid.astype(F32)).astype(BF16)
    return hi, mid, low


def picked(place_ref, order_ref, blocks):
    cols = pl.ds(pl.multiple_of((blocks - 1 - place_ref[1]) * BLOCK, BLOCK), BLOCK)
    rows = lax.broadcasted_iota(jnp.int32, (BLOCK, BLOCK), 0)
    return (rows == lax.rem(order_ref[:, cols], BLOCK)).astype(BF16), cols


def scatter_kernel(place_ref, order_ref, x_ref, o_ref):
    pick, cols = picked(place_ref, order_ref, x_ref.shape[1] // BLOCK)
    hi, mid, low = split3(x_ref[:, cols])
    o_ref[...] = (dot(hi, pick, 1, 1) + dot(mid, pick, 1, 1)) + dot(low, pick, 1, 1)


def gather_kernel(place_ref, order_ref, x_ref, o_ref):
    pick, _ = picked(place_ref, order_ref, order_ref.shape[1] // BLOCK)
    hi, mid, low = split3(x_ref[...])
    o_ref[...] = (dot(hi, pick) + dot(mid, pick)) + dot(low, pick)


def permuted(kernel, place, order, x):
    return pl.pallas_call(
        kernel,
        out_shape=jax.ShapeDtypeStruct((x.shape[0], BLOCK), F32),
        in_specs=smem(1) + vmem(2),
        out_specs=vmem(1)[0],
    )(place, order, x)


def assemble_kernel(place_ref, p0, p1, p2, p3, o_ref):
    blocks = o_ref.shape[1] // BLOCK
    for k, ref in enumerate((p0, p1, p2, p3)):
        at = (blocks - 1 - jnp.bitwise_xor(place_ref[1], k)) * BLOCK
        o_ref[:, pl.ds(pl.multiple_of(at, BLOCK), BLOCK)] = ref[...]


def assembled(place, pieces, tokens):
    return pl.pallas_call(
        assemble_kernel,
        out_shape=jax.ShapeDtypeStruct((pieces[0].shape[0], tokens), F32),
        in_specs=smem(1) + vmem(4),
        out_specs=vmem(1)[0],
    )(place, *pieces)


class Table:
    def __init__(self, ref, blocks):
        self.ref, self.blocks = ref, blocks

    def entry(self, b, j):
        return self.ref[b * LIST + j]

    def count(self, b):
        return self.ref[self.blocks * LIST + b]

    def row(self):
        return self.ref[self.blocks * (LIST + 1)]

    def col(self):
        return self.ref[self.blocks * (LIST + 1) + 1]


def packed(lists, counts, place):
    flat = jnp.concatenate([lists.reshape(-1), counts, place])
    return jnp.pad(flat, (0, -flat.shape[0] % 128))


def live_items(table, regions, blocks, first, items_ref, together):
    row = table.row()
    odd = lax.rem(row, 2)
    slots = len(regions) * blocks
    wanted = [jnp.where(odd == 1, region[1], region[0]) for region in regions]
    found = []
    total = 0
    for b in range(blocks):

        def look(j, count, b=b):
            block = table.entry(b, j)
            distance = row - lax.div(block, blocks)
            slot, hit = b * slots, 0
            for r, want in enumerate(wanted):
                here = (distance == want).astype(jnp.int32)
                slot = slot + here * r * blocks
                hit = hit + here
            items_ref[count] = slot + lax.rem(block, blocks)
            return count + hit

        start = total if together else b * LIST
        total = lax.fori_loop(first, table.count(b), look, start)
        found.append(total - start)
    return total if together else found


def staged(parity_at, regions, refs, raw, sems, act):
    at = 0
    for r, region in enumerate(regions):
        if region[2] == "both":
            act(r, pltpu.make_async_copy(refs[at], raw.at[r], sems.at[r]))
            at += 1
            continue
        for parity in (0, 1):
            if region[parity] >= 0:
                copy = pltpu.make_async_copy(refs[at], raw.at[r], sems.at[r])
                pl.when(parity_at() == parity)(lambda r=r, copy=copy: act(r, copy))
                at += 1


def begin(r, copy):
    copy.start()


def started(pairs, sems):
    copies = [pltpu.make_async_copy(a, b, sems.at[i]) for i, (a, b) in enumerate(pairs)]
    for copy in copies:
        copy.start()
    return copies


def finished(copies):
    for copy in copies:
        copy.wait()


def region_inputs(regions):
    return sum(1 if region[2] == "both" else (region[0] >= 0) + (region[1] >= 0)
               for region in regions)


def causal():
    return (lax.broadcasted_iota(jnp.int32, (BLOCK, BLOCK), 0)
            <= lax.broadcasted_iota(jnp.int32, (BLOCK, BLOCK), 1))


def head_rows(h):
    return slice(h * HEAD_DIM, (h + 1) * HEAD_DIM)


def forward_kernel(regions, opening, closing, table_ref, q_ref, *refs):
    heads = q_ref.shape[0] // HEAD_DIM
    blocks = q_ref.shape[1] // BLOCK
    slots = len(regions) * blocks
    refs = list(refs)
    slabs = [refs.pop(0) for _ in range(region_inputs(regions))]
    given = [] if opening else [refs.pop(0), refs.pop(0)]
    outs = [refs.pop(0), refs.pop(0)]
    (key_rows, value_cols, scaled, items, found_ref, acc_ref, stat_ref, raw, q_vmem, table_smem,
     att_ref, lse_ref, sems, in_sems, out_sems) = refs
    table = Table(table_smem, blocks)
    copies = started([(table_ref, table_smem), (q_ref, q_vmem)]
                     + list(zip(given, (acc_ref, stat_ref))), in_sems)
    copies[0].wait()

    def parity():
        return lax.rem(table.row(), 2)

    staged(parity, regions, slabs, raw, sems, begin)
    for b, found in enumerate(live_items(table, regions, blocks, int(opening), items, False)):
        found_ref[b] = found
    finished(copies[1:])
    for b in range(blocks):
        scaled[b] = q_vmem[:, b * BLOCK:(b + 1) * BLOCK] * BF16(SCALE)

    def spread(r, copy):
        copy.wait()
        for b in range(blocks):
            slot, cols = r * blocks + b, slice(b * BLOCK, (b + 1) * BLOCK)
            value_cols[slot] = raw[r, 1, :, cols]
            for h in range(heads):
                key_rows[slot, h] = raw[r, 0, head_rows(h), cols].T

    staged(parity, regions, slabs, raw, sems, spread)

    def entries(b, chosen, masked=False):
        scores = [[dot(key_rows[slot, h], scaled[b, head_rows(h)]) for slot in chosen]
                  for h in range(heads)]
        for h in range(heads):
            rows = head_rows(h)
            tiles = scores[h]
            if masked:
                keep = causal()
                tiles = [jnp.where(keep, tile, NEG) for tile in tiles]
            peak = tiles[0]
            for tile in tiles[1:]:
                peak = jnp.maximum(peak, tile)
            peak = jnp.max(peak, axis=0, keepdims=True)
            if masked:
                newest, total, acc = peak, 0.0, 0.0
            else:
                top = stat_ref[b, 2 * h:2 * h + 1]
                newest = jnp.maximum(top, peak)
                fade = jnp.exp(top - newest)
                total = stat_ref[b, 2 * h + 1:2 * h + 2] * fade
                acc = acc_ref[b, rows] * fade
            for slot, tile in zip(chosen, tiles):
                weights = jnp.exp(tile - newest)
                total = total + jnp.sum(weights, axis=0, keepdims=True)
                acc = acc + dot(value_cols[slot, rows], weights.astype(BF16))
            acc_ref[b, rows] = acc
            stat_ref[b, 2 * h:2 * h + 1] = newest
            stat_ref[b, 2 * h + 1:2 * h + 2] = total

    def one_block(b, carry):
        found = found_ref[b]
        if opening:
            entries(b, [b], True)

        def slot_at(i):
            return items[b * LIST + i] - b * slots

        @pl.loop(0, lax.div(found, 2))
        def _(i):
            entries(b, [slot_at(2 * i), slot_at(2 * i + 1)])

        @pl.when(lax.rem(found, 2) == 1)
        def _():
            entries(b, [slot_at(found - 1)])

        return carry

    if opening:
        stat_ref[...] = jnp.zeros_like(stat_ref)
    lax.fori_loop(0, blocks, one_block, 0)
    if not closing:
        finished(started(list(zip((acc_ref, stat_ref), outs)), out_sems))
        return
    lse_ref[...] = jnp.zeros_like(lse_ref)
    for b in range(blocks):
        cols = slice(b * BLOCK, (b + 1) * BLOCK)
        for h in range(heads):
            top, total = stat_ref[b, 2 * h:2 * h + 1], stat_ref[b, 2 * h + 1:2 * h + 2]
            att_ref[head_rows(h), cols] = (acc_ref[b, head_rows(h)] / total).astype(BF16)
            lse_ref[b, h:h + 1] = top + jnp.log(total)
    finished(started(list(zip((att_ref, lse_ref), outs)), out_sems))


def forward(tables, queries, regions, slabs, state=None, closing=False, pairs=1):
    width, tokens = queries.shape
    heads, blocks = width // HEAD_DIM, tokens // BLOCK
    slots = len(regions) * blocks
    acc, stat = (blocks, width, BLOCK), (blocks, 8, BLOCK)
    result = (jax.ShapeDtypeStruct((width, tokens), BF16), jax.ShapeDtypeStruct(stat, F32))
    state = () if state is None else state
    return pl.pallas_call(
        functools.partial(forward_kernel, regions, not state, closing),
        out_shape=result if closing else tuple(
            jax.ShapeDtypeStruct(shape, F32) for shape in (acc, stat)),
        in_specs=anywhere(2 + len(slabs) + len(state)),
        out_specs=tuple(anywhere(2)),
        scratch_shapes=[
            pltpu.VMEM((slots, heads, BLOCK, HEAD_DIM), BF16),
            pltpu.VMEM((slots, width, BLOCK), BF16),
            pltpu.VMEM((blocks, width, BLOCK), BF16),
            pltpu.SMEM((blocks * LIST,), jnp.int32),
            pltpu.SMEM((blocks,), jnp.int32),
            pltpu.VMEM(acc, F32),
            pltpu.VMEM(stat, F32),
            pltpu.VMEM((len(regions), 2, width, tokens), BF16),
            pltpu.VMEM((width, tokens), BF16),
            pltpu.SMEM(tables.shape, jnp.int32),
            pltpu.VMEM((width, tokens), BF16),
            pltpu.VMEM(stat, F32),
            pltpu.SemaphoreType.DMA((len(regions),)),
            pltpu.SemaphoreType.DMA((4,)),
            pltpu.SemaphoreType.DMA((2,)),
        ],
        compiler_params=pltpu.CompilerParams(vmem_limit_bytes=48 << 20),
        cost_estimate=pl.CostEstimate(
            flops=pairs * 10 ** 9, bytes_accessed=6 << 20, transcendentals=pairs * 10 ** 5),
    )(tables, queries, *slabs, *state)


def flow_kernel(place_ref, a0, a1, a2, a3, w0, w1, w2, w3, stream_ref, gain_ref, head_ref,
                patch_ref, grad_ref, latent_ref, g0, g1, g2, g3, wide, weights):
    width = a0.shape[0]
    channels = patch_ref.shape[0]
    cols = pl.ds(pl.multiple_of(place_ref[1] * BLOCK, BLOCK), BLOCK)
    for k, (part, weight) in enumerate(zip((a0, a1, a2, a3), (w0, w1, w2, w3))):
        wide[k * width:(k + 1) * width] = part[...]
        weights[k * width:(k + 1) * width] = weight[...]
    hidden = stream_ref[cols].astype(F32) + dot(wide[...], weights[...], 0, 0)
    inverse = lax.rsqrt(jnp.mean(hidden * hidden, axis=-1, keepdims=True) + EPS)
    gain = gain_ref[...]
    normed = (hidden * inverse * gain).astype(BF16)
    params = dot(head_ref[...], normed, 1, 1)
    factor = jnp.exp(-params[channels:])
    latent = (patch_ref[:, cols] - params[:channels]) * factor
    latent_ref[...] = latent
    grad = grad_ref[...]
    grad_params = jnp.concatenate([-grad * factor, -grad * latent - 1.0], axis=0).astype(BF16)
    gained = dot(grad_params, head_ref[...], 0, 0) * gain
    grad_hidden = (
        inverse * gained
        - hidden * inverse ** 3 * jnp.mean(hidden * gained, axis=-1, keepdims=True)
    ).astype(BF16)
    wide[...] = dot(weights[...], grad_hidden, 1, 1).astype(BF16)
    for k, ref in enumerate((g0, g1, g2, g3)):
        ref[...] = wide[k * width:(k + 1) * width]


def flow(place, parts, weights, stream, gain, head_proj, patches, grad):
    width = parts[0].shape[0]
    return pl.pallas_call(
        flow_kernel,
        out_shape=(jax.ShapeDtypeStruct(grad.shape, F32),)
        + (jax.ShapeDtypeStruct((width, BLOCK), BF16),) * 4,
        in_specs=smem(1) + vmem(13),
        out_specs=tuple(vmem(5)),
        scratch_shapes=[
            pltpu.VMEM((4 * width, BLOCK), BF16), pltpu.VMEM((4 * width, stream.shape[1]), BF16)],
        compiler_params=pltpu.CompilerParams(vmem_limit_bytes=48 << 20),
    )(place, *parts, *weights, stream, gain, head_proj, patches, grad)


def backward_kernel(regions, diagonal, last, first, table_ref, q_ref, att_ref, lse_any,
                    g0, g1, g2, g3, *refs):
    heads = q_ref.shape[0] // HEAD_DIM
    blocks = q_ref.shape[1] // BLOCK
    slots = len(regions) * blocks
    refs = list(refs)
    slabs = [refs.pop(0) for _ in range(region_inputs(regions))]
    dq_in = None if first else refs.pop(0)
    dq_out = refs.pop(0)
    outs = [refs.pop(0) for _ in regions]
    (key_rows, value_rows, key_cols, grad_cols, scaled, sums, grad_keys, grad_values, items,
     acc_ref, raw, q_vmem, att_vmem, lse_ref, table_smem, dq_vmem, leaving, sems, in_sems,
     out_sems) = refs
    table = Table(table_smem, blocks)
    copies = started([(table_ref, table_smem), (q_ref, q_vmem), (att_ref, att_vmem),
                      (lse_any, lse_ref)] + ([] if first else [(dq_in, acc_ref)]), in_sems)
    copies[0].wait()
    me = table.col()
    for k, ref in enumerate((g0, g1, g2, g3)):
        copies.append(pltpu.make_async_copy(
            ref, grad_cols.at[jnp.bitwise_xor(me, k)], in_sems.at[5 + k]))
        copies[-1].start()

    def parity():
        return lax.rem(table.row(), 2)

    staged(parity, regions, slabs, raw, sems, begin)
    grad_keys[...] = jnp.zeros_like(grad_keys)
    grad_values[...] = jnp.zeros_like(grad_values)
    if first:
        acc_ref[...] = jnp.zeros_like(acc_ref)
    found = live_items(table, regions, blocks, int(diagonal), items, True)
    finished(copies[1:])
    for b in range(blocks):
        cols = slice(b * BLOCK, (b + 1) * BLOCK)
        scaled[b] = q_vmem[:, cols] * BF16(SCALE)
        for h in range(heads):
            rows = head_rows(h)
            sums[b, h] = jnp.sum(
                grad_cols[b, rows].astype(F32) * att_vmem[rows, cols].astype(F32),
                axis=0, keepdims=True)

    def spread(r, copy):
        copy.wait()
        for b in range(blocks):
            slot, cols = r * blocks + b, slice(b * BLOCK, (b + 1) * BLOCK)
            key_cols[slot] = raw[r, 0, :, cols]
            for h in range(heads):
                key_rows[slot, h] = raw[r, 0, head_rows(h), cols].T
                value_rows[slot, h] = raw[r, 1, head_rows(h), cols].T

    staged(parity, regions, slabs, raw, sems, spread)

    def entries(chosen, masked=False):
        tiles = [(b, slot, h, head_rows(h)) for b, slot in chosen for h in range(heads)]
        scores = [dot(key_rows[slot, h], scaled[b, rows]) for b, slot, h, rows in tiles]
        if masked:
            keep = causal()
            scores = [jnp.where(keep, tile, NEG) for tile in scores]
        grads = [dot(value_rows[slot, h], grad_cols[b, rows]) for b, slot, h, rows in tiles]
        probs = [jnp.exp(tile - lse_ref[b, h:h + 1]) for tile, (b, _, h, _) in zip(scores, tiles)]
        grads = [(p * (g - sums[b, h])).astype(BF16)
                 for p, g, (b, _, h, _) in zip(probs, grads, tiles)]
        probs = [p.astype(BF16) for p in probs]
        for p, g, (b, slot, h, rows) in zip(probs, grads, tiles):
            acc_ref[b, rows] += dot(key_cols[slot, rows], g)
            grad_keys[slot, rows] += dot(scaled[b, rows], g, 1, 1)
            grad_values[slot, rows] += dot(grad_cols[b, rows], p, 1, 1)

    def item_at(i):
        return lax.div(items[i], slots), lax.rem(items[i], slots)

    if diagonal:

        @pl.loop(0, blocks // 2)
        def _(i):
            entries([(2 * i, 2 * i), (2 * i + 1, 2 * i + 1)], True)

    @pl.loop(0, lax.div(found, 2))
    def _(i):
        entries([item_at(2 * i), item_at(2 * i + 1)])

    @pl.when(lax.rem(found, 2) == 1)
    def _():
        entries([item_at(found - 1)])

    if last:
        for b in range(blocks):
            dq_vmem[:, b * BLOCK:(b + 1) * BLOCK] = (acc_ref[b] * SCALE).astype(BF16)
    going = started([(dq_vmem if last else acc_ref, dq_out)], out_sems)
    for r, ref in enumerate(outs):
        for b in range(blocks):
            cols = slice(b * BLOCK, (b + 1) * BLOCK)
            leaving[r, 0, :, cols] = grad_keys[r * blocks + b].astype(ref.dtype)
            leaving[r, 1, :, cols] = grad_values[r * blocks + b].astype(ref.dtype)
        going.append(pltpu.make_async_copy(leaving.at[r], ref, out_sems.at[1 + r]))
        going[-1].start()
    finished(going)


def backward(tables, queries, attended, lse, grads, regions, slabs, dq=None, last=False, pairs=1):
    width, tokens = queries.shape
    heads, blocks = width // HEAD_DIM, tokens // BLOCK
    slots = len(regions) * blocks
    diagonal = regions[0][0] == 0
    given = () if dq is None else (dq,)
    return pl.pallas_call(
        functools.partial(backward_kernel, regions, diagonal, last, dq is None),
        out_shape=(jax.ShapeDtypeStruct((width, tokens), BF16) if last else
                   jax.ShapeDtypeStruct((blocks, width, BLOCK), F32),)
        + (jax.ShapeDtypeStruct((2, width, tokens), F32 if diagonal else BF16),) * len(regions),
        in_specs=anywhere(8 + len(slabs) + len(given)),
        out_specs=tuple(anywhere(1 + len(regions))),
        scratch_shapes=[
            pltpu.VMEM((slots, heads, BLOCK, HEAD_DIM), BF16),
            pltpu.VMEM((slots, heads, BLOCK, HEAD_DIM), BF16),
            pltpu.VMEM((slots, width, BLOCK), BF16),
            pltpu.VMEM((blocks, width, BLOCK), BF16),
            pltpu.VMEM((blocks, width, BLOCK), BF16),
            pltpu.VMEM((blocks, heads, 1, BLOCK), F32),
            pltpu.VMEM((slots, width, BLOCK), F32),
            pltpu.VMEM((slots, width, BLOCK), F32),
            pltpu.SMEM((blocks * LIST,), jnp.int32),
            pltpu.VMEM((blocks, width, BLOCK), F32),
            pltpu.VMEM((len(regions), 2, width, tokens), BF16),
            pltpu.VMEM((width, tokens), BF16),
            pltpu.VMEM((width, tokens), BF16),
            pltpu.VMEM((blocks, 8, BLOCK), F32),
            pltpu.SMEM(tables.shape, jnp.int32),
            pltpu.VMEM((width, tokens), BF16),
            pltpu.VMEM((len(regions), 2, width, tokens), F32 if diagonal else BF16),
            pltpu.SemaphoreType.DMA((len(regions),)),
            pltpu.SemaphoreType.DMA((9,)),
            pltpu.SemaphoreType.DMA((3,)),
        ],
        compiler_params=pltpu.CompilerParams(vmem_limit_bytes=48 << 20),
        cost_estimate=pl.CostEstimate(
            flops=pairs * 10 ** 9, bytes_accessed=8 << 20, transcendentals=pairs * 10 ** 5),
    )(tables, queries, attended, lse, *grads, *slabs, *given)


def on_device(queries, key_rows, values, block_lists, counts, out_proj, stream, norm_gain,
              head_proj, patches, token_order, cotangent):
    width, tokens = queries.shape
    cols = lax.axis_size("col")
    row, col = lax.axis_index("row"), lax.axis_index("col")
    odd = row % 2 == 1
    place = jnp.stack([row, col]).astype(jnp.int32)

    tables = packed(block_lists, counts, place)
    tie = lax.optimization_barrier
    own = jnp.stack([key_rows, values])
    slab2 = hop(own, 2)
    state = forward(tables, queries, [(0, 0, "both")], [own])
    *state, slab2 = tie([*state, slab2])
    slab4 = hop(slab2, 2)
    up1 = upward(own)
    down1 = downward(slab2)
    up2 = upward(slab2)
    state = forward(tables, queries, [(2, 2, "both")], [slab2], tuple(state))
    *state, slab4, cotangent, out_proj = tie([*state, slab4, cotangent, out_proj])
    down2 = downward(slab4)
    order = token_order.reshape(1, tokens)
    grad_latent = mirror(permuted(scatter_kernel, place, order, cotangent.T))
    weights = [across(out_proj, k) for k in range(1, cols)]
    state = forward(tables, queries, [(1, 1, "each")], [down1, up1], tuple(state))
    state = forward(tables, queries, [(4, 4, "both"), (-1, 3, "one")], [slab4, up2], state)
    *state, grad_latent, out_proj, w1, w2, w3 = tie([*state, grad_latent, out_proj, *weights])
    weights = [out_proj, w1, w2, w3]
    attended, lse = forward(tables, queries, [(3, -1, "one")], [down2], tuple(state), True)

    def block_of(array, b):
        return lax.dynamic_slice_in_dim(array, b * BLOCK, BLOCK, 1)

    parts = [block_of(attended, col)] + [
        across(block_of(attended, jnp.bitwise_xor(col, k)), k) for k in range(1, cols)]
    latent, *grads = flow(
        place, parts, weights, stream, norm_gain.reshape(1, -1), head_proj, patches.T,
        grad_latent)
    grads = [grads[0]] + [across(grads[k], k) for k in range(1, cols)]

    shared = (tables, queries, attended, lse, grads)
    grad_queries, part3 = backward(*shared, [(3, 3, "each")], [down2, up2])
    from3 = mate(part3)
    part3, latent = tie([part3, latent])
    mirrored = mirror(latent)
    grad_queries, part4, part1 = backward(
        *shared, [(4, 4, "both"), (1, 1, "each")], [slab4, down1, up1], grad_queries)
    from1 = mate(part1)
    zero = jnp.zeros_like(part1)
    far = part4 + jnp.where(odd, from3, zero)
    grad_queries, far, mirrored = tie([grad_queries, far, mirrored])
    far = hop(far, -2)
    reordered = permuted(gather_kernel, place, order, mirrored)
    pieces = [reordered] + [across(reordered, k) for k in range(1, cols)]
    grad_queries, part2 = backward(*shared, [(2, 2, "both")], [slab2], grad_queries)
    near = part2 + jnp.where(odd, from1, from3) + far
    grad_queries, near, *pieces = tie([grad_queries, near] + pieces)
    near = hop(near, -2)
    grad_queries, own_grad = backward(*shared, [(0, 0, "both")], [own], grad_queries, True)
    own_grad, *pieces = tie([own_grad] + pieces)
    latent_out = assembled(place, pieces, tokens).T
    own_grad = own_grad + jnp.where(odd, zero, from1).astype(F32) + near.astype(F32)
    own_grad = own_grad.astype(BF16)
    return (latent_out, grad_queries, own_grad[0], own_grad[1])


def solution(mesh):
    return jax.shard_map(
        on_device,
        mesh=mesh,
        in_specs=(
            P("col", "row"),
            P("col", "row"),
            P("col", "row"),
            P("row", None),
            P("row"),
            P("col", None),
            P("row", None),
            P(),
            P(),
            P("row", None),
            P("row"),
            P("row", None),
        ),
        out_specs=(P("row", None), P("col", "row"), P("col", "row"), P("col", "row")),
        check_vma=False,
    )
```

```python
import functools

import jax
import jax.numpy as jnp
from jax import lax
from jax.experimental import pallas as pl
from jax.experimental.pallas import tpu as pltpu
from jax.sharding import PartitionSpec as P

HEAD_DIM = 64
BLOCK = 256
LIST = 16
REACH = 4
VMEM_GRANT = 63 << 20

NEG = -1e30
EPS = 1e-05
SCALE = HEAD_DIM ** (-0.5)
F32 = jnp.float32
BF16 = jnp.bfloat16


def dot(a, b, ca=1, cb=0):
    return lax.dot_general(a, b, (((ca,), (cb,)), ((), ())), preferred_element_type=F32)


def vmem(count):
    return [pl.BlockSpec(memory_space=pltpu.VMEM)] * count


def anywhere(count):
    return [pl.BlockSpec(memory_space=pl.ANY)] * count


def smem(count):
    return [pl.BlockSpec(memory_space=pltpu.SMEM)] * count


def hop(array, by):
    size = lax.axis_size("row")
    pairs = [(i, i + by) for i in range(size) if 0 <= i + by < size]
    return lax.ppermute(array, "row", pairs)


def mate(array):
    return lax.ppermute(array, "row", [(i, i ^ 1) for i in range(lax.axis_size("row"))])


def upward(array):
    return lax.ppermute(array, "row", [(i, i + 1) for i in range(0, lax.axis_size("row"), 2)])


def downward(array):
    return lax.ppermute(array, "row", [(i + 1, i) for i in range(0, lax.axis_size("row"), 2)])


def mirror(array):
    size = lax.axis_size("row")
    return lax.ppermute(array, "row", [(i, size - 1 - i) for i in range(size)])


def across(array, bits):
    return lax.ppermute(array, "col", [(i, i ^ bits) for i in range(lax.axis_size("col"))])


def split3(x):
    hi = x.astype(BF16)
    rest = x - hi.astype(F32)
    mid = rest.astype(BF16)
    low = (rest - mid.astype(F32)).astype(BF16)
    return hi, mid, low


def picked(place_ref, order_ref, blocks):
    cols = pl.ds(pl.multiple_of((blocks - 1 - place_ref[1]) * BLOCK, BLOCK), BLOCK)
    rows = lax.broadcasted_iota(jnp.int32, (BLOCK, BLOCK), 0)
    return (rows == lax.rem(order_ref[:, cols], BLOCK)).astype(BF16), cols


def scatter_kernel(place_ref, order_ref, x_ref, o_ref):
    pick, cols = picked(place_ref, order_ref, x_ref.shape[1] // BLOCK)
    hi, mid, low = split3(x_ref[:, cols])
    o_ref[...] = (dot(hi, pick, 1, 1) + dot(mid, pick, 1, 1)) + dot(low, pick, 1, 1)


def gather_kernel(place_ref, order_ref, x_ref, o_ref):
    pick, _ = picked(place_ref, order_ref, order_ref.shape[1] // BLOCK)
    hi, mid, low = split3(x_ref[...])
    o_ref[...] = (dot(hi, pick) + dot(mid, pick)) + dot(low, pick)


def permuted(kernel, place, order, x):
    return pl.pallas_call(
        kernel,
        out_shape=jax.ShapeDtypeStruct((x.shape[0], BLOCK), F32),
        in_specs=smem(1) + vmem(2),
        out_specs=vmem(1)[0],
    )(place, order, x)


def assemble_kernel(place_ref, p0, p1, p2, p3, o_ref):
    blocks = o_ref.shape[1] // BLOCK
    for k, ref in enumerate((p0, p1, p2, p3)):
        at = (blocks - 1 - jnp.bitwise_xor(place_ref[1], k)) * BLOCK
        o_ref[:, pl.ds(pl.multiple_of(at, BLOCK), BLOCK)] = ref[...]


def assembled(place, pieces, tokens):
    return pl.pallas_call(
        assemble_kernel,
        out_shape=jax.ShapeDtypeStruct((pieces[0].shape[0], tokens), F32),
        in_specs=smem(1) + vmem(4),
        out_specs=vmem(1)[0],
    )(place, *pieces)


class Table:
    def __init__(self, ref, blocks):
        self.ref, self.blocks = ref, blocks

    def entry(self, b, j):
        return self.ref[b * LIST + j]

    def count(self, b):
        return self.ref[self.blocks * LIST + b]

    def row(self):
        return self.ref[self.blocks * (LIST + 1)]

    def col(self):
        return self.ref[self.blocks * (LIST + 1) + 1]


def packed(lists, counts, place):
    flat = jnp.concatenate([lists.reshape(-1), counts, place])
    return jnp.pad(flat, (0, -flat.shape[0] % 128))


def live_items(table, regions, blocks, first, items_ref, together):
    row = table.row()
    odd = lax.rem(row, 2)
    slots = len(regions) * blocks
    wanted = [jnp.where(odd == 1, region[1], region[0]) for region in regions]
    found = []
    total = 0
    for b in range(blocks):

        def look(j, count, b=b):
            block = table.entry(b, j)
            distance = row - lax.div(block, blocks)
            slot, hit = b * slots, 0
            for r, want in enumerate(wanted):
                here = (distance == want).astype(jnp.int32)
                slot = slot + here * r * blocks
                hit = hit + here
            items_ref[count] = slot + lax.rem(block, blocks)
            return count + hit

        start = total if together else b * LIST
        total = lax.fori_loop(first, table.count(b), look, start)
        found.append(total - start)
    return total if together else found


def staged(parity_at, regions, refs, raw, sems, act):
    at = 0
    for r, region in enumerate(regions):
        if region[2] == "both":
            act(r, pltpu.make_async_copy(refs[at], raw.at[r], sems.at[r]))
            at += 1
            continue
        for parity in (0, 1):
            if region[parity] >= 0:
                copy = pltpu.make_async_copy(refs[at], raw.at[r], sems.at[r])
                pl.when(parity_at() == parity)(lambda r=r, copy=copy: act(r, copy))
                at += 1


def begin(r, copy):
    copy.start()


def started(pairs, sems):
    copies = [pltpu.make_async_copy(a, b, sems.at[i]) for i, (a, b) in enumerate(pairs)]
    for copy in copies:
        copy.start()
    return copies


def finished(copies):
    for copy in copies:
        copy.wait()


def region_inputs(regions):
    return sum(1 if region[2] == "both" else (region[0] >= 0) + (region[1] >= 0)
               for region in regions)


def causal():
    return (lax.broadcasted_iota(jnp.int32, (BLOCK, BLOCK), 0)
            <= lax.broadcasted_iota(jnp.int32, (BLOCK, BLOCK), 1))


def head_rows(h):
    return slice(h * HEAD_DIM, (h + 1) * HEAD_DIM)


def forward_kernel(regions, opening, closing, table_ref, q_ref, *refs):
    heads = q_ref.shape[0] // HEAD_DIM
    blocks = q_ref.shape[1] // BLOCK
    slots = len(regions) * blocks
    refs = list(refs)
    slabs = [refs.pop(0) for _ in range(region_inputs(regions))]
    given = [] if opening else [refs.pop(0), refs.pop(0)]
    outs = [refs.pop(0), refs.pop(0)]
    (key_rows, value_cols, scaled, items, found_ref, acc_ref, stat_ref, raw, q_vmem, table_smem,
     att_ref, lse_ref, sems, in_sems, out_sems) = refs
    table = Table(table_smem, blocks)
    copies = started([(table_ref, table_smem), (q_ref, q_vmem)]
                     + list(zip(given, (acc_ref, stat_ref))), in_sems)
    copies[0].wait()

    def parity():
        return lax.rem(table.row(), 2)

    staged(parity, regions, slabs, raw, sems, begin)
    for b, found in enumerate(live_items(table, regions, blocks, int(opening), items, False)):
        found_ref[b] = found
    finished(copies[1:])
    for b in range(blocks):
        scaled[b] = q_vmem[:, b * BLOCK:(b + 1) * BLOCK] * BF16(SCALE)

    def spread(r, copy):
        copy.wait()
        for b in range(blocks):
            slot, cols = r * blocks + b, slice(b * BLOCK, (b + 1) * BLOCK)
            value_cols[slot] = raw[r, 1, :, cols]
            for h in range(heads):
                key_rows[slot, h] = raw[r, 0, head_rows(h), cols].T

    staged(parity, regions, slabs, raw, sems, spread)

    def entries(b, chosen, masked=False):
        scores = [[dot(key_rows[slot, h], scaled[b, head_rows(h)]) for slot in chosen]
                  for h in range(heads)]
        for h in range(heads):
            rows = head_rows(h)
            tiles = scores[h]
            if masked:
                keep = causal()
                tiles = [jnp.where(keep, tile, NEG) for tile in tiles]
            peak = tiles[0]
            for tile in tiles[1:]:
                peak = jnp.maximum(peak, tile)
            peak = jnp.max(peak, axis=0, keepdims=True)
            if masked:
                newest, total, acc = peak, 0.0, 0.0
            else:
                top = stat_ref[b, 2 * h:2 * h + 1]
                newest = jnp.maximum(top, peak)
                fade = jnp.exp(top - newest)
                total = stat_ref[b, 2 * h + 1:2 * h + 2] * fade
                acc = acc_ref[b, rows] * fade
            for slot, tile in zip(chosen, tiles):
                weights = jnp.exp(tile - newest)
                total = total + jnp.sum(weights, axis=0, keepdims=True)
                acc = acc + dot(value_cols[slot, rows], weights.astype(BF16))
            acc_ref[b, rows] = acc
            stat_ref[b, 2 * h:2 * h + 1] = newest
            stat_ref[b, 2 * h + 1:2 * h + 2] = total

    def one_block(b, carry):
        found = found_ref[b]
        if opening:
            entries(b, [b], True)

        def slot_at(i):
            return items[b * LIST + i] - b * slots

        @pl.loop(0, lax.div(found, 2))
        def _(i):
            entries(b, [slot_at(2 * i), slot_at(2 * i + 1)])

        @pl.when(lax.rem(found, 2) == 1)
        def _():
            entries(b, [slot_at(found - 1)])

        return carry

    if opening:
        stat_ref[...] = jnp.zeros_like(stat_ref)
    lax.fori_loop(0, blocks, one_block, 0)
    if not closing:
        finished(started(list(zip((acc_ref, stat_ref), outs)), out_sems))
        return
    lse_ref[...] = jnp.zeros_like(lse_ref)
    for b in range(blocks):
        cols = slice(b * BLOCK, (b + 1) * BLOCK)
        for h in range(heads):
            top, total = stat_ref[b, 2 * h:2 * h + 1], stat_ref[b, 2 * h + 1:2 * h + 2]
            att_ref[head_rows(h), cols] = (acc_ref[b, head_rows(h)] / total).astype(BF16)
            lse_ref[b, h:h + 1] = top + jnp.log(total)
    finished(started(list(zip((att_ref, lse_ref), outs)), out_sems))


def forward(tables, queries, regions, slabs, state=None, closing=False, pairs=1):
    width, tokens = queries.shape
    heads, blocks = width // HEAD_DIM, tokens // BLOCK
    slots = len(regions) * blocks
    acc, stat = (blocks, width, BLOCK), (blocks, 8, BLOCK)
    result = (jax.ShapeDtypeStruct((width, tokens), BF16), jax.ShapeDtypeStruct(stat, F32))
    state = () if state is None else state
    return pl.pallas_call(
        functools.partial(forward_kernel, regions, not state, closing),
        out_shape=result if closing else tuple(
            jax.ShapeDtypeStruct(shape, F32) for shape in (acc, stat)),
        in_specs=anywhere(2 + len(slabs) + len(state)),
        out_specs=tuple(anywhere(2)),
        scratch_shapes=[
            pltpu.VMEM((slots, heads, BLOCK, HEAD_DIM), BF16),
            pltpu.VMEM((slots, width, BLOCK), BF16),
            pltpu.VMEM((blocks, width, BLOCK), BF16),
            pltpu.SMEM((blocks * LIST,), jnp.int32),
            pltpu.SMEM((blocks,), jnp.int32),
            pltpu.VMEM(acc, F32),
            pltpu.VMEM(stat, F32),
            pltpu.VMEM((len(regions), 2, width, tokens), BF16),
            pltpu.VMEM((width, tokens), BF16),
            pltpu.SMEM(tables.shape, jnp.int32),
            pltpu.VMEM((width, tokens), BF16),
            pltpu.VMEM(stat, F32),
            pltpu.SemaphoreType.DMA((len(regions),)),
            pltpu.SemaphoreType.DMA((4,)),
            pltpu.SemaphoreType.DMA((2,)),
        ],
        compiler_params=pltpu.CompilerParams(vmem_limit_bytes=VMEM_GRANT),
        cost_estimate=pl.CostEstimate(
            flops=pairs * 10 ** 9, bytes_accessed=6 << 20, transcendentals=pairs * 10 ** 5),
    )(tables, queries, *slabs, *state)


def flow_kernel(place_ref, a0, a1, a2, a3, w0, w1, w2, w3, stream_ref, gain_ref, head_ref,
                patch_ref, grad_ref, latent_ref, g0, g1, g2, g3, wide, weights):
    width = a0.shape[0]
    channels = patch_ref.shape[0]
    cols = pl.ds(pl.multiple_of(place_ref[1] * BLOCK, BLOCK), BLOCK)
    for k, (part, weight) in enumerate(zip((a0, a1, a2, a3), (w0, w1, w2, w3))):
        wide[k * width:(k + 1) * width] = part[...]
        weights[k * width:(k + 1) * width] = weight[...]
    hidden = stream_ref[cols].astype(F32) + dot(wide[...], weights[...], 0, 0)
    inverse = lax.rsqrt(jnp.mean(hidden * hidden, axis=-1, keepdims=True) + EPS)
    gain = gain_ref[...]
    normed = (hidden * inverse * gain).astype(BF16)
    params = dot(head_ref[...], normed, 1, 1)
    factor = jnp.exp(-params[channels:])
    latent = (patch_ref[:, cols] - params[:channels]) * factor
    latent_ref[...] = latent
    grad = grad_ref[...]
    grad_params = jnp.concatenate([-grad * factor, -grad * latent - 1.0], axis=0).astype(BF16)
    gained = dot(grad_params, head_ref[...], 0, 0) * gain
    grad_hidden = (
        inverse * gained
        - hidden * inverse ** 3 * jnp.mean(hidden * gained, axis=-1, keepdims=True)
    ).astype(BF16)
    wide[...] = dot(weights[...], grad_hidden, 1, 1).astype(BF16)
    for k, ref in enumerate((g0, g1, g2, g3)):
        ref[...] = wide[k * width:(k + 1) * width]


def flow(place, parts, weights, stream, gain, head_proj, patches, grad):
    width = parts[0].shape[0]
    return pl.pallas_call(
        flow_kernel,
        out_shape=(jax.ShapeDtypeStruct(grad.shape, F32),)
        + (jax.ShapeDtypeStruct((width, BLOCK), BF16),) * 4,
        in_specs=smem(1) + vmem(13),
        out_specs=tuple(vmem(5)),
        scratch_shapes=[
            pltpu.VMEM((4 * width, BLOCK), BF16), pltpu.VMEM((4 * width, stream.shape[1]), BF16)],
        compiler_params=pltpu.CompilerParams(vmem_limit_bytes=48 << 20),
    )(place, *parts, *weights, stream, gain, head_proj, patches, grad)


def backward_kernel(regions, diagonal, last, first, table_ref, q_ref, att_ref, lse_any,
                    g0, g1, g2, g3, *refs):
    heads = q_ref.shape[0] // HEAD_DIM
    blocks = q_ref.shape[1] // BLOCK
    slots = len(regions) * blocks
    refs = list(refs)
    slabs = [refs.pop(0) for _ in range(region_inputs(regions))]
    dq_in = None if first else refs.pop(0)
    dq_out = refs.pop(0)
    outs = [refs.pop(0) for _ in regions]
    (key_rows, value_rows, key_cols, grad_cols, scaled, sums, grad_keys, grad_values, items,
     acc_ref, raw, q_vmem, att_vmem, lse_ref, table_smem, dq_vmem, leaving, sems, in_sems,
     out_sems) = refs
    table = Table(table_smem, blocks)
    copies = started([(table_ref, table_smem), (q_ref, q_vmem), (att_ref, att_vmem),
                      (lse_any, lse_ref)] + ([] if first else [(dq_in, acc_ref)]), in_sems)
    copies[0].wait()
    me = table.col()
    for k, ref in enumerate((g0, g1, g2, g3)):
        copies.append(pltpu.make_async_copy(
            ref, grad_cols.at[jnp.bitwise_xor(me, k)], in_sems.at[5 + k]))
        copies[-1].start()

    def parity():
        return lax.rem(table.row(), 2)

    staged(parity, regions, slabs, raw, sems, begin)
    grad_keys[...] = jnp.zeros_like(grad_keys)
    grad_values[...] = jnp.zeros_like(grad_values)
    if first:
        acc_ref[...] = jnp.zeros_like(acc_ref)
    found = live_items(table, regions, blocks, int(diagonal), items, True)
    finished(copies[1:])
    for b in range(blocks):
        cols = slice(b * BLOCK, (b + 1) * BLOCK)
        scaled[b] = q_vmem[:, cols] * BF16(SCALE)
        for h in range(heads):
            rows = head_rows(h)
            sums[b, h] = jnp.sum(
                grad_cols[b, rows].astype(F32) * att_vmem[rows, cols].astype(F32),
                axis=0, keepdims=True)

    def spread(r, copy):
        copy.wait()
        for b in range(blocks):
            slot, cols = r * blocks + b, slice(b * BLOCK, (b + 1) * BLOCK)
            key_cols[slot] = raw[r, 0, :, cols]
            for h in range(heads):
                key_rows[slot, h] = raw[r, 0, head_rows(h), cols].T
                value_rows[slot, h] = raw[r, 1, head_rows(h), cols].T

    staged(parity, regions, slabs, raw, sems, spread)

    def entries(chosen, masked=False):
        tiles = [(b, slot, h, head_rows(h)) for b, slot in chosen for h in range(heads)]
        scores = [dot(key_rows[slot, h], scaled[b, rows]) for b, slot, h, rows in tiles]
        if masked:
            keep = causal()
            scores = [jnp.where(keep, tile, NEG) for tile in scores]
        grads = [dot(value_rows[slot, h], grad_cols[b, rows]) for b, slot, h, rows in tiles]
        probs = [jnp.exp(tile - lse_ref[b, h:h + 1]) for tile, (b, _, h, _) in zip(scores, tiles)]
        grads = [(p * (g - sums[b, h])).astype(BF16)
                 for p, g, (b, _, h, _) in zip(probs, grads, tiles)]
        probs = [p.astype(BF16) for p in probs]
        for p, g, (b, slot, h, rows) in zip(probs, grads, tiles):
            acc_ref[b, rows] += dot(key_cols[slot, rows], g)
            grad_keys[slot, rows] += dot(scaled[b, rows], g, 1, 1)
            grad_values[slot, rows] += dot(grad_cols[b, rows], p, 1, 1)

    def item_at(i):
        return lax.div(items[i], slots), lax.rem(items[i], slots)

    if diagonal:

        @pl.loop(0, blocks // 2)
        def _(i):
            entries([(2 * i, 2 * i), (2 * i + 1, 2 * i + 1)], True)

    @pl.loop(0, lax.div(found, 2))
    def _(i):
        entries([item_at(2 * i), item_at(2 * i + 1)])

    @pl.when(lax.rem(found, 2) == 1)
    def _():
        entries([item_at(found - 1)])

    if last:
        for b in range(blocks):
            dq_vmem[:, b * BLOCK:(b + 1) * BLOCK] = (acc_ref[b] * SCALE).astype(BF16)
    going = started([(dq_vmem if last else acc_ref, dq_out)], out_sems)
    for r, ref in enumerate(outs):
        for b in range(blocks):
            cols = slice(b * BLOCK, (b + 1) * BLOCK)
            leaving[r, 0, :, cols] = grad_keys[r * blocks + b].astype(ref.dtype)
            leaving[r, 1, :, cols] = grad_values[r * blocks + b].astype(ref.dtype)
        going.append(pltpu.make_async_copy(leaving.at[r], ref, out_sems.at[1 + r]))
        going[-1].start()
    finished(going)


def backward(tables, queries, attended, lse, grads, regions, slabs, dq=None, last=False, pairs=1):
    width, tokens = queries.shape
    heads, blocks = width // HEAD_DIM, tokens // BLOCK
    slots = len(regions) * blocks
    diagonal = regions[0][0] == 0
    given = () if dq is None else (dq,)
    return pl.pallas_call(
        functools.partial(backward_kernel, regions, diagonal, last, dq is None),
        out_shape=(jax.ShapeDtypeStruct((width, tokens), BF16) if last else
                   jax.ShapeDtypeStruct((blocks, width, BLOCK), F32),)
        + (jax.ShapeDtypeStruct((2, width, tokens), F32 if diagonal else BF16),) * len(regions),
        in_specs=anywhere(8 + len(slabs) + len(given)),
        out_specs=tuple(anywhere(1 + len(regions))),
        scratch_shapes=[
            pltpu.VMEM((slots, heads, BLOCK, HEAD_DIM), BF16),
            pltpu.VMEM((slots, heads, BLOCK, HEAD_DIM), BF16),
            pltpu.VMEM((slots, width, BLOCK), BF16),
            pltpu.VMEM((blocks, width, BLOCK), BF16),
            pltpu.VMEM((blocks, width, BLOCK), BF16),
            pltpu.VMEM((blocks, heads, 1, BLOCK), F32),
            pltpu.VMEM((slots, width, BLOCK), F32),
            pltpu.VMEM((slots, width, BLOCK), F32),
            pltpu.SMEM((blocks * LIST,), jnp.int32),
            pltpu.VMEM((blocks, width, BLOCK), F32),
            pltpu.VMEM((len(regions), 2, width, tokens), BF16),
            pltpu.VMEM((width, tokens), BF16),
            pltpu.VMEM((width, tokens), BF16),
            pltpu.VMEM((blocks, 8, BLOCK), F32),
            pltpu.SMEM(tables.shape, jnp.int32),
            pltpu.VMEM((width, tokens), BF16),
            pltpu.VMEM((len(regions), 2, width, tokens), F32 if diagonal else BF16),
            pltpu.SemaphoreType.DMA((len(regions),)),
            pltpu.SemaphoreType.DMA((9,)),
            pltpu.SemaphoreType.DMA((3,)),
        ],
        compiler_params=pltpu.CompilerParams(vmem_limit_bytes=VMEM_GRANT),
        cost_estimate=pl.CostEstimate(
            flops=pairs * 10 ** 9, bytes_accessed=8 << 20, transcendentals=pairs * 10 ** 5),
    )(tables, queries, attended, lse, *grads, *slabs, *given)


def on_device(queries, key_rows, values, block_lists, counts, out_proj, stream, norm_gain,
              head_proj, patches, token_order, cotangent):
    width, tokens = queries.shape
    cols = lax.axis_size("col")
    row, col = lax.axis_index("row"), lax.axis_index("col")
    odd = row % 2 == 1
    place = jnp.stack([row, col]).astype(jnp.int32)

    tables = packed(block_lists, counts, place)
    tie = lax.optimization_barrier
    own = jnp.stack([key_rows, values])
    slab2 = hop(own, 2)
    state = forward(tables, queries, [(0, 0, "both")], [own])
    *state, slab2 = tie([*state, slab2])
    slab4 = hop(slab2, 2)
    up1 = upward(own)
    down1 = downward(slab2)
    up2 = upward(slab2)
    state = forward(tables, queries, [(2, 2, "both")], [slab2], tuple(state))
    *state, slab4, cotangent, out_proj = tie([*state, slab4, cotangent, out_proj])
    down2 = downward(slab4)
    order = token_order.reshape(1, tokens)
    grad_latent = mirror(permuted(scatter_kernel, place, order, cotangent.T))
    weights = [across(out_proj, k) for k in range(1, cols)]
    state = forward(tables, queries, [(1, 1, "each")], [down1, up1], tuple(state))
    state = forward(tables, queries, [(4, 4, "both"), (-1, 3, "one")], [slab4, up2], state)
    *state, grad_latent, out_proj, w1, w2, w3 = tie([*state, grad_latent, out_proj, *weights])
    weights = [out_proj, w1, w2, w3]
    attended, lse = forward(tables, queries, [(3, -1, "one")], [down2], tuple(state), True)

    def block_of(array, b):
        return lax.dynamic_slice_in_dim(array, b * BLOCK, BLOCK, 1)

    parts = [block_of(attended, col)] + [
        across(block_of(attended, jnp.bitwise_xor(col, k)), k) for k in range(1, cols)]
    latent, *grads = flow(
        place, parts, weights, stream, norm_gain.reshape(1, -1), head_proj, patches.T,
        grad_latent)
    grads = [grads[0]] + [across(grads[k], k) for k in range(1, cols)]
    *grads, latent = tie([*grads, latent])
    mirrored = mirror(latent)

    shared = (tables, queries, attended, lse, grads)
    grad_queries, part3 = backward(*shared, [(3, 3, "each")], [down2, up2])
    part3, mirrored = tie([part3, mirrored])
    from3 = mate(part3)
    grad_queries, part4, part1 = backward(
        *shared, [(4, 4, "both"), (1, 1, "each")], [slab4, down1, up1], grad_queries)
    from1 = mate(part1)
    zero = jnp.zeros_like(part1)
    far = part4 + jnp.where(odd, from3, zero)
    grad_queries, far, mirrored = tie([grad_queries, far, mirrored])
    far = hop(far, -2)
    reordered = permuted(gather_kernel, place, order, mirrored)
    pieces = [reordered] + [across(reordered, k) for k in range(1, cols)]
    grad_queries, part2 = backward(*shared, [(2, 2, "both")], [slab2], grad_queries)
    near = part2 + jnp.where(odd, from1, from3) + far
    grad_queries, near, *pieces = tie([grad_queries, near] + pieces)
    near = hop(near, -2)
    grad_queries, own_grad = backward(*shared, [(0, 0, "both")], [own], grad_queries, True)
    own_grad, *pieces = tie([own_grad] + pieces)
    latent_out = assembled(place, pieces, tokens).T
    grad_keys, grad_values = (
        (own_grad[i] + jnp.where(odd, zero[i], from1[i]).astype(F32) + near[i].astype(F32))
        .astype(BF16) for i in range(2))
    return (latent_out, grad_queries, grad_keys, grad_values)


def solution(mesh):
    return jax.shard_map(
        on_device,
        mesh=mesh,
        in_specs=(
            P("col", "row"),
            P("col", "row"),
            P("col", "row"),
            P("row", None),
            P("row"),
            P("col", None),
            P("row", None),
            P(),
            P(),
            P("row", None),
            P("row"),
            P("row", None),
        ),
        out_specs=(P("row", None), P("col", "row"), P("col", "row"), P("col", "row")),
        check_vma=False,
    )
```

```python
import functools

import jax
import jax.numpy as jnp
from jax import lax
from jax.experimental import pallas as pl
from jax.experimental.pallas import tpu as pltpu
from jax.sharding import PartitionSpec as P

HEAD_DIM = 64
BLOCK = 256
LIST = 16
REACH = 4

NEG = -1e30
EPS = 1e-05
SCALE = HEAD_DIM ** (-0.5)
F32 = jnp.float32
BF16 = jnp.bfloat16


def dot(a, b, ca=1, cb=0):
    return lax.dot_general(a, b, (((ca,), (cb,)), ((), ())), preferred_element_type=F32)


def vmem(count):
    return [pl.BlockSpec(memory_space=pltpu.VMEM)] * count


def smem(count):
    return [pl.BlockSpec(memory_space=pltpu.SMEM)] * count


def hop(array, by):
    size = lax.axis_size("row")
    pairs = [(i, i + by) for i in range(size) if 0 <= i + by < size]
    return lax.ppermute(array, "row", pairs)


def mate(array):
    return lax.ppermute(array, "row", [(i, i ^ 1) for i in range(lax.axis_size("row"))])


def upward(array):
    return lax.ppermute(array, "row", [(i, i + 1) for i in range(0, lax.axis_size("row"), 2)])


def downward(array):
    return lax.ppermute(array, "row", [(i + 1, i) for i in range(0, lax.axis_size("row"), 2)])


def mirror(array):
    size = lax.axis_size("row")
    return lax.ppermute(array, "row", [(i, size - 1 - i) for i in range(size)])


def across(array, bits):
    return lax.ppermute(array, "col", [(i, i ^ bits) for i in range(lax.axis_size("col"))])


def split3(x):
    hi = x.astype(BF16)
    rest = x - hi.astype(F32)
    mid = rest.astype(BF16)
    low = (rest - mid.astype(F32)).astype(BF16)
    return hi, mid, low


def picked(place_ref, order_ref, blocks):
    cols = pl.ds(pl.multiple_of((blocks - 1 - place_ref[1]) * BLOCK, BLOCK), BLOCK)
    rows = lax.broadcasted_iota(jnp.int32, (BLOCK, BLOCK), 0)
    return (rows == lax.rem(order_ref[:, cols], BLOCK)).astype(BF16), cols


def scatter_kernel(place_ref, order_ref, x_ref, o_ref):
    pick, cols = picked(place_ref, order_ref, x_ref.shape[1] // BLOCK)
    hi, mid, low = split3(x_ref[:, cols])
    o_ref[...] = (dot(hi, pick, 1, 1) + dot(mid, pick, 1, 1)) + dot(low, pick, 1, 1)


def gather_kernel(place_ref, order_ref, x_ref, o_ref):
    pick, _ = picked(place_ref, order_ref, order_ref.shape[1] // BLOCK)
    hi, mid, low = split3(x_ref[...])
    o_ref[...] = (dot(hi, pick) + dot(mid, pick)) + dot(low, pick)


def permuted(kernel, place, order, x):
    return pl.pallas_call(
        kernel,
        out_shape=jax.ShapeDtypeStruct((x.shape[0], BLOCK), F32),
        in_specs=smem(1) + vmem(2),
        out_specs=vmem(1)[0],
    )(place, order, x)


def assemble_kernel(place_ref, p0, p1, p2, p3, o_ref):
    blocks = o_ref.shape[1] // BLOCK
    for k, ref in enumerate((p0, p1, p2, p3)):
        at = (blocks - 1 - jnp.bitwise_xor(place_ref[1], k)) * BLOCK
        o_ref[:, pl.ds(pl.multiple_of(at, BLOCK), BLOCK)] = ref[...]


def assembled(place, pieces, tokens):
    return pl.pallas_call(
        assemble_kernel,
        out_shape=jax.ShapeDtypeStruct((pieces[0].shape[0], tokens), F32),
        in_specs=smem(1) + vmem(4),
        out_specs=vmem(1)[0],
    )(place, *pieces)


def live_items(lists_ref, counts_ref, place_ref, regions, blocks, first, items_ref, together):
    row = place_ref[0]
    odd = lax.rem(row, 2)
    slots = len(regions) * blocks
    wanted = [jnp.where(odd == 1, region[1], region[0]) for region in regions]
    found = []
    total = 0
    for b in range(blocks):

        def look(j, count, b=b):
            block = lists_ref[b, j]
            distance = row - lax.div(block, blocks)
            slot, hit = b * slots, 0
            for r, want in enumerate(wanted):
                here = (distance == want).astype(jnp.int32)
                slot = slot + here * r * blocks
                hit = hit + here
            items_ref[count] = slot + lax.rem(block, blocks)
            return count + hit

        start = total if together else b * LIST
        total = lax.fori_loop(first, counts_ref[b], look, start)
        found.append(total - start)
    return total if together else found


def staged(place_ref, regions, refs, copy):
    odd = lax.rem(place_ref[0], 2)
    at = 0
    for r, region in enumerate(regions):
        if region[2] == "both":
            copy(r, refs[at])
            at += 1
            continue
        for parity in (0, 1):
            if region[parity] >= 0:
                pl.when(odd == parity)(lambda r=r, ref=refs[at]: copy(r, ref))
                at += 1


def region_inputs(regions):
    return sum(1 if region[2] == "both" else (region[0] >= 0) + (region[1] >= 0)
               for region in regions)


def causal():
    return (lax.broadcasted_iota(jnp.int32, (BLOCK, BLOCK), 0)
            <= lax.broadcasted_iota(jnp.int32, (BLOCK, BLOCK), 1))


def head_rows(h):
    return slice(h * HEAD_DIM, (h + 1) * HEAD_DIM)


def forward_kernel(regions, opening, closing, lists_ref, counts_ref, place_ref, q_ref, *refs):
    heads = q_ref.shape[0] // HEAD_DIM
    blocks = q_ref.shape[1] // BLOCK
    slots = len(regions) * blocks
    refs = list(refs)
    slabs = [refs.pop(0) for _ in range(region_inputs(regions))]
    if not opening:
        acc_in, stat_in = refs.pop(0), refs.pop(0)
    if closing:
        att_ref, lse_ref = refs.pop(0), refs.pop(0)
    else:
        acc_out, stat_out = refs.pop(0), refs.pop(0)
    key_rows, value_cols, scaled, items, found_ref, acc_ref, stat_ref = refs
    if not closing:
        acc_ref, stat_ref = acc_out, stat_out

    def copy(r, ref):
        for b in range(blocks):
            slot, cols = r * blocks + b, slice(b * BLOCK, (b + 1) * BLOCK)
            value_cols[slot] = ref[1, :, cols]
            for h in range(heads):
                key_rows[slot, h] = ref[0, head_rows(h), cols].T

    staged(place_ref, regions, slabs, copy)
    for b, found in enumerate(live_items(
            lists_ref, counts_ref, place_ref, regions, blocks, int(opening), items, False)):
        found_ref[b] = found
        scaled[b] = q_ref[:, b * BLOCK:(b + 1) * BLOCK] * BF16(SCALE)
    if not opening:
        acc_ref[...] = acc_in[...]
        stat_ref[...] = stat_in[...]

    def entries(b, chosen, masked=False):
        scores = [[dot(key_rows[slot, h], scaled[b, head_rows(h)]) for slot in chosen]
                  for h in range(heads)]
        for h in range(heads):
            rows = head_rows(h)
            tiles = scores[h]
            if masked:
                keep = causal()
                tiles = [jnp.where(keep, tile, NEG) for tile in tiles]
            peak = tiles[0]
            for tile in tiles[1:]:
                peak = jnp.maximum(peak, tile)
            peak = jnp.max(peak, axis=0, keepdims=True)
            if masked:
                newest, total, acc = peak, 0.0, 0.0
            else:
                newest = jnp.maximum(stat_ref[b, 2 * h], peak)
                fade = jnp.exp(stat_ref[b, 2 * h] - newest)
                total = stat_ref[b, 2 * h + 1] * fade
                acc = acc_ref[b, rows] * fade
            for slot, tile in zip(chosen, tiles):
                weights = jnp.exp(tile - newest)
                total = total + jnp.sum(weights, axis=0, keepdims=True)
                acc = acc + dot(value_cols[slot, rows], weights.astype(BF16))
            acc_ref[b, rows] = acc
            stat_ref[b, 2 * h] = newest
            stat_ref[b, 2 * h + 1] = total

    def one_block(b, carry):
        found = found_ref[b]
        if opening:
            entries(b, [b], True)

        def slot_at(i):
            return items[b * LIST + i] - b * slots

        @pl.loop(0, lax.div(found, 4))
        def _(i):
            entries(b, [slot_at(4 * i + n) for n in range(4)])

        left = lax.rem(found, 4)

        @pl.when(left >= 2)
        def _():
            entries(b, [slot_at(found - left), slot_at(found - left + 1)])

        @pl.when(lax.rem(left, 2) == 1)
        def _():
            entries(b, [slot_at(found - 1)])

        return carry

    lax.fori_loop(0, blocks, one_block, 0)
    if closing:
        for b in range(blocks):
            cols = slice(b * BLOCK, (b + 1) * BLOCK)
            for h in range(heads):
                top, total = stat_ref[b, 2 * h], stat_ref[b, 2 * h + 1]
                att_ref[head_rows(h), cols] = (acc_ref[b, head_rows(h)] / total).astype(BF16)
                lse_ref[b, h] = top + jnp.log(total)


def forward(tables, queries, regions, slabs, state=None, closing=False, pairs=16):
    width, tokens = queries.shape
    heads, blocks = width // HEAD_DIM, tokens // BLOCK
    slots = len(regions) * blocks
    acc, stat = (blocks, width, BLOCK), (blocks, 2 * heads, 1, BLOCK)
    result = (jax.ShapeDtypeStruct((width, tokens), BF16),
              jax.ShapeDtypeStruct((blocks, heads, 1, BLOCK), F32))
    state = () if state is None else state
    return pl.pallas_call(
        functools.partial(forward_kernel, regions, not state, closing),
        out_shape=result if closing else tuple(
            jax.ShapeDtypeStruct(shape, F32) for shape in (acc, stat)),
        in_specs=smem(3) + vmem(1 + len(slabs) + len(state)),
        out_specs=tuple(vmem(2)),
        scratch_shapes=[
            pltpu.VMEM((slots, heads, BLOCK, HEAD_DIM), BF16),
            pltpu.VMEM((slots, width, BLOCK), BF16),
            pltpu.VMEM((blocks, width, BLOCK), BF16),
            pltpu.SMEM((blocks * LIST,), jnp.int32),
            pltpu.SMEM((blocks,), jnp.int32),
            pltpu.VMEM(acc if closing else (8, BLOCK), F32),
            pltpu.VMEM(stat if closing else (8, BLOCK), F32),
        ],
        compiler_params=pltpu.CompilerParams(vmem_limit_bytes=48 << 20),
        cost_estimate=pl.CostEstimate(
            flops=pairs * 10 ** 9, bytes_accessed=6 << 20, transcendentals=pairs * 10 ** 5),
    )(*tables, queries, *slabs, *state)


def flow_kernel(place_ref, a0, a1, a2, a3, w0, w1, w2, w3, stream_ref, gain_ref, head_ref,
                patch_ref, grad_ref, latent_ref, g0, g1, g2, g3, wide, weights):
    width = a0.shape[0]
    channels = patch_ref.shape[0]
    cols = pl.ds(pl.multiple_of(place_ref[1] * BLOCK, BLOCK), BLOCK)
    for k, (part, weight) in enumerate(zip((a0, a1, a2, a3), (w0, w1, w2, w3))):
        wide[k * width:(k + 1) * width] = part[...]
        weights[k * width:(k + 1) * width] = weight[...]
    hidden = stream_ref[cols].astype(F32) + dot(wide[...], weights[...], 0, 0)
    inverse = lax.rsqrt(jnp.mean(hidden * hidden, axis=-1, keepdims=True) + EPS)
    gain = gain_ref[...]
    normed = (hidden * inverse * gain).astype(BF16)
    params = dot(head_ref[...], normed, 1, 1)
    factor = jnp.exp(-params[channels:])
    latent = (patch_ref[:, cols] - params[:channels]) * factor
    latent_ref[...] = latent
    grad = grad_ref[...]
    grad_params = jnp.concatenate([-grad * factor, -grad * latent - 1.0], axis=0).astype(BF16)
    gained = dot(grad_params, head_ref[...], 0, 0) * gain
    grad_hidden = (
        inverse * gained
        - hidden * inverse ** 3 * jnp.mean(hidden * gained, axis=-1, keepdims=True)
    ).astype(BF16)
    wide[...] = dot(weights[...], grad_hidden, 1, 1).astype(BF16)
    for k, ref in enumerate((g0, g1, g2, g3)):
        ref[...] = wide[k * width:(k + 1) * width]


def flow(place, parts, weights, stream, gain, head_proj, patches, grad):
    width = parts[0].shape[0]
    return pl.pallas_call(
        flow_kernel,
        out_shape=(jax.ShapeDtypeStruct(grad.shape, F32),)
        + (jax.ShapeDtypeStruct((width, BLOCK), BF16),) * 4,
        in_specs=smem(1) + vmem(13),
        out_specs=tuple(vmem(5)),
        scratch_shapes=[
            pltpu.VMEM((4 * width, BLOCK), BF16), pltpu.VMEM((4 * width, stream.shape[1]), BF16)],
        compiler_params=pltpu.CompilerParams(vmem_limit_bytes=48 << 20),
    )(place, *parts, *weights, stream, gain, head_proj, patches, grad)


def backward_kernel(regions, diagonal, last, lists_ref, counts_ref, place_ref, q_ref, att_ref,
                    lse_ref, g0, g1, g2, g3, *refs):
    heads = q_ref.shape[0] // HEAD_DIM
    blocks = q_ref.shape[1] // BLOCK
    slots = len(regions) * blocks
    refs = list(refs)
    slabs = [refs.pop(0) for _ in range(region_inputs(regions))]
    dq_in = None if len(refs) < 12 + len(regions) else refs.pop(0)
    dq_ref = refs.pop(0)
    outs = [refs.pop(0) for _ in regions]
    (key_rows, value_rows, key_cols, grad_cols, scaled, sums, grad_keys, grad_values, items,
     acc_ref) = refs
    me = place_ref[1]
    for k, ref in enumerate((g0, g1, g2, g3)):
        grad_cols[jnp.bitwise_xor(me, k)] = ref[...]

    def copy(r, ref):
        for b in range(blocks):
            slot, cols = r * blocks + b, slice(b * BLOCK, (b + 1) * BLOCK)
            key_cols[slot] = ref[0, :, cols]
            for h in range(heads):
                key_rows[slot, h] = ref[0, head_rows(h), cols].T
                value_rows[slot, h] = ref[1, head_rows(h), cols].T

    staged(place_ref, regions, slabs, copy)
    grad_keys[...] = jnp.zeros_like(grad_keys)
    grad_values[...] = jnp.zeros_like(grad_values)
    found = live_items(
        lists_ref, counts_ref, place_ref, regions, blocks, int(diagonal), items, True)
    for b in range(blocks):
        cols = slice(b * BLOCK, (b + 1) * BLOCK)
        scaled[b] = q_ref[:, cols] * BF16(SCALE)
        for h in range(heads):
            rows = head_rows(h)
            sums[b, h] = jnp.sum(
                grad_cols[b, rows].astype(F32) * att_ref[rows, cols].astype(F32),
                axis=0, keepdims=True)
    acc_ref[...] = jnp.zeros_like(acc_ref) if dq_in is None else dq_in[...]

    def entries(chosen, masked=False):
        tiles = [(b, slot, h, head_rows(h)) for b, slot in chosen for h in range(heads)]
        probs, grads = [], []
        for b, slot, h, rows in tiles:
            scores = dot(key_rows[slot, h], scaled[b, rows])
            grad_probs = dot(value_rows[slot, h], grad_cols[b, rows])
            if masked:
                scores = jnp.where(causal(), scores, NEG)
            p = jnp.exp(scores - lse_ref[b, h])
            grads.append((p * (grad_probs - sums[b, h])).astype(BF16))
            probs.append(p.astype(BF16))
        for p, g, (b, slot, h, rows) in zip(probs, grads, tiles):
            acc_ref[b, rows] += dot(key_cols[slot, rows], g)
            grad_keys[slot, rows] += dot(scaled[b, rows], g, 1, 1)
            grad_values[slot, rows] += dot(grad_cols[b, rows], p, 1, 1)

    def item_at(i):
        return lax.div(items[i], slots), lax.rem(items[i], slots)

    if diagonal:

        @pl.loop(0, blocks // 2)
        def _(i):
            entries([(2 * i, 2 * i), (2 * i + 1, 2 * i + 1)], True)

    @pl.loop(0, lax.div(found, 2))
    def _(i):
        entries([item_at(2 * i), item_at(2 * i + 1)])

    @pl.when(lax.rem(found, 2) == 1)
    def _():
        entries([item_at(found - 1)])

    if last:
        for b in range(blocks):
            dq_ref[:, b * BLOCK:(b + 1) * BLOCK] = (acc_ref[b] * SCALE).astype(BF16)
    else:
        dq_ref[...] = acc_ref[...]
    for r, ref in enumerate(outs):
        for b in range(blocks):
            cols = slice(b * BLOCK, (b + 1) * BLOCK)
            ref[0, :, cols] = grad_keys[r * blocks + b].astype(ref.dtype)
            ref[1, :, cols] = grad_values[r * blocks + b].astype(ref.dtype)


def backward(tables, queries, attended, lse, grads, regions, slabs, dq=None, last=False, pairs=1):
    width, tokens = queries.shape
    heads, blocks = width // HEAD_DIM, tokens // BLOCK
    slots = len(regions) * blocks
    diagonal = regions[0][0] == 0
    given = () if dq is None else (dq,)
    return pl.pallas_call(
        functools.partial(backward_kernel, regions, diagonal, last),
        out_shape=(jax.ShapeDtypeStruct((width, tokens), BF16) if last else
                   jax.ShapeDtypeStruct((blocks, width, BLOCK), F32),)
        + (jax.ShapeDtypeStruct((2, width, tokens), F32 if diagonal else BF16),) * len(regions),
        in_specs=smem(3) + vmem(7 + len(slabs) + len(given)),
        out_specs=tuple(vmem(1 + len(regions))),
        scratch_shapes=[
            pltpu.VMEM((slots, heads, BLOCK, HEAD_DIM), BF16),
            pltpu.VMEM((slots, heads, BLOCK, HEAD_DIM), BF16),
            pltpu.VMEM((slots, width, BLOCK), BF16),
            pltpu.VMEM((blocks, width, BLOCK), BF16),
            pltpu.VMEM((blocks, width, BLOCK), BF16),
            pltpu.VMEM((blocks, heads, 1, BLOCK), F32),
            pltpu.VMEM((slots, width, BLOCK), F32),
            pltpu.VMEM((slots, width, BLOCK), F32),
            pltpu.SMEM((blocks * LIST,), jnp.int32),
            pltpu.VMEM((blocks, width, BLOCK), F32),
        ],
        compiler_params=pltpu.CompilerParams(vmem_limit_bytes=48 << 20),
        cost_estimate=pl.CostEstimate(
            flops=pairs * 10 ** 9, bytes_accessed=8 << 20, transcendentals=pairs * 10 ** 5),
    )(*tables, queries, attended, lse, *grads, *slabs, *given)


def on_device(queries, key_rows, values, block_lists, counts, out_proj, stream, norm_gain,
              head_proj, patches, token_order, cotangent):
    width, tokens = queries.shape
    cols = lax.axis_size("col")
    row, col = lax.axis_index("row"), lax.axis_index("col")
    odd = row % 2 == 1
    place = jnp.stack([row, col]).astype(jnp.int32)

    tables = (block_lists, counts, place)
    own = jnp.stack([key_rows, values])
    slab2 = hop(own, 2)
    state = forward(tables, queries, [(0, 0, "both")], [own], pairs=1)
    *state, slab2, out_proj = lax.optimization_barrier([*state, slab2, out_proj])
    up1 = upward(own)
    slab4 = hop(slab2, 2)
    up2 = upward(slab2)
    down1 = downward(slab2)

    order = token_order.reshape(1, tokens)
    grad_latent = mirror(permuted(scatter_kernel, place, order, cotangent.T))
    weights = [out_proj] + [across(out_proj, k) for k in range(1, cols)]

    *state, up1 = lax.optimization_barrier([*state, up1])
    state = forward(tables, queries, [(2, 2, "both")], [slab2], tuple(state), pairs=1)
    *state, slab4 = lax.optimization_barrier([*state, slab4])
    down2 = downward(slab4)
    state = forward(tables, queries, [(1, 1, "each")], [down1, up1], tuple(state), pairs=1)
    state = forward(tables, queries, [(4, 4, "both"), (-1, 3, "one")], [slab4, up2], state,
                    pairs=1)
    attended, lse = forward(tables, queries, [(3, -1, "one")], [down2], state, True, pairs=1)

    def block_of(array, b):
        return lax.dynamic_slice_in_dim(array, b * BLOCK, BLOCK, 1)

    parts = [block_of(attended, col)] + [
        across(block_of(attended, jnp.bitwise_xor(col, k)), k) for k in range(1, cols)]
    latent, *grads = flow(
        place, parts, weights, stream, norm_gain.reshape(1, -1), head_proj, patches.T,
        grad_latent)
    *grads, mirrored = lax.optimization_barrier(
        [grads[0]] + [across(grads[k], k) for k in range(1, cols)] + [mirror(latent)])

    shared = (tables, queries, attended, lse, grads)
    grad_queries, part3, part4 = backward(
        *shared, [(3, 3, "each"), (4, 4, "both")], [down2, up2, slab4], pairs=1)
    from3 = mate(part3)
    reordered = permuted(gather_kernel, place, order, mirrored)
    grad_queries, reordered = lax.optimization_barrier((grad_queries, reordered))
    pieces = [reordered] + [across(reordered, k) for k in range(1, cols)]
    grad_queries, part1 = backward(
        *shared, [(1, 1, "each")], [down1, up1], grad_queries, pairs=1)
    from1 = mate(part1)
    zero = jnp.zeros_like(part1)
    far = part4 + jnp.where(odd, from3, zero)
    grad_queries, far, *pieces = lax.optimization_barrier([grad_queries, far] + pieces)
    far = hop(far, -2)
    latent_out = assembled(place, pieces, tokens).T
    grad_queries, part2 = backward(*shared, [(2, 2, "both")], [slab2], grad_queries, pairs=1)
    near = part2 + jnp.where(odd, from1, from3) + far
    grad_queries, near = lax.optimization_barrier((grad_queries, near))
    near = hop(near, -2)
    grad_queries, own_grad = backward(
        *shared, [(0, 0, "both")], [own], grad_queries, True, pairs=1)
    own_grad = own_grad + jnp.where(odd, zero, from1).astype(F32) + near.astype(F32)
    own_grad = own_grad.astype(BF16)
    return (latent_out, grad_queries, own_grad[0], own_grad[1])


def solution(mesh):
    return jax.shard_map(
        on_device,
        mesh=mesh,
        in_specs=(
            P("col", "row"),
            P("col", "row"),
            P("col", "row"),
            P("row", None),
            P("row"),
            P("col", None),
            P("row", None),
            P(),
            P(),
            P("row", None),
            P("row"),
            P("row", None),
        ),
        out_specs=(P("row", None), P("col", "row"), P("col", "row"), P("col", "row")),
        check_vma=False,
    )
```
